32 devices in a mesh: groups: 2 (over y), tiles: 8 (over z, x), subwin: 2 (over core).
Axes of the slice: x: 2, y: 2, z: 4, core: 2. Of those that a mesh axis runs over, the one named last changes fastest.
Arguments:
- increment: float32 [64, 8, 16, 16], P(('groups', 'tiles'), 'subwin'), parts along dimension 0, may hold values from -6 to 6
- dual_vector: float32 [64, 8, 16, 16], P(('groups', 'tiles'), 'subwin'), parts along dimension 0, may hold values from -6 to 6
- wind_u: float32 [32, 16, 16], P('tiles'), may hold values from -0.3 to 0.3
- wind_v: float32 [32, 16, 16], P('tiles'), may hold values from -0.3 to 0.3
- land_sea: int32 [32, 16], P('tiles'), may hold values from 0 to 1
- length_sq: float32 [8, 16], P('subwin', 'tiles'), may hold values from 1 to 300
- spread: float32 [8, 16], P('subwin'), may hold values from 0.5 to 3
Outputs:
- model_side: float32 [64, 8, 16, 16], P(('groups', 'tiles'), 'subwin'), parts along dimension 0
- dual_side: float32 [64, 8, 16, 16], P(('groups', 'tiles'), 'subwin'), parts along dimension 0
The draws below stay inside these ranges and needn't reach their ends.
There are 2 independent parts, one for each index of `groups`. The reference program is written for one: setup_inputs(seed, part) draws one part's arguments, and reference() takes and returns one part's arrays. A program takes and returns all parts, laid end to end along the dimension named above; an argument that names none is the same for every part. Nothing has to cross between parts.
All inputs are finite; a program needn't handle non-finite values.
Results may differ from the reference program's by a relative error of at most 0.000098.
Values sent between devices are 32-bit elements; how exact they have to be, the bound alone decides.
A program may use at most 192 MiB of HBM per device.

```python
import math
import jax
import jax.numpy as jnp
from jax import lax

LEV = 16
STEPS = 8
SWEEPS = 4
SUBWINS = 8
NLON = 32
NLAT = 16


def draw_wind_u(key, part):
    keys = jax.random.split(jax.random.fold_in(key, 23), 2)
    direction = (2 * jax.random.randint(keys[0], (1, LEV, NLAT), 0, 2) - 1).astype(jnp.float32)
    magnitude = jax.random.uniform(keys[1], (NLON, LEV, NLAT), jnp.float32, 0.15, 0.3)
    return direction * magnitude


def draw_land_sea(key, part):
    keys = jax.random.split(jax.random.fold_in(key, 11), 3)
    period = jax.random.randint(keys[0], (NLAT,), 24, 64)
    width = jax.random.randint(keys[1], (NLAT,), 12, 20)
    offset = jax.random.randint(keys[2], (NLAT,), 0, 64)
    index = jnp.arange(NLON, dtype=jnp.int32)[:, None]
    return ((index + offset[None, :]) % period[None, :] < width[None, :]).astype(jnp.int32)


def shard_levels(own_key, dims, shards, smallest, high):
    level = 1.0
    for axis_at, blocks in shards:
        draws = jax.random.uniform(jax.random.fold_in(jax.random.fold_in(own_key, 6), axis_at), (blocks,), jnp.float32, smallest / len(shards), high / len(shards))
        level = level * jnp.repeat(jnp.exp(draws), dims[axis_at] // blocks).reshape((-1,) + (1,) * (len(dims) - 1 - axis_at))
    return level


def noise(rng, shape, scale, bound, shards=(), kind=jnp.bfloat16):
    loudness = shard_levels(rng, shape, shards, -0.22, 0.18) if shards else 1.0
    values = jax.random.normal(rng, shape, jnp.float32) * scale * loudness
    return jnp.minimum(jnp.maximum(values, -bound), bound).astype(kind)


def setup_inputs(seed: int = 0, part: int = 0) -> dict:
    key_of = jax.random.split(jax.random.key(seed), 8)
    own_keys = jax.random.split(jax.random.fold_in(key_of[7], part), 8)
    return {
        "increment": noise(own_keys[0], (NLON, SUBWINS, LEV, NLAT), 1.0, 6.0, ((0, 8), (1, 2)), jnp.float32),
        "dual_vector": noise(own_keys[1], (NLON, SUBWINS, LEV, NLAT), 1.0, 6.0, ((0, 8), (1, 2)), jnp.float32),
        "wind_u": draw_wind_u(jax.random.fold_in(key_of[7], 71), part),
        "wind_v": jnp.clip(jax.random.uniform(key_of[3], (NLON, LEV, NLAT), jnp.float32, -0.3, 0.3) * shard_levels(key_of[3], (NLON, LEV, NLAT), ((0, 8),), -0.4, 0.0), -0.3, 0.3),
        "land_sea": draw_land_sea(jax.random.fold_in(key_of[7], 71), part),
        "length_sq": jnp.clip(jnp.exp(math.log(300.0) - 5.7037825 * jax.random.uniform(key_of[5], (SUBWINS, NLAT), jnp.float32) ** shard_levels(key_of[5], (SUBWINS, NLAT), ((0, 2), (1, 8)), -0.2, 0.2)), 1.0, 300.0),
        "spread": jnp.clip(jnp.exp(math.log(3.0) - 1.7917595 * jax.random.uniform(key_of[6], (SUBWINS, LEV), jnp.float32) ** shard_levels(key_of[6], (SUBWINS, LEV), ((0, 2),), -0.2, 0.2)), 0.5, 3.0),
    }


def from_north(values):
    return jnp.concatenate([values[..., 1:], jnp.zeros_like(values[..., :1])], axis=-1)


def from_south(values):
    return jnp.concatenate([jnp.zeros_like(values[..., :1]), values[..., :-1]], axis=-1)


def coefficients(wind_u, wind_v, land_sea):
    mixing = (0.15 + 0.09 * land_sea.astype(jnp.float32))[:, None, :]
    return (1.0 - 4.0 * mixing, mixing - 0.5 * wind_u, mixing + 0.5 * wind_u, mixing - 0.5 * wind_v, mixing + 0.5 * wind_v)


def tangent_model(fields, coeffs):
    centre, eastward, westward, northward, southward = coeffs
    for repeat in range(STEPS):
        fields = (centre * fields + eastward * jnp.roll(fields, -1, 0) + westward * jnp.roll(fields, 1, 0)
                  + northward * from_north(fields) + southward * from_south(fields))
    return fields


def adjoint_model(fields, coeffs):
    centre, eastward, westward, northward, southward = coeffs
    for repeat in range(STEPS):
        fields = (centre * fields + jnp.roll(eastward * fields, 1, 0) + jnp.roll(westward * fields, -1, 0)
                  + from_south(northward * fields) + from_north(southward * fields))
    return fields


def smooth_one(pair):
    weighted, lengths = pair
    spectra = jnp.fft.rfft(weighted, axis=0)
    wave = jnp.arange(NLON // 2 + 1).astype(jnp.float32)
    basic = 1.0 - jnp.cos(wave * (2.0 * math.pi / NLON))
    damping = (1.0 + 2.0 * lengths[None, None, :] * basic[:, None, None]) ** (-SWEEPS)
    return jnp.fft.irfft(spectra * damping, n=NLON, axis=0).astype(weighted.dtype)


def reference(increment, dual_vector, wind_u, wind_v, land_sea, length_sq, spread):
    coeffs = coefficients(wind_u, wind_v, land_sea)
    previous = jnp.concatenate([jnp.zeros_like(increment[:, :1]), increment[:, :-1]], axis=1)
    following = jnp.concatenate([dual_vector[:, 1:], jnp.zeros_like(dual_vector[:, :1])], axis=1)
    forward = lax.map(lambda fields: tangent_model(fields, coeffs), jnp.moveaxis(previous, 1, 0))
    forward = jnp.moveaxis(forward, 0, 1)
    backward = lax.map(lambda fields: adjoint_model(fields, coeffs), jnp.moveaxis(following, 1, 0))
    backward = jnp.moveaxis(backward, 0, 1)
    weighted = dual_vector * spread[None, :, :, None]
    smoothed = lax.map(smooth_one, (jnp.moveaxis(weighted, 1, 0), length_sq))
    covar = jnp.moveaxis(smoothed, 0, 1) * spread[None, :, :, None]
    return covar + increment - forward, dual_vector - backward
```

```python
import functools
import math

import jax
import jax.numpy as jnp
from jax import lax
from jax.experimental import pallas as pl
from jax.experimental.pallas import tpu as pltpu
from jax.sharding import PartitionSpec as P

STEPS = 8
SWEEPS = 4
LON_DEV = 4


def extended(x, sides, width):
    for axis, dim in sides:
        devices, length = (lax.axis_size(axis), x.shape[dim])
        up = [(i, (i + 1) % devices) for i in range(devices)]
        down = [(j, i) for i, j in up]
        last = lax.slice_in_dim(x, length - width, length, axis=dim)
        leading = lax.slice_in_dim(x, 0, width, axis=dim)
        before = lax.ppermute(last, axis, up)
        after = lax.ppermute(leading, axis, down)
        x = jnp.concatenate([before, x, after], axis=dim)
    return x


def passed_along(x, axis, by):
    devices = lax.axis_size(axis)
    pairs = [(i, i + by) for i in range(devices) if 0 <= i + by < devices]
    return lax.ppermute(x, axis, pairs)


def from_north(values):
    return jnp.concatenate([values[..., 1:], jnp.zeros_like(values[..., :1])], axis=-1)


def from_south(values):
    return jnp.concatenate([jnp.zeros_like(values[..., :1]), values[..., :-1]], axis=-1)


def coefficients(wind_u, wind_v, mixing):
    return (
        1.0 - 4.0 * mixing,
        mixing - 0.5 * wind_u,
        mixing + 0.5 * wind_u,
        mixing - 0.5 * wind_v,
        mixing + 0.5 * wind_v,
    )


def tangent_step(fields, coeffs, offset):
    extent = fields.shape[0]
    centre, eastward, westward, northward, southward = [
        coeff[offset + 1 : offset + extent - 1][:, None] for coeff in coeffs
    ]
    middle = fields[1:-1]
    return (
        centre * middle
        + eastward * fields[2:]
        + westward * fields[:-2]
        + northward * from_north(middle)
        + southward * from_south(middle)
    )


def adjoint_step(fields, coeffs, offset):
    extent = fields.shape[0]
    centre = coeffs[0][offset + 1 : offset + extent - 1][:, None]
    northward = coeffs[3][offset + 1 : offset + extent - 1][:, None]
    southward = coeffs[4][offset + 1 : offset + extent - 1][:, None]
    eastward = coeffs[1][offset : offset + extent][:, None]
    westward = coeffs[2][offset : offset + extent][:, None]
    middle = fields[1:-1]
    return (
        centre * middle
        + (eastward * fields)[:-2]
        + (westward * fields)[2:]
        + from_south(northward * middle)
        + from_north(southward * middle)
    )


def run_tangent(fields, coeffs, margin):
    for repeat in range(STEPS // margin):
        grown = extended(fields, (("tiles", 0),), margin)
        for inner_step in range(margin):
            offset = (coeffs[0].shape[0] - grown.shape[0]) // 2
            grown = tangent_step(grown, coeffs, offset)
        fields = grown
    return fields


def run_adjoint(fields, coeffs, margin):
    for repeat in range(STEPS // margin):
        grown = extended(fields, (("tiles", 0),), margin)
        for inner_step in range(margin):
            offset = (coeffs[0].shape[0] - grown.shape[0]) // 2
            grown = adjoint_step(grown, coeffs, offset)
        fields = grown
    return fields


def square_tables(extent):
    index = jnp.arange(extent, dtype=jnp.int32)
    phases = index[:, None] * index[None, :] % extent
    angles = phases.astype(jnp.float32) * (2.0 * math.pi / extent)
    return (jnp.cos(angles), jnp.sin(angles))


def contract(form, first, second):
    return jnp.einsum(form, first, second, precision=lax.Precision.HIGHEST)


def smooth_bands(bands, length_sq):
    count = bands.shape[0]
    inner = LON_DEV
    outer = count // inner
    columns = bands.reshape(outer, inner, -1)
    cos_outer, sin_outer = square_tables(outer)
    cos_inner, sin_inner = square_tables(inner)
    outer_index = jnp.arange(outer, dtype=jnp.int32)
    inner_index = jnp.arange(inner, dtype=jnp.int32)
    twist = (outer_index[:, None] * inner_index[None, :] % count).astype(jnp.float32) * (
        2.0 * math.pi / count
    )
    twist_cos = jnp.cos(twist)[:, :, None]
    twist_sin = jnp.sin(twist)[:, :, None]
    first_real = contract("ab,bqc->aqc", cos_outer, columns)
    first_imag = -contract("ab,bqc->aqc", sin_outer, columns)
    turned_real = first_real * twist_cos + first_imag * twist_sin
    turned_imag = first_imag * twist_cos - first_real * twist_sin
    modes_real = contract("aqc,kq->akc", turned_real, cos_inner) + contract(
        "aqc,kq->akc", turned_imag, sin_inner
    )
    modes_imag = contract("aqc,kq->akc", turned_imag, cos_inner) - contract(
        "aqc,kq->akc", turned_real, sin_inner
    )
    wave = (outer_index[:, None] + outer * inner_index[None, :]).astype(jnp.float32)
    basic = 1.0 - jnp.cos(wave * (2.0 * math.pi / count))
    damping = (1.0 + 2.0 * length_sq[None, None, :, None, :] * basic[:, :, None, None, None]) ** (
        -SWEEPS
    )
    damping = jnp.broadcast_to(damping, (outer, inner) + bands.shape[1:]).reshape(outer, inner, -1)
    modes_real = modes_real * damping
    modes_imag = modes_imag * damping
    back_real = contract("akc,kq->aqc", modes_real, cos_inner) - contract(
        "akc,kq->aqc", modes_imag, sin_inner
    )
    back_imag = contract("akc,kq->aqc", modes_imag, cos_inner) + contract(
        "akc,kq->aqc", modes_real, sin_inner
    )
    final_real = back_real * twist_cos - back_imag * twist_sin
    final_imag = back_imag * twist_cos + back_real * twist_sin
    smoothed = contract("ab,bqc->aqc", cos_outer, final_real) - contract(
        "ab,bqc->aqc", sin_outer, final_imag
    )
    return (smoothed / count).reshape(bands.shape)


def stepwise_body(increment, dual_vector, wind_u, wind_v, land_sea, length_sq, spread):
    margin = 4
    mixing = 0.15 + 0.09 * land_sea.astype(jnp.float32)
    grown_u, grown_v, grown_mix = (
        extended(wind_u, (("tiles", 0),), margin),
        extended(wind_v, (("tiles", 0),), margin),
        extended(mixing, (("tiles", 0),), margin),
    )
    coeffs = coefficients(grown_u, grown_v, grown_mix[:, None, :])
    carried = passed_along(increment[:, -1:], "subwin", 1)
    previous = jnp.concatenate([carried, increment[:, :-1]], axis=1)
    later = passed_along(dual_vector[:, :1], "subwin", -1)
    following = jnp.concatenate([dual_vector[:, 1:], later], axis=1)
    weighted = dual_vector * spread[None, :, :, None]
    bands = lax.all_to_all(weighted, "tiles", split_axis=3, concat_axis=0, tiled=True)
    smoothed = smooth_bands(bands, length_sq)
    forward = run_tangent(previous, coeffs, margin)
    backward = run_adjoint(following, coeffs, margin)
    returned = lax.all_to_all(smoothed, "tiles", split_axis=0, concat_axis=3, tiled=True)
    covar = returned * spread[None, :, :, None]
    return (covar + increment - forward, dual_vector - backward)


ROWS = 8
LANES = 128
MESH = pl.DeviceIdType.MESH


def circulant_row(lengths, count):
    half = count // 2
    damped = []
    for wave in range(half + 1):
        basic = 1.0 - math.cos(2.0 * math.pi * wave / count)
        base = 1.0 + (2.0 * basic) * lengths
        power = base
        for _ in range(SWEEPS - 1):
            power = power * base
        weight = (1.0 if wave in (0, half) else 2.0) / count
        damped.append(weight / power)
    row = [None] * (half + 1)
    for distance in range(half // 2 + 1):
        sums = [jnp.zeros_like(lengths), jnp.zeros_like(lengths)]
        for wave in range(half + 1):
            factor = math.cos(2.0 * math.pi * (wave * distance % count) / count)
            sums[wave % 2] = sums[wave % 2] + factor * damped[wave]
        row[distance] = sums[0] + sums[1]
        row[half - distance] = sums[0] - sums[1]
    return row


def kernel(
    tiles,
    reach,
    inc_ref,
    dual_ref,
    u_ref,
    v_ref,
    land_ref,
    length_ref,
    spread_ref,
    model_out,
    dual_out,
    data,
    cross,
    other,
    coef,
    send_sem,
    recv_sem,
    cross_send,
    cross_recv,
):
    lons, subs, levs, lats = inc_ref.shape
    high = levs // ROWS
    span = high * lats
    bands = length_ref.shape[1]
    me = lax.axis_index("tiles")
    sub = lax.axis_index("subwin")
    near = [d for d in range(1, reach + 1)] + [tiles - d for d in range(1, reach + 1)]
    far = [d for d in range(1, tiles) if d not in near]
    beside = list(range(-reach, reach + 1))

    def at(distance):
        return lax.rem(me + (distance + tiles), tiles)

    barrier = pltpu.get_barrier_semaphore()
    for d in near + far:
        pl.semaphore_signal(barrier, inc=1, device_id={"tiles": at(d)}, device_id_type=MESH)
    for d in beside:
        pl.semaphore_signal(
            barrier, inc=1, device_id={"tiles": at(d), "subwin": 1 - sub}, device_id_type=MESH
        )

    lane = lax.broadcasted_iota(jnp.int32, (ROWS, LANES), 1)
    row = lax.broadcasted_iota(jnp.int32, (ROWS, LANES), 0)
    group = lane // span
    lat = lane % lats

    def joined(pieces):
        return jnp.concatenate(pieces, axis=1)

    def turned(x, by):
        by = by % LANES
        return x if by == 0 else pltpu.roll(x, by, 1)

    inc = [
        joined([inc_ref[i, s, h * ROWS : (h + 1) * ROWS, :] for s in range(subs) for h in range(high)])
        for i in range(lons)
    ]
    dual = [
        joined([dual_ref[i, s, h * ROWS : (h + 1) * ROWS, :] for s in range(subs) for h in range(high)])
        for i in range(lons)
    ]
    wind_u = joined([u_ref[i, h * ROWS : (h + 1) * ROWS, :] for i in range(lons) for h in range(high)])
    wind_v = joined([v_ref[i, h * ROWS : (h + 1) * ROWS, :] for i in range(lons) for h in range(high)])
    mixing = 0.15 + 0.09 * land_ref[...].astype(jnp.float32)
    mixing = joined([mixing[i : i + 1] for i in range(lons) for h in range(high)])
    lengths = jnp.zeros((ROWS, LANES), jnp.float32)
    for s in range(subs):
        for b in range(bands):
            here = jnp.logical_and(group == s, lat == me * bands + b)
            lengths = jnp.where(here, length_ref[s, b], lengths)
    aux = jnp.where(row < ROWS // 2, lengths, jnp.broadcast_to(mixing, (ROWS, LANES)))
    last_inc = joined(
        [inc_ref[i, subs - 1, h * ROWS : (h + 1) * ROWS, :] for i in range(lons) for h in range(high)]
    )
    first_dual = joined(
        [dual_ref[i, 0, h * ROWS : (h + 1) * ROWS, :] for i in range(lons) for h in range(high)]
    )
    own = inc + [wind_u, wind_v, aux] + dual
    for n, tile in enumerate(own):
        data[0, n * ROWS : (n + 1) * ROWS, :] = tile
    cross[...] = jnp.where(sub == 0, last_inc, first_dual)

    pl.semaphore_wait(barrier, len(near) + len(far) + len(beside))

    far_from = (lons + 2) * ROWS
    near_copies, far_copies, cross_copies = [], [], []
    for d in near:
        copy = pltpu.make_async_remote_copy(
            src_ref=data.at[0],
            dst_ref=data.at[tiles - d],
            send_sem=send_sem.at[d],
            recv_sem=recv_sem.at[tiles - d],
            device_id={"tiles": at(d)},
            device_id_type=MESH,
        )
        copy.start()
        near_copies.append(copy)
    for d in beside:
        copy = pltpu.make_async_remote_copy(
            src_ref=cross,
            dst_ref=other.at[reach - d],
            send_sem=cross_send.at[reach + d],
            recv_sem=cross_recv.at[reach - d],
            device_id={"tiles": at(d), "subwin": 1 - sub},
            device_id_type=MESH,
        )
        copy.start()
        cross_copies.append(copy)
    for d in far:
        copy = pltpu.make_async_remote_copy(
            src_ref=data.at[0, pl.ds(far_from, (lons + 1) * ROWS)],
            dst_ref=data.at[tiles - d, pl.ds(far_from, (lons + 1) * ROWS)],
            send_sem=send_sem.at[d],
            recv_sem=recv_sem.at[tiles - d],
            device_id={"tiles": at(d)},
            device_id_type=MESH,
        )
        copy.start()
        far_copies.append(copy)

    spread = jnp.zeros((ROWS, LANES), jnp.float32)
    eye = lax.broadcasted_iota(jnp.int32, (ROWS, ROWS), 0) == lax.broadcasted_iota(
        jnp.int32, (ROWS, ROWS), 1
    )
    for s in range(subs):
        for h in range(high):
            line = spread_ref[s : s + 1, h * ROWS : (h + 1) * ROWS]
            column = jnp.sum(jnp.where(eye, jnp.broadcast_to(line, (ROWS, ROWS)), 0.0), 1, keepdims=True)
            spread = jnp.where(lane // lats == s * high + h, column, spread)

    for copy in near_copies + cross_copies:
        copy.wait_recv()

    def spread_out(x):
        parts = [turned(x, q * span) for q in range(lons)]
        outs = []
        for i in range(lons):
            out = parts[(0 - i) % lons]
            for g in range(1, subs):
                out = jnp.where(group == g, parts[(g - i) % lons], out)
            outs.append(out)
        return outs

    up = jnp.where(sub > 0, 1.0, 0.0)
    down = jnp.where(sub < 1, 1.0, 0.0)
    previous, following = [], []
    place = 0
    for d in beside:
        slot = d % tiles
        us = spread_out(data[slot, lons * ROWS : (lons + 1) * ROWS, :])
        vs = spread_out(data[slot, (lons + 1) * ROWS : (lons + 2) * ROWS, :])
        mix = data[slot, (lons + 2) * ROWS + ROWS // 2 : (lons + 2) * ROWS + ROWS // 2 + 1, :]
        mixes = spread_out(jnp.broadcast_to(mix, (ROWS, LANES)))
        beyond = other[d + reach]
        for i in range(lons):
            at_rows = pl.ds(place * ROWS, ROWS)
            m, u, v = mixes[i], 0.5 * us[i], 0.5 * vs[i]
            coef[0, at_rows, :] = 1.0 - 4.0 * m
            coef[1, at_rows, :] = m - u
            coef[2, at_rows, :] = m + u
            coef[3, at_rows, :] = jnp.where(lat == lats - 1, 0.0, m - v)
            coef[4, at_rows, :] = jnp.where(lat == 0, 0.0, m + v)
            place += 1
            f = data[slot, i * ROWS : (i + 1) * ROWS, :]
            g = data[slot, (lons + 3 + i) * ROWS : (lons + 4 + i) * ROWS, :]
            previous.append(
                jnp.where(group == 0, up * turned(beyond, -i * span), turned(f, span))
            )
            following.append(
                jnp.where(
                    group == subs - 1, down * turned(beyond, (subs - 1 - i) * span), turned(g, -span)
                )
            )
    extra = reach * lons - STEPS
    extent = place - 2 * extra
    f = jnp.concatenate(previous[extra : place - extra], axis=0)
    g = jnp.concatenate(following[extra : place - extra], axis=0)
    for step in range(STEPS):
        first = extra + step
        count = extent - 2 * step
        inner = pl.ds((first + 1) * ROWS, (count - 2) * ROWS)
        lower = pl.ds(first * ROWS, (count - 2) * ROWS)
        upper = pl.ds((first + 2) * ROWS, (count - 2) * ROWS)
        mid = f[ROWS:-ROWS]
        f = (
            coef[0, inner, :] * mid
            + coef[1, inner, :] * f[2 * ROWS :]
            + coef[2, inner, :] * f[: -2 * ROWS]
            + coef[3, inner, :] * turned(mid, -1)
            + coef[4, inner, :] * turned(mid, 1)
        )
        mid = g[ROWS:-ROWS]
        g = (
            coef[0, inner, :] * mid
            + coef[1, lower, :] * g[: -2 * ROWS]
            + coef[2, upper, :] * g[2 * ROWS :]
            + turned(coef[3, inner, :] * mid, 1)
            + turned(coef[4, inner, :] * mid, -1)
        )

    for copy in far_copies:
        copy.wait_recv()

    total = jnp.zeros((1, LANES), jnp.float32)
    for slot in range(tiles):
        total = total + data[slot, far_from : far_from + 1, :]
    weights = circulant_row(jnp.broadcast_to(total, (ROWS, LANES)), lons * tiles)
    smooth = [jnp.zeros((ROWS, LANES), jnp.float32) for _ in range(lons)]
    ring = lons * tiles
    for slot in range(tiles):
        for n in range(lons):
            x = data[slot, (lons + 3 + n) * ROWS : (lons + 4 + n) * ROWS, :]
            for i in range(lons):
                distance = (slot * lons + n - i) % ring
                smooth[i] = smooth[i] + weights[min(distance, ring - distance)] * x

    square = spread * spread
    for i in range(lons):
        here = slice(i * ROWS, (i + 1) * ROWS)
        model = square * smooth[i] + data[0, here, :] - f[here]
        rest = data[0, (lons + 3 + i) * ROWS : (lons + 4 + i) * ROWS, :] - g[here]
        for s in range(subs):
            for h in range(high):
                by = -(s * high + h) * lats
                at_levels = slice(h * ROWS, (h + 1) * ROWS)
                model_out[i, s, at_levels, :] = turned(model, by)[:, :lats]
                dual_out[i, s, at_levels, :] = turned(rest, by)[:, :lats]

    for copy in near_copies + cross_copies + far_copies:
        copy.wait_send()


def packed(tiles, subwins, increment):
    lons, subs, levs, lats = increment.shape
    reach = -(-STEPS // lons)
    return (
        subwins == 2
        and levs % ROWS == 0
        and subs == lons
        and subs * (levs // ROWS) * lats == LANES
        and 2 * reach < tiles <= 2 * ROWS
        and lons * tiles % 4 == 0
    )


def direct_body(increment, dual_vector, wind_u, wind_v, land_sea, length_sq, spread):
    tiles = lax.axis_size("tiles")
    lons = increment.shape[0]
    reach = -(-STEPS // lons)
    around = 2 * reach + 1
    vmem = pl.BlockSpec(memory_space=pltpu.VMEM)
    smem = pl.BlockSpec(memory_space=pltpu.SMEM)
    return pl.pallas_call(
        functools.partial(kernel, tiles, reach),
        out_shape=(
            jax.ShapeDtypeStruct(increment.shape, jnp.float32),
            jax.ShapeDtypeStruct(increment.shape, jnp.float32),
        ),
        in_specs=[vmem, vmem, vmem, vmem, vmem, smem, vmem],
        out_specs=(vmem, vmem),
        scratch_shapes=[
            pltpu.VMEM((tiles, (2 * lons + 3) * ROWS, LANES), jnp.float32),
            pltpu.VMEM((ROWS, LANES), jnp.float32),
            pltpu.VMEM((around, ROWS, LANES), jnp.float32),
            pltpu.VMEM((5, around * lons * ROWS, LANES), jnp.float32),
            pltpu.SemaphoreType.DMA((tiles,)),
            pltpu.SemaphoreType.DMA((tiles,)),
            pltpu.SemaphoreType.DMA((around,)),
            pltpu.SemaphoreType.DMA((around,)),
        ],
        compiler_params=pltpu.CompilerParams(collective_id=0, has_side_effects=True),
    )(increment, dual_vector, wind_u, wind_v, land_sea, length_sq, spread)


def body(*args):
    fits = packed(lax.axis_size("tiles"), lax.axis_size("subwin"), args[0])
    return direct_body(*args) if fits else stepwise_body(*args)


def solution(mesh):
    placed = (
        P(("groups", "tiles"), "subwin", None, None),
        P(("groups", "tiles"), "subwin", None, None),
        P("tiles", None, None),
        P("tiles", None, None),
        P("tiles", None),
        P("subwin", "tiles"),
        P("subwin", None),
    )
    return jax.shard_map(
        body,
        mesh=mesh,
        in_specs=placed,
        out_specs=(
            P(("groups", "tiles"), "subwin", None, None),
            P(("groups", "tiles"), "subwin", None, None),
        ),
        check_vma=False,
    )
```

```python
import functools
import math

import jax
import jax.numpy as jnp
from jax import lax
from jax.experimental import pallas as pl
from jax.experimental.pallas import tpu as pltpu
from jax.sharding import PartitionSpec as P

STEPS = 8
SWEEPS = 4
LON_DEV = 4


def extended(x, sides, width):
    for axis, dim in sides:
        devices, length = (lax.axis_size(axis), x.shape[dim])
        up = [(i, (i + 1) % devices) for i in range(devices)]
        down = [(j, i) for i, j in up]
        last = lax.slice_in_dim(x, length - width, length, axis=dim)
        leading = lax.slice_in_dim(x, 0, width, axis=dim)
        before = lax.ppermute(last, axis, up)
        after = lax.ppermute(leading, axis, down)
        x = jnp.concatenate([before, x, after], axis=dim)
    return x


def passed_along(x, axis, by):
    devices = lax.axis_size(axis)
    pairs = [(i, i + by) for i in range(devices) if 0 <= i + by < devices]
    return lax.ppermute(x, axis, pairs)


def from_north(values):
    return jnp.concatenate([values[..., 1:], jnp.zeros_like(values[..., :1])], axis=-1)


def from_south(values):
    return jnp.concatenate([jnp.zeros_like(values[..., :1]), values[..., :-1]], axis=-1)


def coefficients(wind_u, wind_v, mixing):
    return (
        1.0 - 4.0 * mixing,
        mixing - 0.5 * wind_u,
        mixing + 0.5 * wind_u,
        mixing - 0.5 * wind_v,
        mixing + 0.5 * wind_v,
    )


def tangent_step(fields, coeffs, offset):
    extent = fields.shape[0]
    centre, eastward, westward, northward, southward = [
        coeff[offset + 1 : offset + extent - 1][:, None] for coeff in coeffs
    ]
    middle = fields[1:-1]
    return (
        centre * middle
        + eastward * fields[2:]
        + westward * fields[:-2]
        + northward * from_north(middle)
        + southward * from_south(middle)
    )


def adjoint_step(fields, coeffs, offset):
    extent = fields.shape[0]
    centre = coeffs[0][offset + 1 : offset + extent - 1][:, None]
    northward = coeffs[3][offset + 1 : offset + extent - 1][:, None]
    southward = coeffs[4][offset + 1 : offset + extent - 1][:, None]
    eastward = coeffs[1][offset : offset + extent][:, None]
    westward = coeffs[2][offset : offset + extent][:, None]
    middle = fields[1:-1]
    return (
        centre * middle
        + (eastward * fields)[:-2]
        + (westward * fields)[2:]
        + from_south(northward * middle)
        + from_north(southward * middle)
    )


def run_tangent(fields, coeffs, margin):
    for repeat in range(STEPS // margin):
        grown = extended(fields, (("tiles", 0),), margin)
        for inner_step in range(margin):
            offset = (coeffs[0].shape[0] - grown.shape[0]) // 2
            grown = tangent_step(grown, coeffs, offset)
        fields = grown
    return fields


def run_adjoint(fields, coeffs, margin):
    for repeat in range(STEPS // margin):
        grown = extended(fields, (("tiles", 0),), margin)
        for inner_step in range(margin):
            offset = (coeffs[0].shape[0] - grown.shape[0]) // 2
            grown = adjoint_step(grown, coeffs, offset)
        fields = grown
    return fields


def square_tables(extent):
    index = jnp.arange(extent, dtype=jnp.int32)
    phases = index[:, None] * index[None, :] % extent
    angles = phases.astype(jnp.float32) * (2.0 * math.pi / extent)
    return (jnp.cos(angles), jnp.sin(angles))


def contract(form, first, second):
    return jnp.einsum(form, first, second, precision=lax.Precision.HIGHEST)


def smooth_bands(bands, length_sq):
    count = bands.shape[0]
    inner = LON_DEV
    outer = count // inner
    columns = bands.reshape(outer, inner, -1)
    cos_outer, sin_outer = square_tables(outer)
    cos_inner, sin_inner = square_tables(inner)
    outer_index = jnp.arange(outer, dtype=jnp.int32)
    inner_index = jnp.arange(inner, dtype=jnp.int32)
    twist = (outer_index[:, None] * inner_index[None, :] % count).astype(jnp.float32) * (
        2.0 * math.pi / count
    )
    twist_cos = jnp.cos(twist)[:, :, None]
    twist_sin = jnp.sin(twist)[:, :, None]
    first_real = contract("ab,bqc->aqc", cos_outer, columns)
    first_imag = -contract("ab,bqc->aqc", sin_outer, columns)
    turned_real = first_real * twist_cos + first_imag * twist_sin
    turned_imag = first_imag * twist_cos - first_real * twist_sin
    modes_real = contract("aqc,kq->akc", turned_real, cos_inner) + contract(
        "aqc,kq->akc", turned_imag, sin_inner
    )
    modes_imag = contract("aqc,kq->akc", turned_imag, cos_inner) - contract(
        "aqc,kq->akc", turned_real, sin_inner
    )
    wave = (outer_index[:, None] + outer * inner_index[None, :]).astype(jnp.float32)
    basic = 1.0 - jnp.cos(wave * (2.0 * math.pi / count))
    damping = (1.0 + 2.0 * length_sq[None, None, :, None, :] * basic[:, :, None, None, None]) ** (
        -SWEEPS
    )
    damping = jnp.broadcast_to(damping, (outer, inner) + bands.shape[1:]).reshape(outer, inner, -1)
    modes_real = modes_real * damping
    modes_imag = modes_imag * damping
    back_real = contract("akc,kq->aqc", modes_real, cos_inner) - contract(
        "akc,kq->aqc", modes_imag, sin_inner
    )
    back_imag = contract("akc,kq->aqc", modes_imag, cos_inner) + contract(
        "akc,kq->aqc", modes_real, sin_inner
    )
    final_real = back_real * twist_cos - back_imag * twist_sin
    final_imag = back_imag * twist_cos + back_real * twist_sin
    smoothed = contract("ab,bqc->aqc", cos_outer, final_real) - contract(
        "ab,bqc->aqc", sin_outer, final_imag
    )
    return (smoothed / count).reshape(bands.shape)


def stepwise_body(increment, dual_vector, wind_u, wind_v, land_sea, length_sq, spread):
    margin = 4
    mixing = 0.15 + 0.09 * land_sea.astype(jnp.float32)
    grown_u, grown_v, grown_mix = (
        extended(wind_u, (("tiles", 0),), margin),
        extended(wind_v, (("tiles", 0),), margin),
        extended(mixing, (("tiles", 0),), margin),
    )
    coeffs = coefficients(grown_u, grown_v, grown_mix[:, None, :])
    carried = passed_along(increment[:, -1:], "subwin", 1)
    previous = jnp.concatenate([carried, increment[:, :-1]], axis=1)
    later = passed_along(dual_vector[:, :1], "subwin", -1)
    following = jnp.concatenate([dual_vector[:, 1:], later], axis=1)
    weighted = dual_vector * spread[None, :, :, None]
    bands = lax.all_to_all(weighted, "tiles", split_axis=3, concat_axis=0, tiled=True)
    smoothed = smooth_bands(bands, length_sq)
    forward = run_tangent(previous, coeffs, margin)
    backward = run_adjoint(following, coeffs, margin)
    returned = lax.all_to_all(smoothed, "tiles", split_axis=0, concat_axis=3, tiled=True)
    covar = returned * spread[None, :, :, None]
    return (covar + increment - forward, dual_vector - backward)


ROWS = 8
LANES = 128
MESH = pl.DeviceIdType.MESH


def circulant_row(lengths, count):
    half = count // 2
    damped = []
    for wave in range(half + 1):
        basic = 1.0 - math.cos(2.0 * math.pi * wave / count)
        base = 1.0 + (2.0 * basic) * lengths
        power = base
        for _ in range(SWEEPS - 1):
            power = power * base
        weight = (1.0 if wave in (0, half) else 2.0) / count
        damped.append(weight / power)
    row = [None] * (half + 1)
    for distance in range(half // 2 + 1):
        sums = [jnp.zeros_like(lengths), jnp.zeros_like(lengths)]
        for wave in range(half + 1):
            factor = math.cos(2.0 * math.pi * (wave * distance % count) / count)
            sums[wave % 2] = sums[wave % 2] + factor * damped[wave]
        row[distance] = sums[0] + sums[1]
        row[half - distance] = sums[0] - sums[1]
    return row


def kernel(
    tiles,
    reach,
    *refs,
):
    count = 7
    held, packed_out = refs[:count], refs[count]
    here_refs = refs[count + 1 : 2 * count + 1]
    inc_ref, dual_ref, u_ref, v_ref, land_ref, length_ref, spread_ref = here_refs
    (
    data,
    cross,
    other,
    coef,
    send_sem,
    recv_sem,
    cross_send,
    cross_recv,
    load_sem,
    ) = refs[2 * count + 1 :]
    loads = [
        pltpu.make_async_copy(held[n], here_refs[n], load_sem.at[n]) for n in range(count)
    ]
    for load in loads:
        load.start()
    lons, subs, levs, lats = inc_ref.shape
    high = levs // ROWS
    span = high * lats
    bands = length_ref.shape[0]
    me = lax.axis_index("tiles")
    sub = lax.axis_index("subwin")
    near = [d for d in range(1, reach + 1)] + [tiles - d for d in range(1, reach + 1)]
    far = [d for d in range(1, tiles) if d not in near]
    beside = list(range(-reach, reach + 1))

    def at(distance):
        return lax.rem(me + (distance + tiles), tiles)

    barrier = pltpu.get_barrier_semaphore()
    for d in near + far:
        pl.semaphore_signal(barrier, inc=1, device_id={"tiles": at(d)}, device_id_type=MESH)
    for d in beside:
        pl.semaphore_signal(
            barrier, inc=1, device_id={"tiles": at(d), "subwin": 1 - sub}, device_id_type=MESH
        )

    lane = lax.broadcasted_iota(jnp.int32, (ROWS, LANES), 1)
    row = lax.broadcasted_iota(jnp.int32, (ROWS, LANES), 0)
    group = lane // span
    lat = lane % lats

    def joined(pieces):
        return jnp.concatenate(pieces, axis=1)

    def turned(x, by):
        by = by % LANES
        return x if by == 0 else pltpu.roll(x, by, 1)

    for load in loads:
        load.wait()
    inc = [
        joined([inc_ref[i, s, h * ROWS : (h + 1) * ROWS, :] for s in range(subs) for h in range(high)])
        for i in range(lons)
    ]
    dual = [
        joined([dual_ref[i, s, h * ROWS : (h + 1) * ROWS, :] for s in range(subs) for h in range(high)])
        for i in range(lons)
    ]
    wind_u = joined([u_ref[i, h * ROWS : (h + 1) * ROWS, :] for i in range(lons) for h in range(high)])
    wind_v = joined([v_ref[i, h * ROWS : (h + 1) * ROWS, :] for i in range(lons) for h in range(high)])
    mixing = 0.15 + 0.09 * land_ref[...].astype(jnp.float32)
    mixing = joined([mixing[i : i + 1] for i in range(lons) for h in range(high)])
    lengths = jnp.zeros((ROWS, LANES), jnp.float32)
    for s in range(subs):
        for b in range(bands):
            here = jnp.logical_and(group == s, lat == me * bands + b)
            lengths = jnp.where(here, length_ref[b : b + 1, s : s + 1], lengths)
    aux = jnp.where(row < ROWS // 2, lengths, jnp.broadcast_to(mixing, (ROWS, LANES)))
    last_inc = joined(
        [inc_ref[i, subs - 1, h * ROWS : (h + 1) * ROWS, :] for i in range(lons) for h in range(high)]
    )
    first_dual = joined(
        [dual_ref[i, 0, h * ROWS : (h + 1) * ROWS, :] for i in range(lons) for h in range(high)]
    )
    own = inc + [wind_u, wind_v, aux] + dual
    for n, tile in enumerate(own):
        data[0, n * ROWS : (n + 1) * ROWS, :] = tile
    cross[...] = jnp.where(sub == 0, last_inc, first_dual)

    pl.semaphore_wait(barrier, len(near) + len(far) + len(beside))

    far_from = (lons + 2) * ROWS
    near_copies, far_copies, cross_copies = [], [], []
    for d in near:
        copy = pltpu.make_async_remote_copy(
            src_ref=data.at[0],
            dst_ref=data.at[tiles - d],
            send_sem=send_sem.at[d],
            recv_sem=recv_sem.at[tiles - d],
            device_id={"tiles": at(d)},
            device_id_type=MESH,
        )
        copy.start()
        near_copies.append(copy)
    for d in beside:
        copy = pltpu.make_async_remote_copy(
            src_ref=cross,
            dst_ref=other.at[reach - d],
            send_sem=cross_send.at[reach + d],
            recv_sem=cross_recv.at[reach - d],
            device_id={"tiles": at(d), "subwin": 1 - sub},
            device_id_type=MESH,
        )
        copy.start()
        cross_copies.append(copy)
    for d in far:
        copy = pltpu.make_async_remote_copy(
            src_ref=data.at[0, pl.ds(far_from, (lons + 1) * ROWS)],
            dst_ref=data.at[tiles - d, pl.ds(far_from, (lons + 1) * ROWS)],
            send_sem=send_sem.at[d],
            recv_sem=recv_sem.at[tiles - d],
            device_id={"tiles": at(d)},
            device_id_type=MESH,
        )
        copy.start()
        far_copies.append(copy)

    spread = jnp.zeros((ROWS, LANES), jnp.float32)
    eye = lax.broadcasted_iota(jnp.int32, (ROWS, ROWS), 0) == lax.broadcasted_iota(
        jnp.int32, (ROWS, ROWS), 1
    )
    for s in range(subs):
        for h in range(high):
            line = spread_ref[s : s + 1, h * ROWS : (h + 1) * ROWS]
            column = jnp.sum(jnp.where(eye, jnp.broadcast_to(line, (ROWS, ROWS)), 0.0), 1, keepdims=True)
            spread = jnp.where(lane // lats == s * high + h, column, spread)

    for copy in near_copies + cross_copies:
        copy.wait_recv()

    def spread_out(x):
        parts = [turned(x, q * span) for q in range(lons)]
        outs = []
        for i in range(lons):
            out = parts[(0 - i) % lons]
            for g in range(1, subs):
                out = jnp.where(group == g, parts[(g - i) % lons], out)
            outs.append(out)
        return outs

    up = jnp.where(sub > 0, 1.0, 0.0)
    down = jnp.where(sub < 1, 1.0, 0.0)
    previous, following = [], []
    place = 0
    for d in beside:
        slot = d % tiles
        us = spread_out(data[slot, lons * ROWS : (lons + 1) * ROWS, :])
        vs = spread_out(data[slot, (lons + 1) * ROWS : (lons + 2) * ROWS, :])
        mix = data[slot, (lons + 2) * ROWS + ROWS // 2 : (lons + 2) * ROWS + ROWS // 2 + 1, :]
        mixes = spread_out(jnp.broadcast_to(mix, (ROWS, LANES)))
        beyond = other[d + reach]
        for i in range(lons):
            at_rows = pl.ds(place * ROWS, ROWS)
            m, u, v = mixes[i], 0.5 * us[i], 0.5 * vs[i]
            coef[0, at_rows, :] = 1.0 - 4.0 * m
            coef[1, at_rows, :] = m - u
            coef[2, at_rows, :] = m + u
            coef[3, at_rows, :] = jnp.where(lat == lats - 1, 0.0, m - v)
            coef[4, at_rows, :] = jnp.where(lat == 0, 0.0, m + v)
            place += 1
            f = data[slot, i * ROWS : (i + 1) * ROWS, :]
            g = data[slot, (lons + 3 + i) * ROWS : (lons + 4 + i) * ROWS, :]
            previous.append(
                jnp.where(group == 0, up * turned(beyond, -i * span), turned(f, span))
            )
            following.append(
                jnp.where(
                    group == subs - 1, down * turned(beyond, (subs - 1 - i) * span), turned(g, -span)
                )
            )
    extra = reach * lons - STEPS
    extent = place - 2 * extra
    f = jnp.concatenate(previous[extra : place - extra], axis=0)
    g = jnp.concatenate(following[extra : place - extra], axis=0)
    for step in range(STEPS):
        first = extra + step
        count = extent - 2 * step
        inner = pl.ds((first + 1) * ROWS, (count - 2) * ROWS)
        lower = pl.ds(first * ROWS, (count - 2) * ROWS)
        upper = pl.ds((first + 2) * ROWS, (count - 2) * ROWS)
        mid = f[ROWS:-ROWS]
        f = (
            coef[0, inner, :] * mid
            + coef[1, inner, :] * f[2 * ROWS :]
            + coef[2, inner, :] * f[: -2 * ROWS]
            + coef[3, inner, :] * turned(mid, -1)
            + coef[4, inner, :] * turned(mid, 1)
        )
        mid = g[ROWS:-ROWS]
        g = (
            coef[0, inner, :] * mid
            + coef[1, lower, :] * g[: -2 * ROWS]
            + coef[2, upper, :] * g[2 * ROWS :]
            + turned(coef[3, inner, :] * mid, 1)
            + turned(coef[4, inner, :] * mid, -1)
        )

    for copy in far_copies:
        copy.wait_recv()

    total = jnp.zeros((1, LANES), jnp.float32)
    for slot in range(tiles):
        total = total + data[slot, far_from : far_from + 1, :]
    weights = circulant_row(jnp.broadcast_to(total, (ROWS, LANES)), lons * tiles)
    smooth = [jnp.zeros((ROWS, LANES), jnp.float32) for _ in range(lons)]
    ring = lons * tiles
    for slot in range(tiles):
        for n in range(lons):
            x = data[slot, (lons + 3 + n) * ROWS : (lons + 4 + n) * ROWS, :]
            for i in range(lons):
                distance = (slot * lons + n - i) % ring
                smooth[i] = smooth[i] + weights[min(distance, ring - distance)] * x

    square = spread * spread
    for i in range(lons):
        here = slice(i * ROWS, (i + 1) * ROWS)
        packed_out[0, here, :] = square * smooth[i] + data[0, here, :] - f[here]
        rest = data[0, (lons + 3 + i) * ROWS : (lons + 4 + i) * ROWS, :]
        packed_out[1, here, :] = rest - g[here]

    for copy in near_copies + cross_copies + far_copies:
        copy.wait_send()


def unpack(packed_ref, model_out, dual_out):
    lons, subs, levs, lats = model_out.shape
    high = levs // ROWS
    for i in range(lons):
        for n, out in enumerate((model_out, dual_out)):
            tile = packed_ref[n, i * ROWS : (i + 1) * ROWS, :]
            for s in range(subs):
                for h in range(high):
                    by = (s * high + h) * lats
                    moved = pltpu.roll(tile, LANES - by, 1) if by else tile
                    out[i, s, h * ROWS : (h + 1) * ROWS, :] = moved[:, :lats]


def fills_tiles(tiles, subwins, increment):
    lons, subs, levs, lats = increment.shape
    reach = -(-STEPS // lons)
    return (
        subwins == 2
        and levs % ROWS == 0
        and subs == lons
        and subs * (levs // ROWS) * lats == LANES
        and 2 * reach < tiles <= 2 * ROWS
        and lons * tiles % 4 == 0
    )


def direct_body(increment, dual_vector, wind_u, wind_v, land_sea, length_sq, spread):
    tiles = lax.axis_size("tiles")
    lons = increment.shape[0]
    reach = -(-STEPS // lons)
    around = 2 * reach + 1
    vmem = pl.BlockSpec(memory_space=pltpu.VMEM)
    hbm = pl.BlockSpec(memory_space=pltpu.HBM)
    args = (increment, dual_vector, wind_u, wind_v, land_sea, length_sq.T, spread)
    result = jax.ShapeDtypeStruct(increment.shape, jnp.float32)
    packed = pl.pallas_call(
        functools.partial(kernel, tiles, reach),
        out_shape=jax.ShapeDtypeStruct((2, lons * ROWS, LANES), jnp.float32),
        in_specs=[hbm] * len(args),
        out_specs=vmem,
        scratch_shapes=[pltpu.VMEM(x.shape, x.dtype) for x in args]
        + [
            pltpu.VMEM((tiles, (2 * lons + 3) * ROWS, LANES), jnp.float32),
            pltpu.VMEM((ROWS, LANES), jnp.float32),
            pltpu.VMEM((around, ROWS, LANES), jnp.float32),
            pltpu.VMEM((5, around * lons * ROWS, LANES), jnp.float32),
            pltpu.SemaphoreType.DMA((tiles,)),
            pltpu.SemaphoreType.DMA((tiles,)),
            pltpu.SemaphoreType.DMA((around,)),
            pltpu.SemaphoreType.DMA((around,)),
            pltpu.SemaphoreType.DMA((len(args),)),
        ],
        compiler_params=pltpu.CompilerParams(collective_id=0, has_side_effects=True),
    )(*args)
    return pl.pallas_call(
        unpack, out_shape=(result, result), in_specs=[vmem], out_specs=(vmem, vmem)
    )(packed)


def body(*args):
    fits = fills_tiles(lax.axis_size("tiles"), lax.axis_size("subwin"), args[0])
    return direct_body(*args) if fits else stepwise_body(*args)


def solution(mesh):
    placed = (
        P(("groups", "tiles"), "subwin", None, None),
        P(("groups", "tiles"), "subwin", None, None),
        P("tiles", None, None),
        P("tiles", None, None),
        P("tiles", None),
        P("subwin", "tiles"),
        P("subwin", None),
    )
    return jax.shard_map(
        body,
        mesh=mesh,
        in_specs=placed,
        out_specs=(
            P(("groups", "tiles"), "subwin", None, None),
            P(("groups", "tiles"), "subwin", None, None),
        ),
        check_vma=False,
    )
```

```python
import functools
import math

import jax
import jax.numpy as jnp
from jax import lax
from jax.experimental import pallas as pl
from jax.experimental.pallas import tpu as pltpu
from jax.sharding import PartitionSpec as P

STEPS = 8
SWEEPS = 4
LON_DEV = 4


def extended(x, sides, width):
    for axis, dim in sides:
        devices, length = (lax.axis_size(axis), x.shape[dim])
        up = [(i, (i + 1) % devices) for i in range(devices)]
        down = [(j, i) for i, j in up]
        last = lax.slice_in_dim(x, length - width, length, axis=dim)
        leading = lax.slice_in_dim(x, 0, width, axis=dim)
        before = lax.ppermute(last, axis, up)
        after = lax.ppermute(leading, axis, down)
        x = jnp.concatenate([before, x, after], axis=dim)
    return x


def passed_along(x, axis, by):
    devices = lax.axis_size(axis)
    pairs = [(i, i + by) for i in range(devices) if 0 <= i + by < devices]
    return lax.ppermute(x, axis, pairs)


def from_north(values):
    return jnp.concatenate([values[..., 1:], jnp.zeros_like(values[..., :1])], axis=-1)


def from_south(values):
    return jnp.concatenate([jnp.zeros_like(values[..., :1]), values[..., :-1]], axis=-1)


def coefficients(wind_u, wind_v, mixing):
    return (
        1.0 - 4.0 * mixing,
        mixing - 0.5 * wind_u,
        mixing + 0.5 * wind_u,
        mixing - 0.5 * wind_v,
        mixing + 0.5 * wind_v,
    )


def tangent_step(fields, coeffs, offset):
    extent = fields.shape[0]
    centre, eastward, westward, northward, southward = [
        coeff[offset + 1 : offset + extent - 1][:, None] for coeff in coeffs
    ]
    middle = fields[1:-1]
    return (
        centre * middle
        + eastward * fields[2:]
        + westward * fields[:-2]
        + northward * from_north(middle)
        + southward * from_south(middle)
    )


def adjoint_step(fields, coeffs, offset):
    extent = fields.shape[0]
    centre = coeffs[0][offset + 1 : offset + extent - 1][:, None]
    northward = coeffs[3][offset + 1 : offset + extent - 1][:, None]
    southward = coeffs[4][offset + 1 : offset + extent - 1][:, None]
    eastward = coeffs[1][offset : offset + extent][:, None]
    westward = coeffs[2][offset : offset + extent][:, None]
    middle = fields[1:-1]
    return (
        centre * middle
        + (eastward * fields)[:-2]
        + (westward * fields)[2:]
        + from_south(northward * middle)
        + from_north(southward * middle)
    )


def run_tangent(fields, coeffs, margin):
    for repeat in range(STEPS // margin):
        grown = extended(fields, (("tiles", 0),), margin)
        for inner_step in range(margin):
            offset = (coeffs[0].shape[0] - grown.shape[0]) // 2
            grown = tangent_step(grown, coeffs, offset)
        fields = grown
    return fields


def run_adjoint(fields, coeffs, margin):
    for repeat in range(STEPS // margin):
        grown = extended(fields, (("tiles", 0),), margin)
        for inner_step in range(margin):
            offset = (coeffs[0].shape[0] - grown.shape[0]) // 2
            grown = adjoint_step(grown, coeffs, offset)
        fields = grown
    return fields


def square_tables(extent):
    index = jnp.arange(extent, dtype=jnp.int32)
    phases = index[:, None] * index[None, :] % extent
    angles = phases.astype(jnp.float32) * (2.0 * math.pi / extent)
    return (jnp.cos(angles), jnp.sin(angles))


def contract(form, first, second):
    return jnp.einsum(form, first, second, precision=lax.Precision.HIGHEST)


def smooth_bands(bands, length_sq):
    count = bands.shape[0]
    inner = LON_DEV
    outer = count // inner
    columns = bands.reshape(outer, inner, -1)
    cos_outer, sin_outer = square_tables(outer)
    cos_inner, sin_inner = square_tables(inner)
    outer_index = jnp.arange(outer, dtype=jnp.int32)
    inner_index = jnp.arange(inner, dtype=jnp.int32)
    twist = (outer_index[:, None] * inner_index[None, :] % count).astype(jnp.float32) * (
        2.0 * math.pi / count
    )
    twist_cos = jnp.cos(twist)[:, :, None]
    twist_sin = jnp.sin(twist)[:, :, None]
    first_real = contract("ab,bqc->aqc", cos_outer, columns)
    first_imag = -contract("ab,bqc->aqc", sin_outer, columns)
    turned_real = first_real * twist_cos + first_imag * twist_sin
    turned_imag = first_imag * twist_cos - first_real * twist_sin
    modes_real = contract("aqc,kq->akc", turned_real, cos_inner) + contract(
        "aqc,kq->akc", turned_imag, sin_inner
    )
    modes_imag = contract("aqc,kq->akc", turned_imag, cos_inner) - contract(
        "aqc,kq->akc", turned_real, sin_inner
    )
    wave = (outer_index[:, None] + outer * inner_index[None, :]).astype(jnp.float32)
    basic = 1.0 - jnp.cos(wave * (2.0 * math.pi / count))
    damping = (1.0 + 2.0 * length_sq[None, None, :, None, :] * basic[:, :, None, None, None]) ** (
        -SWEEPS
    )
    damping = jnp.broadcast_to(damping, (outer, inner) + bands.shape[1:]).reshape(outer, inner, -1)
    modes_real = modes_real * damping
    modes_imag = modes_imag * damping
    back_real = contract("akc,kq->aqc", modes_real, cos_inner) - contract(
        "akc,kq->aqc", modes_imag, sin_inner
    )
    back_imag = contract("akc,kq->aqc", modes_imag, cos_inner) + contract(
        "akc,kq->aqc", modes_real, sin_inner
    )
    final_real = back_real * twist_cos - back_imag * twist_sin
    final_imag = back_imag * twist_cos + back_real * twist_sin
    smoothed = contract("ab,bqc->aqc", cos_outer, final_real) - contract(
        "ab,bqc->aqc", sin_outer, final_imag
    )
    return (smoothed / count).reshape(bands.shape)


def stepwise_body(increment, dual_vector, wind_u, wind_v, land_sea, length_sq, spread):
    margin = 4
    mixing = 0.15 + 0.09 * land_sea.astype(jnp.float32)
    grown_u, grown_v, grown_mix = (
        extended(wind_u, (("tiles", 0),), margin),
        extended(wind_v, (("tiles", 0),), margin),
        extended(mixing, (("tiles", 0),), margin),
    )
    coeffs = coefficients(grown_u, grown_v, grown_mix[:, None, :])
    carried = passed_along(increment[:, -1:], "subwin", 1)
    previous = jnp.concatenate([carried, increment[:, :-1]], axis=1)
    later = passed_along(dual_vector[:, :1], "subwin", -1)
    following = jnp.concatenate([dual_vector[:, 1:], later], axis=1)
    weighted = dual_vector * spread[None, :, :, None]
    bands = lax.all_to_all(weighted, "tiles", split_axis=3, concat_axis=0, tiled=True)
    smoothed = smooth_bands(bands, length_sq)
    forward = run_tangent(previous, coeffs, margin)
    backward = run_adjoint(following, coeffs, margin)
    returned = lax.all_to_all(smoothed, "tiles", split_axis=0, concat_axis=3, tiled=True)
    covar = returned * spread[None, :, :, None]
    return (covar + increment - forward, dual_vector - backward)


ROWS = 8
LANES = 128
MESH = pl.DeviceIdType.MESH


def circulant_row(lengths, count):
    half = count // 2
    damped = []
    for wave in range(half + 1):
        basic = 1.0 - math.cos(2.0 * math.pi * wave / count)
        base = 1.0 + (2.0 * basic) * lengths
        power = base
        for _ in range(SWEEPS - 1):
            power = power * base
        weight = (1.0 if wave in (0, half) else 2.0) / count
        damped.append(weight / power)
    row = [None] * (half + 1)
    for distance in range(half // 2 + 1):
        sums = [jnp.zeros_like(lengths), jnp.zeros_like(lengths)]
        for wave in range(half + 1):
            factor = math.cos(2.0 * math.pi * (wave * distance % count) / count)
            sums[wave % 2] = sums[wave % 2] + factor * damped[wave]
        row[distance] = sums[0] + sums[1]
        row[half - distance] = sums[0] - sums[1]
    return row


def kernel(
    tiles,
    reach,
    *refs,
):
    count = 7
    held, packed_out = refs[:count], refs[count]
    here_refs = refs[count + 1 : 2 * count + 1]
    inc_ref, dual_ref, u_ref, v_ref, land_ref, length_ref, spread_ref = here_refs
    (
        halo,
        cross,
        other,
        coef,
        bands_out,
        bands_in,
        smooth_out,
        smooth_in,
        halo_send,
        halo_recv,
        cross_send,
        cross_recv,
        band_send,
        band_recv,
        back_send,
        back_recv,
        load_sem,
    ) = refs[2 * count + 1 :]
    loads = [
        pltpu.make_async_copy(held[n], here_refs[n], load_sem.at[n]) for n in range(count)
    ]
    for load in loads:
        load.start()
    lons, subs, levs, lats = inc_ref.shape
    high = levs // ROWS
    span = high * lats
    width = length_ref.shape[0]
    ring = lons * tiles
    merged = tiles // lons
    me = lax.axis_index("tiles")
    sub = lax.axis_index("subwin")
    others = list(range(1, tiles))
    beside = list(range(-reach, reach + 1))
    near = [d for d in beside if d]

    def at(distance):
        return lax.rem(me + (distance + tiles), tiles)

    barrier = pltpu.get_barrier_semaphore()
    for d in others:
        pl.semaphore_signal(barrier, inc=1, device_id={"tiles": at(d)}, device_id_type=MESH)
    for d in beside:
        pl.semaphore_signal(
            barrier, inc=1, device_id={"tiles": at(d), "subwin": 1 - sub}, device_id_type=MESH
        )

    lane = lax.broadcasted_iota(jnp.int32, (ROWS, LANES), 1)
    row = lax.broadcasted_iota(jnp.int32, (ROWS, LANES), 0)
    group = lane // span
    lat = lane % lats

    def joined(pieces):
        return jnp.concatenate(pieces, axis=1)

    def turned(x, by):
        by = by % LANES
        return x if by == 0 else pltpu.roll(x, by, 1)

    for load in loads:
        load.wait()
    def pieces(ref, *index):
        return [ref[(*index, slice(h * ROWS, (h + 1) * ROWS), slice(None))] for h in range(high)]

    inc, dual = [], []
    for i in range(lons):
        of_inc = [pieces(inc_ref, i, s) for s in range(subs)]
        of_dual = [pieces(dual_ref, i, s) for s in range(subs)]
        inc.append(joined(sum(of_inc, [])))
        dual.append(joined(sum(of_dual, [])))
        halo[reach, i * ROWS : (i + 1) * ROWS, :] = joined(sum(of_inc[:-1], []) + pieces(u_ref, i))
        halo[reach, (lons + i) * ROWS : (lons + i + 1) * ROWS, :] = joined(
            pieces(v_ref, i) + sum(of_dual[1:], [])
        )
    mixing = 0.15 + 0.09 * land_ref[...].astype(jnp.float32)
    mixing = joined([mixing[i : i + 1] for i in range(lons) for h in range(high)])
    halo[reach, 2 * lons * ROWS :, :] = jnp.broadcast_to(mixing, (ROWS, LANES))
    last_inc = joined(sum([pieces(inc_ref, i, subs - 1) for i in range(lons)], []))
    first_dual = joined(sum([pieces(dual_ref, i, 0) for i in range(lons)], []))
    cross[...] = jnp.where(sub == 0, last_inc, first_dual)
    slot = lat // width
    for t in range(tiles):
        out = turned(dual[0], -width * t)
        for i in range(1, lons):
            out = jnp.where(slot == i, turned(dual[i], width * (i - t)), out)
        bands_out[t] = out

    pl.semaphore_wait(barrier, len(others) + len(beside))

    band_copies, near_copies, cross_copies, back_copies = [], [], [], []
    for d in others:
        copy = pltpu.make_async_remote_copy(
            src_ref=bands_out.at[at(d)],
            dst_ref=bands_in.at[me],
            send_sem=band_send.at[d],
            recv_sem=band_recv.at[tiles - d],
            device_id={"tiles": at(d)},
            device_id_type=MESH,
        )
        copy.start()
        band_copies.append(copy)
    for d in near:
        copy = pltpu.make_async_remote_copy(
            src_ref=halo.at[reach],
            dst_ref=halo.at[reach - d],
            send_sem=halo_send.at[reach + d],
            recv_sem=halo_recv.at[reach - d],
            device_id={"tiles": at(d)},
            device_id_type=MESH,
        )
        copy.start()
        near_copies.append(copy)
    for d in beside:
        copy = pltpu.make_async_remote_copy(
            src_ref=cross,
            dst_ref=other.at[reach - d],
            send_sem=cross_send.at[reach + d],
            recv_sem=cross_recv.at[reach - d],
            device_id={"tiles": at(d), "subwin": 1 - sub},
            device_id_type=MESH,
        )
        copy.start()
        cross_copies.append(copy)
    bands_in[pl.ds(me, 1)] = bands_out[pl.ds(me, 1)]

    lengths = jnp.zeros((ROWS, LANES), jnp.float32)
    for s in range(subs):
        for b in range(width):
            here = jnp.logical_and(group == s, lane % width == b)
            lengths = jnp.where(here, length_ref[b : b + 1, s : s + 1], lengths)
    weights = circulant_row(lengths, ring)

    def weight(distance):
        distance = distance % ring
        return weights[min(distance, ring - distance)]

    turned_weights = [
        [jnp.where(slot >= r, weight(tiles * k + r), weight(tiles * k + r - tiles)) for r in range(tiles)]
        for k in range(lons)
    ]

    spread = jnp.zeros((ROWS, LANES), jnp.float32)
    eye = lax.broadcasted_iota(jnp.int32, (ROWS, ROWS), 0) == lax.broadcasted_iota(
        jnp.int32, (ROWS, ROWS), 1
    )
    for s in range(subs):
        for h in range(high):
            line = spread_ref[s : s + 1, h * ROWS : (h + 1) * ROWS]
            column = jnp.sum(jnp.where(eye, jnp.broadcast_to(line, (ROWS, ROWS)), 0.0), 1, keepdims=True)
            spread = jnp.where(lane // lats == s * high + h, column, spread)

    for copy in band_copies:
        copy.wait_recv()
    sums = [jnp.zeros((ROWS, LANES), jnp.float32) for _ in range(lons)]
    for m in range(lons):
        x = bands_in[m * merged]
        for p in range(1, merged):
            x = jnp.where(slot // lons == p, turned(bands_in[m * merged + p], p * lons * width), x)
        for r in range(tiles):
            moved = x
            if r:
                moved = jnp.where(slot >= r, turned(x, r * width), turned(x, r * width - lats))
            for n in range(lons):
                sums[n] = sums[n] + turned_weights[(n - m) % lons][r] * moved
    for n in range(lons):
        smooth_out[n] = sums[n]
    for d in others:
        copy = pltpu.make_async_remote_copy(
            src_ref=smooth_out.at[lax.div(at(d), merged)],
            dst_ref=smooth_in.at[me],
            send_sem=back_send.at[d],
            recv_sem=back_recv.at[tiles - d],
            device_id={"tiles": at(d)},
            device_id_type=MESH,
        )
        copy.start()
        back_copies.append(copy)
    smooth_in[pl.ds(me, 1)] = smooth_out[pl.ds(lax.div(me, merged), 1)]

    for copy in near_copies + cross_copies:
        copy.wait_recv()

    def spread_out(x):
        parts = [turned(x, q * span) for q in range(lons)]
        outs = []
        for i in range(lons):
            out = parts[(0 - i) % lons]
            for g in range(1, subs):
                out = jnp.where(group == g, parts[(g - i) % lons], out)
            outs.append(out)
        return outs

    def to_all(x, g):
        x = jnp.where(group == g, x, 0.0)
        outs = x
        by = 1
        while by < subs:
            outs = outs + turned(outs, by * span)
            by *= 2
        return outs

    up = jnp.where(sub > 0, 1.0, 0.0)
    down = jnp.where(sub < 1, 1.0, 0.0)
    previous, following = [], []
    place = 0
    for d in beside:
        at_tile = d + reach
        mixes = spread_out(halo[at_tile, 2 * lons * ROWS :, :])
        beyond = other[d + reach]
        for i in range(lons):
            at_rows = pl.ds(place * ROWS, ROWS)
            f = halo[at_tile, i * ROWS : (i + 1) * ROWS, :]
            g = halo[at_tile, (lons + i) * ROWS : (lons + i + 1) * ROWS, :]
            m, u, v = mixes[i], 0.5 * to_all(f, subs - 1), 0.5 * to_all(g, 0)
            coef[0, at_rows, :] = 1.0 - 4.0 * m
            coef[1, at_rows, :] = m - u
            coef[2, at_rows, :] = m + u
            coef[3, at_rows, :] = jnp.where(lat == lats - 1, 0.0, m - v)
            coef[4, at_rows, :] = jnp.where(lat == 0, 0.0, m + v)
            place += 1
            previous.append(
                jnp.where(group == 0, up * turned(beyond, -i * span), turned(f, span))
            )
            following.append(
                jnp.where(
                    group == subs - 1, down * turned(beyond, (subs - 1 - i) * span), turned(g, -span)
                )
            )
    extra = reach * lons - STEPS
    extent = place - 2 * extra
    f = jnp.concatenate(previous[extra : place - extra], axis=0)
    g = jnp.concatenate(following[extra : place - extra], axis=0)
    for step in range(STEPS):
        first = extra + step
        count = extent - 2 * step
        inner = pl.ds((first + 1) * ROWS, (count - 2) * ROWS)
        lower = pl.ds(first * ROWS, (count - 2) * ROWS)
        upper = pl.ds((first + 2) * ROWS, (count - 2) * ROWS)
        mid = f[ROWS:-ROWS]
        f = (
            coef[0, inner, :] * mid
            + coef[1, inner, :] * f[2 * ROWS :]
            + coef[2, inner, :] * f[: -2 * ROWS]
            + coef[3, inner, :] * turned(mid, -1)
            + coef[4, inner, :] * turned(mid, 1)
        )
        mid = g[ROWS:-ROWS]
        g = (
            coef[0, inner, :] * mid
            + coef[1, lower, :] * g[: -2 * ROWS]
            + coef[2, upper, :] * g[2 * ROWS :]
            + turned(coef[3, inner, :] * mid, 1)
            + turned(coef[4, inner, :] * mid, -1)
        )

    for copy in back_copies:
        copy.wait_recv()
    own_part = lax.rem(me, merged)
    returned = []
    for t in range(tiles):
        x = smooth_in[t]
        out = x
        for p in range(1, merged):
            out = jnp.where(own_part == p, turned(x, -p * lons * width), out)
        returned.append(out)
    square = spread * spread
    for i in range(lons):
        here = slice(i * ROWS, (i + 1) * ROWS)
        smooth = turned(returned[0], -i * width)
        for t in range(1, tiles):
            smooth = jnp.where(slot == t, turned(returned[t], (t - i) * width), smooth)
        packed_out[0, here, :] = square * smooth + inc[i] - f[here]
        packed_out[1, here, :] = dual[i] - g[here]

    for copy in band_copies + near_copies + cross_copies + back_copies:
        copy.wait_send()


def unpack(packed_ref, model_out, dual_out):
    lons, subs, levs, lats = model_out.shape
    high = levs // ROWS
    for i in range(lons):
        for n, out in enumerate((model_out, dual_out)):
            tile = packed_ref[n, i * ROWS : (i + 1) * ROWS, :]
            for s in range(subs):
                for h in range(high):
                    by = (s * high + h) * lats
                    moved = pltpu.roll(tile, LANES - by, 1) if by else tile
                    out[i, s, h * ROWS : (h + 1) * ROWS, :] = moved[:, :lats]


def fills_tiles(tiles, subwins, increment):
    lons, subs, levs, lats = increment.shape
    reach = -(-STEPS // lons)
    return (
        subwins == 2
        and levs % ROWS == 0
        and subs == lons
        and subs * (levs // ROWS) * lats == LANES
        and 2 * reach < tiles <= 2 * ROWS
        and tiles % lons == 0
        and lats % tiles == 0
        and lons & (lons - 1) == 0
    )


def direct_body(increment, dual_vector, wind_u, wind_v, land_sea, length_sq, spread):
    tiles = lax.axis_size("tiles")
    lons = increment.shape[0]
    reach = -(-STEPS // lons)
    around = 2 * reach + 1
    vmem = pl.BlockSpec(memory_space=pltpu.VMEM)
    hbm = pl.BlockSpec(memory_space=pltpu.HBM)
    args = (increment, dual_vector, wind_u, wind_v, land_sea, length_sq.T, spread)
    result = jax.ShapeDtypeStruct(increment.shape, jnp.float32)
    packed = pl.pallas_call(
        functools.partial(kernel, tiles, reach),
        out_shape=jax.ShapeDtypeStruct((2, lons * ROWS, LANES), jnp.float32),
        in_specs=[hbm] * len(args),
        out_specs=vmem,
        scratch_shapes=[pltpu.VMEM(x.shape, x.dtype) for x in args]
        + [
            pltpu.VMEM((around, (2 * lons + 1) * ROWS, LANES), jnp.float32),
            pltpu.VMEM((ROWS, LANES), jnp.float32),
            pltpu.VMEM((around, ROWS, LANES), jnp.float32),
            pltpu.VMEM((5, around * lons * ROWS, LANES), jnp.float32),
            pltpu.VMEM((tiles, ROWS, LANES), jnp.float32),
            pltpu.VMEM((tiles, ROWS, LANES), jnp.float32),
            pltpu.VMEM((lons, ROWS, LANES), jnp.float32),
            pltpu.VMEM((tiles, ROWS, LANES), jnp.float32),
        ]
        + [pltpu.SemaphoreType.DMA((size,)) for size in (around,) * 4 + (tiles,) * 4]
        + [
            pltpu.SemaphoreType.DMA((len(args),)),
        ],
        compiler_params=pltpu.CompilerParams(collective_id=0, has_side_effects=True),
    )(*args)
    return pl.pallas_call(
        unpack, out_shape=(result, result), in_specs=[vmem], out_specs=(vmem, vmem)
    )(packed)


def body(*args):
    fits = fills_tiles(lax.axis_size("tiles"), lax.axis_size("subwin"), args[0])
    return direct_body(*args) if fits else stepwise_body(*args)


def solution(mesh):
    placed = (
        P(("groups", "tiles"), "subwin", None, None),
        P(("groups", "tiles"), "subwin", None, None),
        P("tiles", None, None),
        P("tiles", None, None),
        P("tiles", None),
        P("subwin", "tiles"),
        P("subwin", None),
    )
    return jax.shard_map(
        body,
        mesh=mesh,
        in_specs=placed,
        out_specs=(
            P(("groups", "tiles"), "subwin", None, None),
            P(("groups", "tiles"), "subwin", None, None),
        ),
        check_vma=False,
    )
```

```python
import functools
import math

import jax
import jax.numpy as jnp
from jax import lax
from jax.experimental import pallas as pl
from jax.experimental.pallas import tpu as pltpu
from jax.sharding import PartitionSpec as P

STEPS = 8
SWEEPS = 4
LON_DEV = 4


def extended(x, sides, width):
    for axis, dim in sides:
        devices, length = (lax.axis_size(axis), x.shape[dim])
        up = [(i, (i + 1) % devices) for i in range(devices)]
        down = [(j, i) for i, j in up]
        last = lax.slice_in_dim(x, length - width, length, axis=dim)
        leading = lax.slice_in_dim(x, 0, width, axis=dim)
        before = lax.ppermute(last, axis, up)
        after = lax.ppermute(leading, axis, down)
        x = jnp.concatenate([before, x, after], axis=dim)
    return x


def passed_along(x, axis, by):
    devices = lax.axis_size(axis)
    pairs = [(i, i + by) for i in range(devices) if 0 <= i + by < devices]
    return lax.ppermute(x, axis, pairs)


def from_north(values):
    return jnp.concatenate([values[..., 1:], jnp.zeros_like(values[..., :1])], axis=-1)


def from_south(values):
    return jnp.concatenate([jnp.zeros_like(values[..., :1]), values[..., :-1]], axis=-1)


def coefficients(wind_u, wind_v, mixing):
    return (
        1.0 - 4.0 * mixing,
        mixing - 0.5 * wind_u,
        mixing + 0.5 * wind_u,
        mixing - 0.5 * wind_v,
        mixing + 0.5 * wind_v,
    )


def tangent_step(fields, coeffs, offset):
    extent = fields.shape[0]
    centre, eastward, westward, northward, southward = [
        coeff[offset + 1 : offset + extent - 1][:, None] for coeff in coeffs
    ]
    middle = fields[1:-1]
    return (
        centre * middle
        + eastward * fields[2:]
        + westward * fields[:-2]
        + northward * from_north(middle)
        + southward * from_south(middle)
    )


def adjoint_step(fields, coeffs, offset):
    extent = fields.shape[0]
    centre = coeffs[0][offset + 1 : offset + extent - 1][:, None]
    northward = coeffs[3][offset + 1 : offset + extent - 1][:, None]
    southward = coeffs[4][offset + 1 : offset + extent - 1][:, None]
    eastward = coeffs[1][offset : offset + extent][:, None]
    westward = coeffs[2][offset : offset + extent][:, None]
    middle = fields[1:-1]
    return (
        centre * middle
        + (eastward * fields)[:-2]
        + (westward * fields)[2:]
        + from_south(northward * middle)
        + from_north(southward * middle)
    )


def run_tangent(fields, coeffs, margin):
    for repeat in range(STEPS // margin):
        grown = extended(fields, (("tiles", 0),), margin)
        for inner_step in range(margin):
            offset = (coeffs[0].shape[0] - grown.shape[0]) // 2
            grown = tangent_step(grown, coeffs, offset)
        fields = grown
    return fields


def run_adjoint(fields, coeffs, margin):
    for repeat in range(STEPS // margin):
        grown = extended(fields, (("tiles", 0),), margin)
        for inner_step in range(margin):
            offset = (coeffs[0].shape[0] - grown.shape[0]) // 2
            grown = adjoint_step(grown, coeffs, offset)
        fields = grown
    return fields


def square_tables(extent):
    index = jnp.arange(extent, dtype=jnp.int32)
    phases = index[:, None] * index[None, :] % extent
    angles = phases.astype(jnp.float32) * (2.0 * math.pi / extent)
    return (jnp.cos(angles), jnp.sin(angles))


def contract(form, first, second):
    return jnp.einsum(form, first, second, precision=lax.Precision.HIGHEST)


def smooth_bands(bands, length_sq):
    count = bands.shape[0]
    inner = LON_DEV
    outer = count // inner
    columns = bands.reshape(outer, inner, -1)
    cos_outer, sin_outer = square_tables(outer)
    cos_inner, sin_inner = square_tables(inner)
    outer_index = jnp.arange(outer, dtype=jnp.int32)
    inner_index = jnp.arange(inner, dtype=jnp.int32)
    twist = (outer_index[:, None] * inner_index[None, :] % count).astype(jnp.float32) * (
        2.0 * math.pi / count
    )
    twist_cos = jnp.cos(twist)[:, :, None]
    twist_sin = jnp.sin(twist)[:, :, None]
    first_real = contract("ab,bqc->aqc", cos_outer, columns)
    first_imag = -contract("ab,bqc->aqc", sin_outer, columns)
    turned_real = first_real * twist_cos + first_imag * twist_sin
    turned_imag = first_imag * twist_cos - first_real * twist_sin
    modes_real = contract("aqc,kq->akc", turned_real, cos_inner) + contract(
        "aqc,kq->akc", turned_imag, sin_inner
    )
    modes_imag = contract("aqc,kq->akc", turned_imag, cos_inner) - contract(
        "aqc,kq->akc", turned_real, sin_inner
    )
    wave = (outer_index[:, None] + outer * inner_index[None, :]).astype(jnp.float32)
    basic = 1.0 - jnp.cos(wave * (2.0 * math.pi / count))
    damping = (1.0 + 2.0 * length_sq[None, None, :, None, :] * basic[:, :, None, None, None]) ** (
        -SWEEPS
    )
    damping = jnp.broadcast_to(damping, (outer, inner) + bands.shape[1:]).reshape(outer, inner, -1)
    modes_real = modes_real * damping
    modes_imag = modes_imag * damping
    back_real = contract("akc,kq->aqc", modes_real, cos_inner) - contract(
        "akc,kq->aqc", modes_imag, sin_inner
    )
    back_imag = contract("akc,kq->aqc", modes_imag, cos_inner) + contract(
        "akc,kq->aqc", modes_real, sin_inner
    )
    final_real = back_real * twist_cos - back_imag * twist_sin
    final_imag = back_imag * twist_cos + back_real * twist_sin
    smoothed = contract("ab,bqc->aqc", cos_outer, final_real) - contract(
        "ab,bqc->aqc", sin_outer, final_imag
    )
    return (smoothed / count).reshape(bands.shape)


def stepwise_body(increment, dual_vector, wind_u, wind_v, land_sea, length_sq, spread):
    margin = 4
    mixing = 0.15 + 0.09 * land_sea.astype(jnp.float32)
    grown_u, grown_v, grown_mix = (
        extended(wind_u, (("tiles", 0),), margin),
        extended(wind_v, (("tiles", 0),), margin),
        extended(mixing, (("tiles", 0),), margin),
    )
    coeffs = coefficients(grown_u, grown_v, grown_mix[:, None, :])
    carried = passed_along(increment[:, -1:], "subwin", 1)
    previous = jnp.concatenate([carried, increment[:, :-1]], axis=1)
    later = passed_along(dual_vector[:, :1], "subwin", -1)
    following = jnp.concatenate([dual_vector[:, 1:], later], axis=1)
    weighted = dual_vector * spread[None, :, :, None]
    bands = lax.all_to_all(weighted, "tiles", split_axis=3, concat_axis=0, tiled=True)
    smoothed = smooth_bands(bands, length_sq)
    forward = run_tangent(previous, coeffs, margin)
    backward = run_adjoint(following, coeffs, margin)
    returned = lax.all_to_all(smoothed, "tiles", split_axis=0, concat_axis=3, tiled=True)
    covar = returned * spread[None, :, :, None]
    return (covar + increment - forward, dual_vector - backward)


ROWS = 8
LANES = 128
MESH = pl.DeviceIdType.MESH


def circulant_row(lengths, count):
    half = count // 2
    damped = []
    for wave in range(half + 1):
        basic = 1.0 - math.cos(2.0 * math.pi * wave / count)
        base = 1.0 + (2.0 * basic) * lengths
        power = base
        for _ in range(SWEEPS - 1):
            power = power * base
        weight = (1.0 if wave in (0, half) else 2.0) / count
        damped.append(weight / power)
    row = [None] * (half + 1)
    for distance in range(half // 2 + 1):
        sums = [jnp.zeros_like(lengths), jnp.zeros_like(lengths)]
        for wave in range(half + 1):
            factor = math.cos(2.0 * math.pi * (wave * distance % count) / count)
            sums[wave % 2] = sums[wave % 2] + factor * damped[wave]
        row[distance] = sums[0] + sums[1]
        row[half - distance] = sums[0] - sums[1]
    return row


def kernel(
    tiles,
    reach,
    *refs,
):
    count = 7
    held, packed_out = refs[:count], refs[count]
    here_refs = refs[count + 1 : 2 * count + 1]
    inc_ref, dual_ref, u_ref, v_ref, land_ref, length_ref, spread_ref = here_refs
    (
    data,
    rows,
    cross,
    other,
    coef,
    send_sem,
    recv_sem,
    row_send,
    row_recv,
    cross_send,
    cross_recv,
    load_sem,
    ) = refs[2 * count + 1 :]
    loads = [
        pltpu.make_async_copy(held[n], here_refs[n], load_sem.at[n]) for n in range(count)
    ]
    for load in loads:
        load.start()
    lons, subs, levs, lats = inc_ref.shape
    high = levs // ROWS
    span = high * lats
    bands = length_ref.shape[0]
    me = lax.axis_index("tiles")
    sub = lax.axis_index("subwin")
    near = [d for d in range(1, reach + 1)] + [tiles - d for d in range(1, reach + 1)]
    far = [d for d in range(1, tiles) if d not in near]
    beside = list(range(-reach, reach + 1))

    def at(distance):
        return lax.rem(me + (distance + tiles), tiles)

    barrier = pltpu.get_barrier_semaphore()
    for d in near + far:
        pl.semaphore_signal(barrier, inc=1, device_id={"tiles": at(d)}, device_id_type=MESH)
    for d in beside:
        pl.semaphore_signal(
            barrier, inc=1, device_id={"tiles": at(d), "subwin": 1 - sub}, device_id_type=MESH
        )

    lane = lax.broadcasted_iota(jnp.int32, (ROWS, LANES), 1)
    row = lax.broadcasted_iota(jnp.int32, (ROWS, LANES), 0)
    group = lane // span
    lat = lane % lats

    def joined(pieces):
        return jnp.concatenate(pieces, axis=1)

    def turned(x, by):
        by = by % LANES
        return x if by == 0 else pltpu.roll(x, by, 1)

    for load in loads:
        load.wait()
    inc = [
        joined([inc_ref[i, s, h * ROWS : (h + 1) * ROWS, :] for s in range(subs) for h in range(high)])
        for i in range(lons)
    ]
    dual = [
        joined([dual_ref[i, s, h * ROWS : (h + 1) * ROWS, :] for s in range(subs) for h in range(high)])
        for i in range(lons)
    ]
    wind_v = joined([v_ref[i, h * ROWS : (h + 1) * ROWS, :] for i in range(lons) for h in range(high)])
    mixing = 0.15 + 0.09 * land_ref[...].astype(jnp.float32)
    mixing = joined([mixing[i : i + 1] for i in range(lons) for h in range(high)])
    lengths = jnp.zeros((ROWS, LANES), jnp.float32)
    for s in range(subs):
        for b in range(bands):
            here = jnp.logical_and(group == s, lat == me * bands + b)
            lengths = jnp.where(here, length_ref[b : b + 1, s : s + 1], lengths)
    rows[0, 0:1, :] = lengths[:1]
    rows[0, 1:2, :] = mixing
    last_inc = joined(
        [inc_ref[i, subs - 1, h * ROWS : (h + 1) * ROWS, :] for i in range(lons) for h in range(high)]
    )
    first_dual = joined(
        [dual_ref[i, 0, h * ROWS : (h + 1) * ROWS, :] for i in range(lons) for h in range(high)]
    )
    inc_u = [
        joined(
            [inc_ref[i, s, h * ROWS : (h + 1) * ROWS, :] for s in range(subs - 1) for h in range(high)]
            + [u_ref[i, h * ROWS : (h + 1) * ROWS, :] for h in range(high)]
        )
        for i in range(lons)
    ]
    own = inc_u + [wind_v] + dual
    for n, tile in enumerate(own):
        data[0, n * ROWS : (n + 1) * ROWS, :] = tile
    cross[...] = jnp.where(sub == 0, last_inc, first_dual)

    pl.semaphore_wait(barrier, len(near) + len(far) + len(beside))

    far_from = (lons + 1) * ROWS
    near_copies, far_copies, cross_copies, row_copies = [], [], [], []
    for d in near + far:
        copy = pltpu.make_async_remote_copy(
            src_ref=rows.at[0],
            dst_ref=rows.at[tiles - d],
            send_sem=row_send.at[d],
            recv_sem=row_recv.at[tiles - d],
            device_id={"tiles": at(d)},
            device_id_type=MESH,
        )
        copy.start()
        row_copies.append(copy)
    for d in near:
        copy = pltpu.make_async_remote_copy(
            src_ref=data.at[0],
            dst_ref=data.at[tiles - d],
            send_sem=send_sem.at[d],
            recv_sem=recv_sem.at[tiles - d],
            device_id={"tiles": at(d)},
            device_id_type=MESH,
        )
        copy.start()
        near_copies.append(copy)
    for d in beside:
        copy = pltpu.make_async_remote_copy(
            src_ref=cross,
            dst_ref=other.at[reach - d],
            send_sem=cross_send.at[reach + d],
            recv_sem=cross_recv.at[reach - d],
            device_id={"tiles": at(d), "subwin": 1 - sub},
            device_id_type=MESH,
        )
        copy.start()
        cross_copies.append(copy)
    for d in far:
        copy = pltpu.make_async_remote_copy(
            src_ref=data.at[0, pl.ds(far_from, lons * ROWS)],
            dst_ref=data.at[tiles - d, pl.ds(far_from, lons * ROWS)],
            send_sem=send_sem.at[d],
            recv_sem=recv_sem.at[tiles - d],
            device_id={"tiles": at(d)},
            device_id_type=MESH,
        )
        copy.start()
        far_copies.append(copy)

    spread = jnp.zeros((ROWS, LANES), jnp.float32)
    eye = lax.broadcasted_iota(jnp.int32, (ROWS, ROWS), 0) == lax.broadcasted_iota(
        jnp.int32, (ROWS, ROWS), 1
    )
    for s in range(subs):
        for h in range(high):
            line = spread_ref[s : s + 1, h * ROWS : (h + 1) * ROWS]
            column = jnp.sum(jnp.where(eye, jnp.broadcast_to(line, (ROWS, ROWS)), 0.0), 1, keepdims=True)
            spread = jnp.where(lane // lats == s * high + h, column, spread)

    for copy in row_copies:
        copy.wait_recv()
    total = jnp.zeros((1, LANES), jnp.float32)
    for slot in range(tiles):
        total = total + rows[slot, 0:1, :]
    weights = circulant_row(jnp.broadcast_to(total, (ROWS, LANES)), lons * tiles)

    for copy in near_copies + cross_copies:
        copy.wait_recv()

    def spread_out(x):
        parts = [turned(x, q * span) for q in range(lons)]
        outs = []
        for i in range(lons):
            out = parts[(0 - i) % lons]
            for g in range(1, subs):
                out = jnp.where(group == g, parts[(g - i) % lons], out)
            outs.append(out)
        return outs

    def to_all(x, g):
        outs = jnp.where(group == g, x, 0.0)
        by = 1
        while by < subs:
            outs = outs + turned(outs, by * span)
            by *= 2
        return outs

    up = jnp.where(sub > 0, 1.0, 0.0)
    down = jnp.where(sub < 1, 1.0, 0.0)
    previous, following = [], []
    place = 0
    for d in beside:
        slot = d % tiles
        vs = spread_out(data[slot, lons * ROWS : (lons + 1) * ROWS, :])
        mixes = spread_out(jnp.broadcast_to(rows[slot, 1:2, :], (ROWS, LANES)))
        beyond = other[d + reach]
        for i in range(lons):
            at_rows = pl.ds(place * ROWS, ROWS)
            f = data[slot, i * ROWS : (i + 1) * ROWS, :]
            m, u, v = mixes[i], 0.5 * to_all(f, subs - 1), 0.5 * vs[i]
            coef[0, at_rows, :] = 1.0 - 4.0 * m
            coef[1, at_rows, :] = m - u
            coef[2, at_rows, :] = m + u
            coef[3, at_rows, :] = jnp.where(lat == lats - 1, 0.0, m - v)
            coef[4, at_rows, :] = jnp.where(lat == 0, 0.0, m + v)
            place += 1
            g = data[slot, (lons + 1 + i) * ROWS : (lons + 2 + i) * ROWS, :]
            previous.append(
                jnp.where(group == 0, up * turned(beyond, -i * span), turned(f, span))
            )
            following.append(
                jnp.where(
                    group == subs - 1, down * turned(beyond, (subs - 1 - i) * span), turned(g, -span)
                )
            )
    extra = reach * lons - STEPS
    extent = place - 2 * extra
    f = jnp.concatenate(previous[extra : place - extra], axis=0)
    g = jnp.concatenate(following[extra : place - extra], axis=0)
    for step in range(STEPS):
        first = extra + step
        count = extent - 2 * step
        inner = pl.ds((first + 1) * ROWS, (count - 2) * ROWS)
        lower = pl.ds(first * ROWS, (count - 2) * ROWS)
        upper = pl.ds((first + 2) * ROWS, (count - 2) * ROWS)
        mid = f[ROWS:-ROWS]
        f = (
            coef[0, inner, :] * mid
            + coef[1, inner, :] * f[2 * ROWS :]
            + coef[2, inner, :] * f[: -2 * ROWS]
            + coef[3, inner, :] * turned(mid, -1)
            + coef[4, inner, :] * turned(mid, 1)
        )
        mid = g[ROWS:-ROWS]
        g = (
            coef[0, inner, :] * mid
            + coef[1, lower, :] * g[: -2 * ROWS]
            + coef[2, upper, :] * g[2 * ROWS :]
            + turned(coef[3, inner, :] * mid, 1)
            + turned(coef[4, inner, :] * mid, -1)
        )

    for copy in far_copies:
        copy.wait_recv()

    smooth = [jnp.zeros((ROWS, LANES), jnp.float32) for _ in range(lons)]
    ring = lons * tiles
    for slot in range(tiles):
        for n in range(lons):
            x = data[slot, (lons + 1 + n) * ROWS : (lons + 2 + n) * ROWS, :]
            for i in range(lons):
                distance = (slot * lons + n - i) % ring
                smooth[i] = smooth[i] + weights[min(distance, ring - distance)] * x

    square = spread * spread
    for i in range(lons):
        here = slice(i * ROWS, (i + 1) * ROWS)
        packed_out[0, here, :] = square * smooth[i] + inc[i] - f[here]
        rest = data[0, (lons + 1 + i) * ROWS : (lons + 2 + i) * ROWS, :]
        packed_out[1, here, :] = rest - g[here]

    for copy in row_copies + near_copies + cross_copies + far_copies:
        copy.wait_send()


def unpack(packed_ref, model_out, dual_out):
    lons, subs, levs, lats = model_out.shape
    high = levs // ROWS
    for i in range(lons):
        for n, out in enumerate((model_out, dual_out)):
            tile = packed_ref[n, i * ROWS : (i + 1) * ROWS, :]
            for s in range(subs):
                for h in range(high):
                    by = (s * high + h) * lats
                    moved = pltpu.roll(tile, LANES - by, 1) if by else tile
                    out[i, s, h * ROWS : (h + 1) * ROWS, :] = moved[:, :lats]


def fills_tiles(tiles, subwins, increment):
    lons, subs, levs, lats = increment.shape
    reach = -(-STEPS // lons)
    return (
        subwins == 2
        and levs % ROWS == 0
        and subs == lons
        and subs * (levs // ROWS) * lats == LANES
        and 2 * reach < tiles <= 2 * ROWS
        and lons * tiles % 4 == 0
        and subs & (subs - 1) == 0
    )


def direct_body(increment, dual_vector, wind_u, wind_v, land_sea, length_sq, spread):
    tiles = lax.axis_size("tiles")
    lons = increment.shape[0]
    reach = -(-STEPS // lons)
    around = 2 * reach + 1
    vmem = pl.BlockSpec(memory_space=pltpu.VMEM)
    hbm = pl.BlockSpec(memory_space=pltpu.HBM)
    args = (increment, dual_vector, wind_u, wind_v, land_sea, length_sq.T, spread)
    result = jax.ShapeDtypeStruct(increment.shape, jnp.float32)
    packed = pl.pallas_call(
        functools.partial(kernel, tiles, reach),
        out_shape=pltpu.VMEM((2, lons * ROWS, LANES), jnp.float32),
        in_specs=[hbm] * len(args),
        out_specs=vmem,
        scratch_shapes=[pltpu.VMEM(x.shape, x.dtype) for x in args]
        + [
            pltpu.VMEM((tiles, (2 * lons + 1) * ROWS, LANES), jnp.float32),
            pltpu.VMEM((tiles, 2, LANES), jnp.float32),
            pltpu.VMEM((ROWS, LANES), jnp.float32),
            pltpu.VMEM((around, ROWS, LANES), jnp.float32),
            pltpu.VMEM((5, around * lons * ROWS, LANES), jnp.float32),
            pltpu.SemaphoreType.DMA((tiles,)),
            pltpu.SemaphoreType.DMA((tiles,)),
            pltpu.SemaphoreType.DMA((tiles,)),
            pltpu.SemaphoreType.DMA((tiles,)),
            pltpu.SemaphoreType.DMA((around,)),
            pltpu.SemaphoreType.DMA((around,)),
            pltpu.SemaphoreType.DMA((len(args),)),
        ],
        compiler_params=pltpu.CompilerParams(collective_id=0, has_side_effects=True),
    )(*args)
    return pl.pallas_call(
        unpack, out_shape=(result, result), in_specs=[vmem], out_specs=(vmem, vmem)
    )(packed)


def body(*args):
    fits = fills_tiles(lax.axis_size("tiles"), lax.axis_size("subwin"), args[0])
    return direct_body(*args) if fits else stepwise_body(*args)


def solution(mesh):
    placed = (
        P(("groups", "tiles"), "subwin", None, None),
        P(("groups", "tiles"), "subwin", None, None),
        P("tiles", None, None),
        P("tiles", None, None),
        P("tiles", None),
        P("subwin", "tiles"),
        P("subwin", None),
    )
    return jax.shard_map(
        body,
        mesh=mesh,
        in_specs=placed,
        out_specs=(
            P(("groups", "tiles"), "subwin", None, None),
            P(("groups", "tiles"), "subwin", None, None),
        ),
        check_vma=False,
    )
```

```python
import functools
import math

import jax
import jax.numpy as jnp
from jax import lax
from jax.experimental import pallas as pl
from jax.experimental.pallas import tpu as pltpu
from jax.sharding import PartitionSpec as P

STEPS = 8
SWEEPS = 4
LON_DEV = 4


def extended(x, sides, width):
    for axis, dim in sides:
        devices, length = (lax.axis_size(axis), x.shape[dim])
        up = [(i, (i + 1) % devices) for i in range(devices)]
        down = [(j, i) for i, j in up]
        last = lax.slice_in_dim(x, length - width, length, axis=dim)
        leading = lax.slice_in_dim(x, 0, width, axis=dim)
        before = lax.ppermute(last, axis, up)
        after = lax.ppermute(leading, axis, down)
        x = jnp.concatenate([before, x, after], axis=dim)
    return x


def passed_along(x, axis, by):
    devices = lax.axis_size(axis)
    pairs = [(i, i + by) for i in range(devices) if 0 <= i + by < devices]
    return lax.ppermute(x, axis, pairs)


def from_north(values):
    return jnp.concatenate([values[..., 1:], jnp.zeros_like(values[..., :1])], axis=-1)


def from_south(values):
    return jnp.concatenate([jnp.zeros_like(values[..., :1]), values[..., :-1]], axis=-1)


def coefficients(wind_u, wind_v, mixing):
    return (
        1.0 - 4.0 * mixing,
        mixing - 0.5 * wind_u,
        mixing + 0.5 * wind_u,
        mixing - 0.5 * wind_v,
        mixing + 0.5 * wind_v,
    )


def tangent_step(fields, coeffs, offset):
    extent = fields.shape[0]
    centre, eastward, westward, northward, southward = [
        coeff[offset + 1 : offset + extent - 1][:, None] for coeff in coeffs
    ]
    middle = fields[1:-1]
    return (
        centre * middle
        + eastward * fields[2:]
        + westward * fields[:-2]
        + northward * from_north(middle)
        + southward * from_south(middle)
    )


def adjoint_step(fields, coeffs, offset):
    extent = fields.shape[0]
    centre = coeffs[0][offset + 1 : offset + extent - 1][:, None]
    northward = coeffs[3][offset + 1 : offset + extent - 1][:, None]
    southward = coeffs[4][offset + 1 : offset + extent - 1][:, None]
    eastward = coeffs[1][offset : offset + extent][:, None]
    westward = coeffs[2][offset : offset + extent][:, None]
    middle = fields[1:-1]
    return (
        centre * middle
        + (eastward * fields)[:-2]
        + (westward * fields)[2:]
        + from_south(northward * middle)
        + from_north(southward * middle)
    )


def run_tangent(fields, coeffs, margin):
    for repeat in range(STEPS // margin):
        grown = extended(fields, (("tiles", 0),), margin)
        for inner_step in range(margin):
            offset = (coeffs[0].shape[0] - grown.shape[0]) // 2
            grown = tangent_step(grown, coeffs, offset)
        fields = grown
    return fields


def run_adjoint(fields, coeffs, margin):
    for repeat in range(STEPS // margin):
        grown = extended(fields, (("tiles", 0),), margin)
        for inner_step in range(margin):
            offset = (coeffs[0].shape[0] - grown.shape[0]) // 2
            grown = adjoint_step(grown, coeffs, offset)
        fields = grown
    return fields


def square_tables(extent):
    index = jnp.arange(extent, dtype=jnp.int32)
    phases = index[:, None] * index[None, :] % extent
    angles = phases.astype(jnp.float32) * (2.0 * math.pi / extent)
    return (jnp.cos(angles), jnp.sin(angles))


def contract(form, first, second):
    return jnp.einsum(form, first, second, precision=lax.Precision.HIGHEST)


def smooth_bands(bands, length_sq):
    count = bands.shape[0]
    inner = LON_DEV
    outer = count // inner
    columns = bands.reshape(outer, inner, -1)
    cos_outer, sin_outer = square_tables(outer)
    cos_inner, sin_inner = square_tables(inner)
    outer_index = jnp.arange(outer, dtype=jnp.int32)
    inner_index = jnp.arange(inner, dtype=jnp.int32)
    twist = (outer_index[:, None] * inner_index[None, :] % count).astype(jnp.float32) * (
        2.0 * math.pi / count
    )
    twist_cos = jnp.cos(twist)[:, :, None]
    twist_sin = jnp.sin(twist)[:, :, None]
    first_real = contract("ab,bqc->aqc", cos_outer, columns)
    first_imag = -contract("ab,bqc->aqc", sin_outer, columns)
    turned_real = first_real * twist_cos + first_imag * twist_sin
    turned_imag = first_imag * twist_cos - first_real * twist_sin
    modes_real = contract("aqc,kq->akc", turned_real, cos_inner) + contract(
        "aqc,kq->akc", turned_imag, sin_inner
    )
    modes_imag = contract("aqc,kq->akc", turned_imag, cos_inner) - contract(
        "aqc,kq->akc", turned_real, sin_inner
    )
    wave = (outer_index[:, None] + outer * inner_index[None, :]).astype(jnp.float32)
    basic = 1.0 - jnp.cos(wave * (2.0 * math.pi / count))
    damping = (1.0 + 2.0 * length_sq[None, None, :, None, :] * basic[:, :, None, None, None]) ** (
        -SWEEPS
    )
    damping = jnp.broadcast_to(damping, (outer, inner) + bands.shape[1:]).reshape(outer, inner, -1)
    modes_real = modes_real * damping
    modes_imag = modes_imag * damping
    back_real = contract("akc,kq->aqc", modes_real, cos_inner) - contract(
        "akc,kq->aqc", modes_imag, sin_inner
    )
    back_imag = contract("akc,kq->aqc", modes_imag, cos_inner) + contract(
        "akc,kq->aqc", modes_real, sin_inner
    )
    final_real = back_real * twist_cos - back_imag * twist_sin
    final_imag = back_imag * twist_cos + back_real * twist_sin
    smoothed = contract("ab,bqc->aqc", cos_outer, final_real) - contract(
        "ab,bqc->aqc", sin_outer, final_imag
    )
    return (smoothed / count).reshape(bands.shape)


def stepwise_body(increment, dual_vector, wind_u, wind_v, land_sea, length_sq, spread):
    margin = 4
    mixing = 0.15 + 0.09 * land_sea.astype(jnp.float32)
    grown_u, grown_v, grown_mix = (
        extended(wind_u, (("tiles", 0),), margin),
        extended(wind_v, (("tiles", 0),), margin),
        extended(mixing, (("tiles", 0),), margin),
    )
    coeffs = coefficients(grown_u, grown_v, grown_mix[:, None, :])
    carried = passed_along(increment[:, -1:], "subwin", 1)
    previous = jnp.concatenate([carried, increment[:, :-1]], axis=1)
    later = passed_along(dual_vector[:, :1], "subwin", -1)
    following = jnp.concatenate([dual_vector[:, 1:], later], axis=1)
    weighted = dual_vector * spread[None, :, :, None]
    bands = lax.all_to_all(weighted, "tiles", split_axis=3, concat_axis=0, tiled=True)
    smoothed = smooth_bands(bands, length_sq)
    forward = run_tangent(previous, coeffs, margin)
    backward = run_adjoint(following, coeffs, margin)
    returned = lax.all_to_all(smoothed, "tiles", split_axis=0, concat_axis=3, tiled=True)
    covar = returned * spread[None, :, :, None]
    return (covar + increment - forward, dual_vector - backward)


ROWS = 8
LANES = 128
MESH = pl.DeviceIdType.MESH


def circulant_row(lengths, count):
    half = count // 2
    damped = []
    for wave in range(half + 1):
        basic = 1.0 - math.cos(2.0 * math.pi * wave / count)
        base = 1.0 + (2.0 * basic) * lengths
        power = base
        for _ in range(SWEEPS - 1):
            power = power * base
        weight = (1.0 if wave in (0, half) else 2.0) / count
        damped.append(weight / power)
    row = [None] * (half + 1)
    for distance in range(half // 2 + 1):
        sums = [jnp.zeros_like(lengths), jnp.zeros_like(lengths)]
        for wave in range(half + 1):
            factor = math.cos(2.0 * math.pi * (wave * distance % count) / count)
            sums[wave % 2] = sums[wave % 2] + factor * damped[wave]
        row[distance] = sums[0] + sums[1]
        row[half - distance] = sums[0] - sums[1]
    return row


def kernel(
    tiles,
    reach,
    *refs,
):
    count = 7
    held, packed_out = refs[:count], refs[count]
    here_refs = refs[count + 1 : 2 * count + 1]
    inc_ref, dual_ref, u_ref, v_ref, land_ref, length_ref, spread_ref = here_refs
    (
    data,
    rows,
    cross,
    other,
    coef,
    send_sem,
    recv_sem,
    row_send,
    row_recv,
    cross_send,
    cross_recv,
    load_sem,
    ) = refs[2 * count + 1 :]
    loads = [
        pltpu.make_async_copy(held[n], here_refs[n], load_sem.at[n]) for n in range(count)
    ]
    for load in loads:
        load.start()
    lons, subs, levs, lats = inc_ref.shape
    high = levs // ROWS
    span = high * lats
    bands = length_ref.shape[0]
    me = lax.axis_index("tiles")
    sub = lax.axis_index("subwin")
    near = [d for d in range(1, reach + 1)] + [tiles - d for d in range(1, reach + 1)]
    far = [d for d in range(1, tiles) if d not in near]
    beside = list(range(-reach, reach + 1))

    def at(distance):
        return lax.rem(me + (distance + tiles), tiles)

    barrier = pltpu.get_barrier_semaphore()
    for d in near + far:
        pl.semaphore_signal(barrier, inc=1, device_id={"tiles": at(d)}, device_id_type=MESH)
    for d in beside:
        pl.semaphore_signal(
            barrier, inc=1, device_id={"tiles": at(d), "subwin": 1 - sub}, device_id_type=MESH
        )

    lane = lax.broadcasted_iota(jnp.int32, (ROWS, LANES), 1)
    group = lane // span
    lat = lane % lats

    def joined(pieces):
        return jnp.concatenate(pieces, axis=1)

    def turned(x, by):
        by = by % LANES
        return x if by == 0 else pltpu.roll(x, by, 1)

    for load in loads:
        load.wait()
    dual = [
        joined([dual_ref[i, s, h * ROWS : (h + 1) * ROWS, :] for s in range(subs) for h in range(high)])
        for i in range(lons)
    ]
    wind_v = joined([v_ref[i, h * ROWS : (h + 1) * ROWS, :] for i in range(lons) for h in range(high)])
    mixing = 0.15 + 0.09 * land_ref[...].astype(jnp.float32)
    mixing = joined([mixing[i : i + 1] for i in range(lons) for h in range(high)])
    lengths = jnp.zeros((ROWS, LANES), jnp.float32)
    for s in range(subs):
        for b in range(bands):
            here = jnp.logical_and(group == s, lat == me * bands + b)
            lengths = jnp.where(here, length_ref[b : b + 1, s : s + 1], lengths)
    rows[0, 0:1, :] = lengths[:1]
    rows[0, 1:2, :] = mixing
    last_inc = joined(
        [inc_ref[i, subs - 1, h * ROWS : (h + 1) * ROWS, :] for i in range(lons) for h in range(high)]
    )
    first_dual = joined(
        [dual_ref[i, 0, h * ROWS : (h + 1) * ROWS, :] for i in range(lons) for h in range(high)]
    )
    inc_u = [
        joined(
            [inc_ref[i, s, h * ROWS : (h + 1) * ROWS, :] for s in range(subs - 1) for h in range(high)]
            + [u_ref[i, h * ROWS : (h + 1) * ROWS, :] for h in range(high)]
        )
        for i in range(lons)
    ]
    own = inc_u + [wind_v] + dual
    for n, tile in enumerate(own):
        data[0, n * ROWS : (n + 1) * ROWS, :] = tile
    cross[...] = jnp.where(sub == 0, last_inc, first_dual)

    pl.semaphore_wait(barrier, len(near) + len(far) + len(beside))

    far_from = (lons + 1) * ROWS
    near_copies, far_copies, cross_copies, row_copies = [], [], [], []
    for d in near + far:
        copy = pltpu.make_async_remote_copy(
            src_ref=rows.at[0],
            dst_ref=rows.at[tiles - d],
            send_sem=row_send.at[d],
            recv_sem=row_recv.at[tiles - d],
            device_id={"tiles": at(d)},
            device_id_type=MESH,
        )
        copy.start()
        row_copies.append(copy)
    for d in near:
        copy = pltpu.make_async_remote_copy(
            src_ref=data.at[0],
            dst_ref=data.at[tiles - d],
            send_sem=send_sem.at[d],
            recv_sem=recv_sem.at[tiles - d],
            device_id={"tiles": at(d)},
            device_id_type=MESH,
        )
        copy.start()
        near_copies.append(copy)
    for d in beside:
        copy = pltpu.make_async_remote_copy(
            src_ref=cross,
            dst_ref=other.at[reach - d],
            send_sem=cross_send.at[reach + d],
            recv_sem=cross_recv.at[reach - d],
            device_id={"tiles": at(d), "subwin": 1 - sub},
            device_id_type=MESH,
        )
        copy.start()
        cross_copies.append(copy)
    for d in far:
        copy = pltpu.make_async_remote_copy(
            src_ref=data.at[0, pl.ds(far_from, lons * ROWS)],
            dst_ref=data.at[tiles - d, pl.ds(far_from, lons * ROWS)],
            send_sem=send_sem.at[d],
            recv_sem=recv_sem.at[tiles - d],
            device_id={"tiles": at(d)},
            device_id_type=MESH,
        )
        copy.start()
        far_copies.append(copy)

    inc = [
        joined([inc_ref[i, s, h * ROWS : (h + 1) * ROWS, :] for s in range(subs) for h in range(high)])
        for i in range(lons)
    ]

    spread = jnp.zeros((ROWS, LANES), jnp.float32)
    eye = lax.broadcasted_iota(jnp.int32, (ROWS, ROWS), 0) == lax.broadcasted_iota(
        jnp.int32, (ROWS, ROWS), 1
    )
    for s in range(subs):
        for h in range(high):
            line = spread_ref[s : s + 1, h * ROWS : (h + 1) * ROWS]
            column = jnp.sum(jnp.where(eye, jnp.broadcast_to(line, (ROWS, ROWS)), 0.0), 1, keepdims=True)
            spread = jnp.where(lane // lats == s * high + h, column, spread)

    for copy in row_copies:
        copy.wait_recv()
    total = jnp.zeros((1, LANES), jnp.float32)
    for slot in range(tiles):
        total = total + rows[slot, 0:1, :]
    weights = circulant_row(jnp.broadcast_to(total, (ROWS, LANES)), lons * tiles)

    for copy in near_copies + cross_copies:
        copy.wait_recv()

    def spread_out(x):
        parts = [turned(x, q * span) for q in range(lons)]
        outs = []
        for i in range(lons):
            out = parts[(0 - i) % lons]
            for g in range(1, subs):
                out = jnp.where(group == g, parts[(g - i) % lons], out)
            outs.append(out)
        return outs

    def to_all(x, g):
        outs = jnp.where(group == g, x, 0.0)
        by = 1
        while by < subs:
            outs = outs + turned(outs, by * span)
            by *= 2
        return outs

    up = jnp.where(sub > 0, 1.0, 0.0)
    down = jnp.where(sub < 1, 1.0, 0.0)
    previous, following = [], []
    place = 0
    for d in beside:
        slot = d % tiles
        vs = spread_out(data[slot, lons * ROWS : (lons + 1) * ROWS, :])
        mixes = spread_out(jnp.broadcast_to(rows[slot, 1:2, :], (ROWS, LANES)))
        beyond = other[d + reach]
        for i in range(lons):
            at_rows = pl.ds(place * ROWS, ROWS)
            f = data[slot, i * ROWS : (i + 1) * ROWS, :]
            m, u, v = mixes[i], 0.5 * to_all(f, subs - 1), 0.5 * vs[i]
            coef[0, at_rows, :] = 1.0 - 4.0 * m
            coef[1, at_rows, :] = m - u
            coef[2, at_rows, :] = m + u
            coef[3, at_rows, :] = jnp.where(lat == lats - 1, 0.0, m - v)
            coef[4, at_rows, :] = jnp.where(lat == 0, 0.0, m + v)
            place += 1
            g = data[slot, (lons + 1 + i) * ROWS : (lons + 2 + i) * ROWS, :]
            previous.append(
                jnp.where(group == 0, up * turned(beyond, -i * span), turned(f, span))
            )
            following.append(
                jnp.where(
                    group == subs - 1, down * turned(beyond, (subs - 1 - i) * span), turned(g, -span)
                )
            )
    extra = reach * lons - STEPS
    extent = place - 2 * extra
    f = jnp.concatenate(previous[extra : place - extra], axis=0)
    g = jnp.concatenate(following[extra : place - extra], axis=0)
    for step in range(STEPS):
        first = extra + step
        count = extent - 2 * step
        inner = pl.ds((first + 1) * ROWS, (count - 2) * ROWS)
        lower = pl.ds(first * ROWS, (count - 2) * ROWS)
        upper = pl.ds((first + 2) * ROWS, (count - 2) * ROWS)
        mid = f[ROWS:-ROWS]
        f = (
            coef[0, inner, :] * mid
            + coef[1, inner, :] * f[2 * ROWS :]
            + coef[2, inner, :] * f[: -2 * ROWS]
            + coef[3, inner, :] * turned(mid, -1)
            + coef[4, inner, :] * turned(mid, 1)
        )
        mid = g[ROWS:-ROWS]
        g = (
            coef[0, inner, :] * mid
            + coef[1, lower, :] * g[: -2 * ROWS]
            + coef[2, upper, :] * g[2 * ROWS :]
            + turned(coef[3, inner, :] * mid, 1)
            + turned(coef[4, inner, :] * mid, -1)
        )

    smooth = [jnp.zeros((ROWS, LANES), jnp.float32) for _ in range(lons)]
    ring = lons * tiles
    for slot in [0] + near + far:
        if slot in far:
            far_copies[far.index(tiles - slot)].wait_recv()
        for n in range(lons):
            x = data[slot, (lons + 1 + n) * ROWS : (lons + 2 + n) * ROWS, :]
            for i in range(lons):
                distance = (slot * lons + n - i) % ring
                smooth[i] = smooth[i] + weights[min(distance, ring - distance)] * x

    square = spread * spread
    for i in range(lons):
        here = slice(i * ROWS, (i + 1) * ROWS)
        packed_out[0, here, :] = square * smooth[i] + inc[i] - f[here]
        rest = data[0, (lons + 1 + i) * ROWS : (lons + 2 + i) * ROWS, :]
        packed_out[1, here, :] = rest - g[here]

    for copy in row_copies + near_copies + cross_copies + far_copies:
        copy.wait_send()


def unpack(packed_ref, model_out, dual_out):
    lons, subs, levs, lats = model_out.shape
    high = levs // ROWS
    for i in range(lons):
        for n, out in enumerate((model_out, dual_out)):
            tile = packed_ref[n, i * ROWS : (i + 1) * ROWS, :]
            for s in range(subs):
                for h in range(high):
                    by = (s * high + h) * lats
                    moved = pltpu.roll(tile, LANES - by, 1) if by else tile
                    out[i, s, h * ROWS : (h + 1) * ROWS, :] = moved[:, :lats]


def fills_tiles(tiles, subwins, increment):
    lons, subs, levs, lats = increment.shape
    reach = -(-STEPS // lons)
    return (
        subwins == 2
        and levs % ROWS == 0
        and subs == lons
        and subs * (levs // ROWS) * lats == LANES
        and 2 * reach < tiles <= 2 * ROWS
        and lons * tiles % 4 == 0
        and subs & (subs - 1) == 0
    )


def direct_body(increment, dual_vector, wind_u, wind_v, land_sea, length_sq, spread):
    tiles = lax.axis_size("tiles")
    lons = increment.shape[0]
    reach = -(-STEPS // lons)
    around = 2 * reach + 1
    vmem = pl.BlockSpec(memory_space=pltpu.VMEM)
    hbm = pl.BlockSpec(memory_space=pltpu.HBM)
    args = (increment, dual_vector, wind_u, wind_v, land_sea, length_sq.T, spread)
    result = jax.ShapeDtypeStruct(increment.shape, jnp.float32)
    packed = pl.pallas_call(
        functools.partial(kernel, tiles, reach),
        out_shape=pltpu.VMEM((2, lons * ROWS, LANES), jnp.float32),
        in_specs=[hbm] * len(args),
        out_specs=vmem,
        scratch_shapes=[pltpu.VMEM(x.shape, x.dtype) for x in args]
        + [
            pltpu.VMEM((tiles, (2 * lons + 1) * ROWS, LANES), jnp.float32),
            pltpu.VMEM((tiles, 2, LANES), jnp.float32),
            pltpu.VMEM((ROWS, LANES), jnp.float32),
            pltpu.VMEM((around, ROWS, LANES), jnp.float32),
            pltpu.VMEM((5, around * lons * ROWS, LANES), jnp.float32),
            pltpu.SemaphoreType.DMA((tiles,)),
            pltpu.SemaphoreType.DMA((tiles,)),
            pltpu.SemaphoreType.DMA((tiles,)),
            pltpu.SemaphoreType.DMA((tiles,)),
            pltpu.SemaphoreType.DMA((around,)),
            pltpu.SemaphoreType.DMA((around,)),
            pltpu.SemaphoreType.DMA((len(args),)),
        ],
        compiler_params=pltpu.CompilerParams(collective_id=0, has_side_effects=True),
    )(*args)
    return pl.pallas_call(
        unpack,
        out_shape=(result, result),
        in_specs=[vmem],
        out_specs=(vmem, vmem),
        compiler_params=pltpu.CompilerParams(vmem_limit_bytes=2 * 2**20),
    )(packed)


def body(*args):
    fits = fills_tiles(lax.axis_size("tiles"), lax.axis_size("subwin"), args[0])
    return direct_body(*args) if fits else stepwise_body(*args)


def solution(mesh):
    placed = (
        P(("groups", "tiles"), "subwin", None, None),
        P(("groups", "tiles"), "subwin", None, None),
        P("tiles", None, None),
        P("tiles", None, None),
        P("tiles", None),
        P("subwin", "tiles"),
        P("subwin", None),
    )
    return jax.shard_map(
        body,
        mesh=mesh,
        in_specs=placed,
        out_specs=(
            P(("groups", "tiles"), "subwin", None, None),
            P(("groups", "tiles"), "subwin", None, None),
        ),
        check_vma=False,
    )
```

```python
import functools
import math

import jax
import jax.numpy as jnp
from jax import lax
from jax.experimental import pallas as pl
from jax.experimental.pallas import tpu as pltpu
from jax.sharding import PartitionSpec as P

STEPS = 8
SWEEPS = 4
LON_DEV = 4


def extended(x, sides, width):
    for axis, dim in sides:
        devices, length = (lax.axis_size(axis), x.shape[dim])
        up = [(i, (i + 1) % devices) for i in range(devices)]
        down = [(j, i) for i, j in up]
        last = lax.slice_in_dim(x, length - width, length, axis=dim)
        leading = lax.slice_in_dim(x, 0, width, axis=dim)
        before = lax.ppermute(last, axis, up)
        after = lax.ppermute(leading, axis, down)
        x = jnp.concatenate([before, x, after], axis=dim)
    return x


def passed_along(x, axis, by):
    devices = lax.axis_size(axis)
    pairs = [(i, i + by) for i in range(devices) if 0 <= i + by < devices]
    return lax.ppermute(x, axis, pairs)


def from_north(values):
    return jnp.concatenate([values[..., 1:], jnp.zeros_like(values[..., :1])], axis=-1)


def from_south(values):
    return jnp.concatenate([jnp.zeros_like(values[..., :1]), values[..., :-1]], axis=-1)


def coefficients(wind_u, wind_v, mixing):
    return (
        1.0 - 4.0 * mixing,
        mixing - 0.5 * wind_u,
        mixing + 0.5 * wind_u,
        mixing - 0.5 * wind_v,
        mixing + 0.5 * wind_v,
    )


def tangent_step(fields, coeffs, offset):
    extent = fields.shape[0]
    centre, eastward, westward, northward, southward = [
        coeff[offset + 1 : offset + extent - 1][:, None] for coeff in coeffs
    ]
    middle = fields[1:-1]
    return (
        centre * middle
        + eastward * fields[2:]
        + westward * fields[:-2]
        + northward * from_north(middle)
        + southward * from_south(middle)
    )


def adjoint_step(fields, coeffs, offset):
    extent = fields.shape[0]
    centre = coeffs[0][offset + 1 : offset + extent - 1][:, None]
    northward = coeffs[3][offset + 1 : offset + extent - 1][:, None]
    southward = coeffs[4][offset + 1 : offset + extent - 1][:, None]
    eastward = coeffs[1][offset : offset + extent][:, None]
    westward = coeffs[2][offset : offset + extent][:, None]
    middle = fields[1:-1]
    return (
        centre * middle
        + (eastward * fields)[:-2]
        + (westward * fields)[2:]
        + from_south(northward * middle)
        + from_north(southward * middle)
    )


def run_tangent(fields, coeffs, margin):
    for repeat in range(STEPS // margin):
        grown = extended(fields, (("tiles", 0),), margin)
        for inner_step in range(margin):
            offset = (coeffs[0].shape[0] - grown.shape[0]) // 2
            grown = tangent_step(grown, coeffs, offset)
        fields = grown
    return fields


def run_adjoint(fields, coeffs, margin):
    for repeat in range(STEPS // margin):
        grown = extended(fields, (("tiles", 0),), margin)
        for inner_step in range(margin):
            offset = (coeffs[0].shape[0] - grown.shape[0]) // 2
            grown = adjoint_step(grown, coeffs, offset)
        fields = grown
    return fields


def square_tables(extent):
    index = jnp.arange(extent, dtype=jnp.int32)
    phases = index[:, None] * index[None, :] % extent
    angles = phases.astype(jnp.float32) * (2.0 * math.pi / extent)
    return (jnp.cos(angles), jnp.sin(angles))


def contract(form, first, second):
    return jnp.einsum(form, first, second, precision=lax.Precision.HIGHEST)


def smooth_bands(bands, length_sq):
    count = bands.shape[0]
    inner = LON_DEV
    outer = count // inner
    columns = bands.reshape(outer, inner, -1)
    cos_outer, sin_outer = square_tables(outer)
    cos_inner, sin_inner = square_tables(inner)
    outer_index = jnp.arange(outer, dtype=jnp.int32)
    inner_index = jnp.arange(inner, dtype=jnp.int32)
    twist = (outer_index[:, None] * inner_index[None, :] % count).astype(jnp.float32) * (
        2.0 * math.pi / count
    )
    twist_cos = jnp.cos(twist)[:, :, None]
    twist_sin = jnp.sin(twist)[:, :, None]
    first_real = contract("ab,bqc->aqc", cos_outer, columns)
    first_imag = -contract("ab,bqc->aqc", sin_outer, columns)
    turned_real = first_real * twist_cos + first_imag * twist_sin
    turned_imag = first_imag * twist_cos - first_real * twist_sin
    modes_real = contract("aqc,kq->akc", turned_real, cos_inner) + contract(
        "aqc,kq->akc", turned_imag, sin_inner
    )
    modes_imag = contract("aqc,kq->akc", turned_imag, cos_inner) - contract(
        "aqc,kq->akc", turned_real, sin_inner
    )
    wave = (outer_index[:, None] + outer * inner_index[None, :]).astype(jnp.float32)
    basic = 1.0 - jnp.cos(wave * (2.0 * math.pi / count))
    damping = (1.0 + 2.0 * length_sq[None, None, :, None, :] * basic[:, :, None, None, None]) ** (
        -SWEEPS
    )
    damping = jnp.broadcast_to(damping, (outer, inner) + bands.shape[1:]).reshape(outer, inner, -1)
    modes_real = modes_real * damping
    modes_imag = modes_imag * damping
    back_real = contract("akc,kq->aqc", modes_real, cos_inner) - contract(
        "akc,kq->aqc", modes_imag, sin_inner
    )
    back_imag = contract("akc,kq->aqc", modes_imag, cos_inner) + contract(
        "akc,kq->aqc", modes_real, sin_inner
    )
    final_real = back_real * twist_cos - back_imag * twist_sin
    final_imag = back_imag * twist_cos + back_real * twist_sin
    smoothed = contract("ab,bqc->aqc", cos_outer, final_real) - contract(
        "ab,bqc->aqc", sin_outer, final_imag
    )
    return (smoothed / count).reshape(bands.shape)


def stepwise_body(increment, dual_vector, wind_u, wind_v, land_sea, length_sq, spread):
    margin = 4
    mixing = 0.15 + 0.09 * land_sea.astype(jnp.float32)
    grown_u, grown_v, grown_mix = (
        extended(wind_u, (("tiles", 0),), margin),
        extended(wind_v, (("tiles", 0),), margin),
        extended(mixing, (("tiles", 0),), margin),
    )
    coeffs = coefficients(grown_u, grown_v, grown_mix[:, None, :])
    carried = passed_along(increment[:, -1:], "subwin", 1)
    previous = jnp.concatenate([carried, increment[:, :-1]], axis=1)
    later = passed_along(dual_vector[:, :1], "subwin", -1)
    following = jnp.concatenate([dual_vector[:, 1:], later], axis=1)
    weighted = dual_vector * spread[None, :, :, None]
    bands = lax.all_to_all(weighted, "tiles", split_axis=3, concat_axis=0, tiled=True)
    smoothed = smooth_bands(bands, length_sq)
    forward = run_tangent(previous, coeffs, margin)
    backward = run_adjoint(following, coeffs, margin)
    returned = lax.all_to_all(smoothed, "tiles", split_axis=0, concat_axis=3, tiled=True)
    covar = returned * spread[None, :, :, None]
    return (covar + increment - forward, dual_vector - backward)


ROWS = 8
LANES = 128
MESH = pl.DeviceIdType.MESH


def circulant_row(lengths, count):
    half = count // 2
    damped = []
    for wave in range(half + 1):
        basic = 1.0 - math.cos(2.0 * math.pi * wave / count)
        base = 1.0 + (2.0 * basic) * lengths
        power = base
        for _ in range(SWEEPS - 1):
            power = power * base
        weight = (1.0 if wave in (0, half) else 2.0) / count
        damped.append(weight / power)
    row = [None] * (half + 1)
    for distance in range(half // 2 + 1):
        sums = [jnp.zeros_like(lengths), jnp.zeros_like(lengths)]
        for wave in range(half + 1):
            factor = math.cos(2.0 * math.pi * (wave * distance % count) / count)
            sums[wave % 2] = sums[wave % 2] + factor * damped[wave]
        row[distance] = sums[0] + sums[1]
        row[half - distance] = sums[0] - sums[1]
    return row


def kernel(
    tiles,
    reach,
    *refs,
):
    count = 7
    held, packed_out = refs[:count], refs[count]
    here_refs = refs[count + 1 : 2 * count + 1]
    inc_ref, dual_ref, u_ref, v_ref, land_ref, length_ref, spread_ref = here_refs
    (
    data,
    rows,
    cross,
    other,
    coef,
    send_sem,
    recv_sem,
    row_send,
    row_recv,
    cross_send,
    cross_recv,
    load_sem,
    ) = refs[2 * count + 1 :]
    loads = [
        pltpu.make_async_copy(held[n], here_refs[n], load_sem.at[n]) for n in range(count)
    ]
    for load in loads:
        load.start()
    lons, subs, levs, lats = inc_ref.shape
    high = levs // ROWS
    span = high * lats
    bands = length_ref.shape[0]
    me = lax.axis_index("tiles")
    sub = lax.axis_index("subwin")
    near = [d for d in range(1, reach + 1)] + [tiles - d for d in range(1, reach + 1)]
    far = [d for d in range(1, tiles) if d not in near]
    beside = list(range(-reach, reach + 1))

    def at(distance):
        return lax.rem(me + (distance + tiles), tiles)

    barrier = pltpu.get_barrier_semaphore()
    for d in near + far:
        pl.semaphore_signal(barrier, inc=1, device_id={"tiles": at(d)}, device_id_type=MESH)
    for d in beside:
        pl.semaphore_signal(
            barrier, inc=1, device_id={"tiles": at(d), "subwin": 1 - sub}, device_id_type=MESH
        )

    lane = lax.broadcasted_iota(jnp.int32, (ROWS, LANES), 1)
    group = lane // span
    lat = lane % lats

    def joined(pieces):
        return jnp.concatenate(pieces, axis=1)

    def turned(x, by):
        by = by % LANES
        return x if by == 0 else pltpu.roll(x, by, 1)

    for load in loads:
        load.wait()
    dual = [
        joined([dual_ref[i, s, h * ROWS : (h + 1) * ROWS, :] for s in range(subs) for h in range(high)])
        for i in range(lons)
    ]
    wind_v = joined([v_ref[i, h * ROWS : (h + 1) * ROWS, :] for i in range(lons) for h in range(high)])
    mixing = 0.15 + 0.09 * land_ref[...].astype(jnp.float32)
    mixing = joined([mixing[i : i + 1] for i in range(lons) for h in range(high)])
    lengths = jnp.zeros((ROWS, LANES), jnp.float32)
    for s in range(subs):
        for b in range(bands):
            here = jnp.logical_and(group == s, lat == me * bands + b)
            lengths = jnp.where(here, length_ref[b : b + 1, s : s + 1], lengths)
    rows[0, 0:1, :] = lengths[:1]
    rows[0, 1:2, :] = mixing
    last_inc = joined(
        [inc_ref[i, subs - 1, h * ROWS : (h + 1) * ROWS, :] for i in range(lons) for h in range(high)]
    )
    first_dual = joined(
        [dual_ref[i, 0, h * ROWS : (h + 1) * ROWS, :] for i in range(lons) for h in range(high)]
    )
    inc_u = [
        joined(
            [inc_ref[i, s, h * ROWS : (h + 1) * ROWS, :] for s in range(subs - 1) for h in range(high)]
            + [u_ref[i, h * ROWS : (h + 1) * ROWS, :] for h in range(high)]
        )
        for i in range(lons)
    ]
    own = inc_u + [wind_v] + dual
    for n, tile in enumerate(own):
        data[0, n * ROWS : (n + 1) * ROWS, :] = tile
    cross[...] = jnp.where(sub == 0, last_inc, first_dual)

    pl.semaphore_wait(barrier, len(near) + len(far) + len(beside))

    far_from = (lons + 1) * ROWS
    far_copies, cross_copies, row_copies = [], [], []
    for d in near + far:
        copy = pltpu.make_async_remote_copy(
            src_ref=rows.at[0],
            dst_ref=rows.at[tiles - d],
            send_sem=row_send.at[d],
            recv_sem=row_recv.at[tiles - d],
            device_id={"tiles": at(d)},
            device_id_type=MESH,
        )
        copy.start()
        row_copies.append(copy)
    for d in beside:
        copy = pltpu.make_async_remote_copy(
            src_ref=cross,
            dst_ref=other.at[reach - d],
            send_sem=cross_send.at[reach + d],
            recv_sem=cross_recv.at[reach - d],
            device_id={"tiles": at(d), "subwin": 1 - sub},
            device_id_type=MESH,
        )
        copy.start()
        cross_copies.append(copy)
    outward = jnp.where(2 * me < tiles, -1, 1)

    def near_copy(d):
        slot = lax.rem(tiles - d, tiles)
        return pltpu.make_async_remote_copy(
            src_ref=data.at[0],
            dst_ref=data.at[slot],
            send_sem=send_sem.at[lax.rem(d + tiles, tiles)],
            recv_sem=recv_sem.at[slot],
            device_id={"tiles": at(d)},
            device_id_type=MESH,
        )

    for side in (outward, -outward):
        for d in range(reach, 0, -1):
            near_copy(side * d).start()
    near_copies = [near_copy(d) for d in near]
    for d in far:
        copy = pltpu.make_async_remote_copy(
            src_ref=data.at[0, pl.ds(far_from, lons * ROWS)],
            dst_ref=data.at[tiles - d, pl.ds(far_from, lons * ROWS)],
            send_sem=send_sem.at[d],
            recv_sem=recv_sem.at[tiles - d],
            device_id={"tiles": at(d)},
            device_id_type=MESH,
        )
        copy.start()
        far_copies.append(copy)

    inc = [
        joined([inc_ref[i, s, h * ROWS : (h + 1) * ROWS, :] for s in range(subs) for h in range(high)])
        for i in range(lons)
    ]

    spread = jnp.zeros((ROWS, LANES), jnp.float32)
    eye = lax.broadcasted_iota(jnp.int32, (ROWS, ROWS), 0) == lax.broadcasted_iota(
        jnp.int32, (ROWS, ROWS), 1
    )
    for s in range(subs):
        for h in range(high):
            line = spread_ref[s : s + 1, h * ROWS : (h + 1) * ROWS]
            column = jnp.sum(jnp.where(eye, jnp.broadcast_to(line, (ROWS, ROWS)), 0.0), 1, keepdims=True)
            spread = jnp.where(lane // lats == s * high + h, column, spread)

    for copy in row_copies:
        copy.wait_recv()
    total = jnp.zeros((1, LANES), jnp.float32)
    for slot in range(tiles):
        total = total + rows[slot, 0:1, :]
    weights = circulant_row(jnp.broadcast_to(total, (ROWS, LANES)), lons * tiles)

    for copy in near_copies + cross_copies:
        copy.wait_recv()

    def spread_out(x):
        parts = [turned(x, q * span) for q in range(lons)]
        outs = []
        for i in range(lons):
            out = parts[(0 - i) % lons]
            for g in range(1, subs):
                out = jnp.where(group == g, parts[(g - i) % lons], out)
            outs.append(out)
        return outs

    def to_all(x, g):
        outs = jnp.where(group == g, x, 0.0)
        by = 1
        while by < subs:
            outs = outs + turned(outs, by * span)
            by *= 2
        return outs

    up = jnp.where(sub > 0, 1.0, 0.0)
    down = jnp.where(sub < 1, 1.0, 0.0)
    previous, following = [], []
    place = 0
    for d in beside:
        slot = d % tiles
        vs = spread_out(data[slot, lons * ROWS : (lons + 1) * ROWS, :])
        mixes = spread_out(jnp.broadcast_to(rows[slot, 1:2, :], (ROWS, LANES)))
        beyond = other[d + reach]
        for i in range(lons):
            at_rows = pl.ds(place * ROWS, ROWS)
            f = data[slot, i * ROWS : (i + 1) * ROWS, :]
            m, u, v = mixes[i], 0.5 * to_all(f, subs - 1), 0.5 * vs[i]
            coef[0, at_rows, :] = 1.0 - 4.0 * m
            coef[1, at_rows, :] = m - u
            coef[2, at_rows, :] = m + u
            coef[3, at_rows, :] = jnp.where(lat == lats - 1, 0.0, m - v)
            coef[4, at_rows, :] = jnp.where(lat == 0, 0.0, m + v)
            place += 1
            g = data[slot, (lons + 1 + i) * ROWS : (lons + 2 + i) * ROWS, :]
            previous.append(
                jnp.where(group == 0, up * turned(beyond, -i * span), turned(f, span))
            )
            following.append(
                jnp.where(
                    group == subs - 1, down * turned(beyond, (subs - 1 - i) * span), turned(g, -span)
                )
            )
    extra = reach * lons - STEPS
    extent = place - 2 * extra
    f = jnp.concatenate(previous[extra : place - extra], axis=0)
    g = jnp.concatenate(following[extra : place - extra], axis=0)
    for step in range(STEPS):
        first = extra + step
        count = extent - 2 * step
        inner = pl.ds((first + 1) * ROWS, (count - 2) * ROWS)
        lower = pl.ds(first * ROWS, (count - 2) * ROWS)
        upper = pl.ds((first + 2) * ROWS, (count - 2) * ROWS)
        mid = f[ROWS:-ROWS]
        f = (
            coef[0, inner, :] * mid
            + coef[1, inner, :] * f[2 * ROWS :]
            + coef[2, inner, :] * f[: -2 * ROWS]
            + coef[3, inner, :] * turned(mid, -1)
            + coef[4, inner, :] * turned(mid, 1)
        )
        mid = g[ROWS:-ROWS]
        g = (
            coef[0, inner, :] * mid
            + coef[1, lower, :] * g[: -2 * ROWS]
            + coef[2, upper, :] * g[2 * ROWS :]
            + turned(coef[3, inner, :] * mid, 1)
            + turned(coef[4, inner, :] * mid, -1)
        )

    smooth = [jnp.zeros((ROWS, LANES), jnp.float32) for _ in range(lons)]
    ring = lons * tiles
    for slot in [0] + near + far:
        if slot in far:
            far_copies[far.index(tiles - slot)].wait_recv()
        for n in range(lons):
            x = data[slot, (lons + 1 + n) * ROWS : (lons + 2 + n) * ROWS, :]
            for i in range(lons):
                distance = (slot * lons + n - i) % ring
                smooth[i] = smooth[i] + weights[min(distance, ring - distance)] * x

    square = spread * spread
    for i in range(lons):
        here = slice(i * ROWS, (i + 1) * ROWS)
        packed_out[0, here, :] = square * smooth[i] + inc[i] - f[here]
        rest = data[0, (lons + 1 + i) * ROWS : (lons + 2 + i) * ROWS, :]
        packed_out[1, here, :] = rest - g[here]

    for copy in row_copies + near_copies + cross_copies + far_copies:
        copy.wait_send()


def unpack(packed_ref, model_out, dual_out):
    lons, subs, levs, lats = model_out.shape
    high = levs // ROWS
    for i in range(lons):
        for n, out in enumerate((model_out, dual_out)):
            tile = packed_ref[n, i * ROWS : (i + 1) * ROWS, :]
            for s in range(subs):
                for h in range(high):
                    by = (s * high + h) * lats
                    moved = pltpu.roll(tile, LANES - by, 1) if by else tile
                    out[i, s, h * ROWS : (h + 1) * ROWS, :] = moved[:, :lats]


def fills_tiles(tiles, subwins, increment):
    lons, subs, levs, lats = increment.shape
    reach = -(-STEPS // lons)
    return (
        subwins == 2
        and levs % ROWS == 0
        and subs == lons
        and subs * (levs // ROWS) * lats == LANES
        and 2 * reach < tiles <= 2 * ROWS
        and lons * tiles % 4 == 0
        and subs & (subs - 1) == 0
    )


def direct_body(increment, dual_vector, wind_u, wind_v, land_sea, length_sq, spread):
    tiles = lax.axis_size("tiles")
    lons = increment.shape[0]
    reach = -(-STEPS // lons)
    around = 2 * reach + 1
    vmem = pl.BlockSpec(memory_space=pltpu.VMEM)
    hbm = pl.BlockSpec(memory_space=pltpu.HBM)
    args = (increment, dual_vector, wind_u, wind_v, land_sea, length_sq.T, spread)
    result = jax.ShapeDtypeStruct(increment.shape, jnp.float32)
    packed = pl.pallas_call(
        functools.partial(kernel, tiles, reach),
        out_shape=pltpu.VMEM((2, lons * ROWS, LANES), jnp.float32),
        in_specs=[hbm] * len(args),
        out_specs=vmem,
        scratch_shapes=[pltpu.VMEM(x.shape, x.dtype) for x in args]
        + [
            pltpu.VMEM((tiles, (2 * lons + 1) * ROWS, LANES), jnp.float32),
            pltpu.VMEM((tiles, 2, LANES), jnp.float32),
            pltpu.VMEM((ROWS, LANES), jnp.float32),
            pltpu.VMEM((around, ROWS, LANES), jnp.float32),
            pltpu.VMEM((5, around * lons * ROWS, LANES), jnp.float32),
            pltpu.SemaphoreType.DMA((tiles,)),
            pltpu.SemaphoreType.DMA((tiles,)),
            pltpu.SemaphoreType.DMA((tiles,)),
            pltpu.SemaphoreType.DMA((tiles,)),
            pltpu.SemaphoreType.DMA((around,)),
            pltpu.SemaphoreType.DMA((around,)),
            pltpu.SemaphoreType.DMA((len(args),)),
        ],
        compiler_params=pltpu.CompilerParams(collective_id=0, has_side_effects=True),
    )(*args)
    return pl.pallas_call(
        unpack,
        out_shape=(result, result),
        in_specs=[vmem],
        out_specs=(vmem, vmem),
        compiler_params=pltpu.CompilerParams(vmem_limit_bytes=2 * 2**20),
    )(packed)


def body(*args):
    fits = fills_tiles(lax.axis_size("tiles"), lax.axis_size("subwin"), args[0])
    return direct_body(*args) if fits else stepwise_body(*args)


def solution(mesh):
    placed = (
        P(("groups", "tiles"), "subwin", None, None),
        P(("groups", "tiles"), "subwin", None, None),
        P("tiles", None, None),
        P("tiles", None, None),
        P("tiles", None),
        P("subwin", "tiles"),
        P("subwin", None),
    )
    return jax.shard_map(
        body,
        mesh=mesh,
        in_specs=placed,
        out_specs=(
            P(("groups", "tiles"), "subwin", None, None),
            P(("groups", "tiles"), "subwin", None, None),
        ),
        check_vma=False,
    )
```

```python
import functools
import math

import jax
import jax.numpy as jnp
from jax import lax
from jax.experimental import pallas as pl
from jax.experimental.pallas import tpu as pltpu
from jax.sharding import PartitionSpec as P

STEPS = 8
SWEEPS = 4
LON_DEV = 4


def extended(x, sides, width):
    for axis, dim in sides:
        devices, length = (lax.axis_size(axis), x.shape[dim])
        up = [(i, (i + 1) % devices) for i in range(devices)]
        down = [(j, i) for i, j in up]
        last = lax.slice_in_dim(x, length - width, length, axis=dim)
        leading = lax.slice_in_dim(x, 0, width, axis=dim)
        before = lax.ppermute(last, axis, up)
        after = lax.ppermute(leading, axis, down)
        x = jnp.concatenate([before, x, after], axis=dim)
    return x


def passed_along(x, axis, by):
    devices = lax.axis_size(axis)
    pairs = [(i, i + by) for i in range(devices) if 0 <= i + by < devices]
    return lax.ppermute(x, axis, pairs)


def from_north(values):
    return jnp.concatenate([values[..., 1:], jnp.zeros_like(values[..., :1])], axis=-1)


def from_south(values):
    return jnp.concatenate([jnp.zeros_like(values[..., :1]), values[..., :-1]], axis=-1)


def coefficients(wind_u, wind_v, mixing):
    return (
        1.0 - 4.0 * mixing,
        mixing - 0.5 * wind_u,
        mixing + 0.5 * wind_u,
        mixing - 0.5 * wind_v,
        mixing + 0.5 * wind_v,
    )


def tangent_step(fields, coeffs, offset):
    extent = fields.shape[0]
    centre, eastward, westward, northward, southward = [
        coeff[offset + 1 : offset + extent - 1][:, None] for coeff in coeffs
    ]
    middle = fields[1:-1]
    return (
        centre * middle
        + eastward * fields[2:]
        + westward * fields[:-2]
        + northward * from_north(middle)
        + southward * from_south(middle)
    )


def adjoint_step(fields, coeffs, offset):
    extent = fields.shape[0]
    centre = coeffs[0][offset + 1 : offset + extent - 1][:, None]
    northward = coeffs[3][offset + 1 : offset + extent - 1][:, None]
    southward = coeffs[4][offset + 1 : offset + extent - 1][:, None]
    eastward = coeffs[1][offset : offset + extent][:, None]
    westward = coeffs[2][offset : offset + extent][:, None]
    middle = fields[1:-1]
    return (
        centre * middle
        + (eastward * fields)[:-2]
        + (westward * fields)[2:]
        + from_south(northward * middle)
        + from_north(southward * middle)
    )


def run_tangent(fields, coeffs, margin):
    for repeat in range(STEPS // margin):
        grown = extended(fields, (("tiles", 0),), margin)
        for inner_step in range(margin):
            offset = (coeffs[0].shape[0] - grown.shape[0]) // 2
            grown = tangent_step(grown, coeffs, offset)
        fields = grown
    return fields


def run_adjoint(fields, coeffs, margin):
    for repeat in range(STEPS // margin):
        grown = extended(fields, (("tiles", 0),), margin)
        for inner_step in range(margin):
            offset = (coeffs[0].shape[0] - grown.shape[0]) // 2
            grown = adjoint_step(grown, coeffs, offset)
        fields = grown
    return fields


def square_tables(extent):
    index = jnp.arange(extent, dtype=jnp.int32)
    phases = index[:, None] * index[None, :] % extent
    angles = phases.astype(jnp.float32) * (2.0 * math.pi / extent)
    return (jnp.cos(angles), jnp.sin(angles))


def contract(form, first, second):
    return jnp.einsum(form, first, second, precision=lax.Precision.HIGHEST)


def smooth_bands(bands, length_sq):
    count = bands.shape[0]
    inner = LON_DEV
    outer = count // inner
    columns = bands.reshape(outer, inner, -1)
    cos_outer, sin_outer = square_tables(outer)
    cos_inner, sin_inner = square_tables(inner)
    outer_index = jnp.arange(outer, dtype=jnp.int32)
    inner_index = jnp.arange(inner, dtype=jnp.int32)
    twist = (outer_index[:, None] * inner_index[None, :] % count).astype(jnp.float32) * (
        2.0 * math.pi / count
    )
    twist_cos = jnp.cos(twist)[:, :, None]
    twist_sin = jnp.sin(twist)[:, :, None]
    first_real = contract("ab,bqc->aqc", cos_outer, columns)
    first_imag = -contract("ab,bqc->aqc", sin_outer, columns)
    turned_real = first_real * twist_cos + first_imag * twist_sin
    turned_imag = first_imag * twist_cos - first_real * twist_sin
    modes_real = contract("aqc,kq->akc", turned_real, cos_inner) + contract(
        "aqc,kq->akc", turned_imag, sin_inner
    )
    modes_imag = contract("aqc,kq->akc", turned_imag, cos_inner) - contract(
        "aqc,kq->akc", turned_real, sin_inner
    )
    wave = (outer_index[:, None] + outer * inner_index[None, :]).astype(jnp.float32)
    basic = 1.0 - jnp.cos(wave * (2.0 * math.pi / count))
    damping = (1.0 + 2.0 * length_sq[None, None, :, None, :] * basic[:, :, None, None, None]) ** (
        -SWEEPS
    )
    damping = jnp.broadcast_to(damping, (outer, inner) + bands.shape[1:]).reshape(outer, inner, -1)
    modes_real = modes_real * damping
    modes_imag = modes_imag * damping
    back_real = contract("akc,kq->aqc", modes_real, cos_inner) - contract(
        "akc,kq->aqc", modes_imag, sin_inner
    )
    back_imag = contract("akc,kq->aqc", modes_imag, cos_inner) + contract(
        "akc,kq->aqc", modes_real, sin_inner
    )
    final_real = back_real * twist_cos - back_imag * twist_sin
    final_imag = back_imag * twist_cos + back_real * twist_sin
    smoothed = contract("ab,bqc->aqc", cos_outer, final_real) - contract(
        "ab,bqc->aqc", sin_outer, final_imag
    )
    return (smoothed / count).reshape(bands.shape)


def stepwise_body(increment, dual_vector, wind_u, wind_v, land_sea, length_sq, spread):
    margin = 4
    mixing = 0.15 + 0.09 * land_sea.astype(jnp.float32)
    grown_u, grown_v, grown_mix = (
        extended(wind_u, (("tiles", 0),), margin),
        extended(wind_v, (("tiles", 0),), margin),
        extended(mixing, (("tiles", 0),), margin),
    )
    coeffs = coefficients(grown_u, grown_v, grown_mix[:, None, :])
    carried = passed_along(increment[:, -1:], "subwin", 1)
    previous = jnp.concatenate([carried, increment[:, :-1]], axis=1)
    later = passed_along(dual_vector[:, :1], "subwin", -1)
    following = jnp.concatenate([dual_vector[:, 1:], later], axis=1)
    weighted = dual_vector * spread[None, :, :, None]
    bands = lax.all_to_all(weighted, "tiles", split_axis=3, concat_axis=0, tiled=True)
    smoothed = smooth_bands(bands, length_sq)
    forward = run_tangent(previous, coeffs, margin)
    backward = run_adjoint(following, coeffs, margin)
    returned = lax.all_to_all(smoothed, "tiles", split_axis=0, concat_axis=3, tiled=True)
    covar = returned * spread[None, :, :, None]
    return (covar + increment - forward, dual_vector - backward)


ROWS = 8
LANES = 128
MESH = pl.DeviceIdType.MESH


def circulant_row(lengths, count):
    half = count // 2
    damped = []
    for wave in range(half + 1):
        basic = 1.0 - math.cos(2.0 * math.pi * wave / count)
        base = 1.0 + (2.0 * basic) * lengths
        power = base
        for _ in range(SWEEPS - 1):
            power = power * base
        weight = (1.0 if wave in (0, half) else 2.0) / count
        damped.append(weight / power)
    row = [None] * (half + 1)
    for distance in range(half // 2 + 1):
        sums = [jnp.zeros_like(lengths), jnp.zeros_like(lengths)]
        for wave in range(half + 1):
            factor = math.cos(2.0 * math.pi * (wave * distance % count) / count)
            sums[wave % 2] = sums[wave % 2] + factor * damped[wave]
        row[distance] = sums[0] + sums[1]
        row[half - distance] = sums[0] - sums[1]
    return row


def kernel(
    tiles,
    reach,
    *refs,
):
    count = 7
    held, packed_out = refs[:count], refs[count]
    here_refs = refs[count + 1 : 2 * count + 1]
    inc_ref, dual_ref, u_ref, v_ref, land_ref, length_ref, spread_ref = here_refs
    (
    data,
    rows,
    cross,
    other,
    coef,
    send_sem,
    recv_sem,
    row_send,
    row_recv,
    cross_send,
    cross_recv,
    load_sem,
    ) = refs[2 * count + 1 :]
    loads = [
        pltpu.make_async_copy(held[n], here_refs[n], load_sem.at[n]) for n in range(count)
    ]
    for load in loads:
        load.start()
    lons, subs, levs, lats = inc_ref.shape
    high = levs // ROWS
    span = high * lats
    bands = length_ref.shape[0]
    me = lax.axis_index("tiles")
    sub = lax.axis_index("subwin")
    near = [d for d in range(1, reach + 1)] + [tiles - d for d in range(1, reach + 1)]
    far = [d for d in range(1, tiles) if d not in near]
    beside = list(range(-reach, reach + 1))

    def at(distance):
        return lax.rem(me + (distance + tiles), tiles)

    barrier = pltpu.get_barrier_semaphore()
    for d in near + far:
        pl.semaphore_signal(barrier, inc=1, device_id={"tiles": at(d)}, device_id_type=MESH)
    for d in beside:
        pl.semaphore_signal(
            barrier, inc=1, device_id={"tiles": at(d), "subwin": 1 - sub}, device_id_type=MESH
        )

    lane = lax.broadcasted_iota(jnp.int32, (ROWS, LANES), 1)
    group = lane // span
    lat = lane % lats

    def joined(pieces):
        return jnp.concatenate(pieces, axis=1)

    def turned(x, by):
        by = by % LANES
        return x if by == 0 else pltpu.roll(x, by, 1)

    for load in loads:
        load.wait()
    dual = [
        joined([dual_ref[i, s, h * ROWS : (h + 1) * ROWS, :] for s in range(subs) for h in range(high)])
        for i in range(lons)
    ]
    wind_v = joined([v_ref[i, h * ROWS : (h + 1) * ROWS, :] for i in range(lons) for h in range(high)])
    mixing = 0.15 + 0.09 * land_ref[...].astype(jnp.float32)
    mixing = joined([mixing[i : i + 1] for i in range(lons) for h in range(high)])
    lengths = jnp.zeros((ROWS, LANES), jnp.float32)
    for s in range(subs):
        for b in range(bands):
            here = jnp.logical_and(group == s, lat == me * bands + b)
            lengths = jnp.where(here, length_ref[b : b + 1, s : s + 1], lengths)
    rows[0, 0:1, :] = lengths[:1]
    rows[0, 1:2, :] = mixing
    last_inc = joined(
        [inc_ref[i, subs - 1, h * ROWS : (h + 1) * ROWS, :] for i in range(lons) for h in range(high)]
    )
    first_dual = joined(
        [dual_ref[i, 0, h * ROWS : (h + 1) * ROWS, :] for i in range(lons) for h in range(high)]
    )
    inc_u = [
        joined(
            [inc_ref[i, s, h * ROWS : (h + 1) * ROWS, :] for s in range(subs - 1) for h in range(high)]
            + [u_ref[i, h * ROWS : (h + 1) * ROWS, :] for h in range(high)]
        )
        for i in range(lons)
    ]
    own = inc_u + [wind_v] + dual
    for n, tile in enumerate(own):
        data[0, n * ROWS : (n + 1) * ROWS, :] = tile
    cross[...] = jnp.where(sub == 0, last_inc, first_dual)

    pl.semaphore_wait(barrier, len(near) + len(far) + len(beside))

    far_from = (lons + 1) * ROWS
    far_copies, cross_copies, row_copies = [], [], []
    for d in near + far:
        copy = pltpu.make_async_remote_copy(
            src_ref=rows.at[0],
            dst_ref=rows.at[tiles - d],
            send_sem=row_send.at[d],
            recv_sem=row_recv.at[tiles - d],
            device_id={"tiles": at(d)},
            device_id_type=MESH,
        )
        copy.start()
        row_copies.append(copy)
    for d in beside:
        copy = pltpu.make_async_remote_copy(
            src_ref=cross,
            dst_ref=other.at[reach - d],
            send_sem=cross_send.at[reach + d],
            recv_sem=cross_recv.at[reach - d],
            device_id={"tiles": at(d), "subwin": 1 - sub},
            device_id_type=MESH,
        )
        copy.start()
        cross_copies.append(copy)
    outward = jnp.where(2 * me < tiles, -1, 1)

    def near_copy(d):
        slot = lax.rem(tiles - d, tiles)
        return pltpu.make_async_remote_copy(
            src_ref=data.at[0],
            dst_ref=data.at[slot],
            send_sem=send_sem.at[lax.rem(d + tiles, tiles)],
            recv_sem=recv_sem.at[slot],
            device_id={"tiles": at(d)},
            device_id_type=MESH,
        )

    for side in (outward, -outward):
        for d in range(reach, 0, -1):
            near_copy(side * d).start()
    near_copies = [near_copy(d) for d in near]
    for d in far:
        copy = pltpu.make_async_remote_copy(
            src_ref=data.at[0, pl.ds(far_from, lons * ROWS)],
            dst_ref=data.at[tiles - d, pl.ds(far_from, lons * ROWS)],
            send_sem=send_sem.at[d],
            recv_sem=recv_sem.at[tiles - d],
            device_id={"tiles": at(d)},
            device_id_type=MESH,
        )
        copy.start()
        far_copies.append(copy)

    inc = [
        joined([inc_ref[i, s, h * ROWS : (h + 1) * ROWS, :] for s in range(subs) for h in range(high)])
        for i in range(lons)
    ]

    spread = jnp.zeros((ROWS, LANES), jnp.float32)
    eye = lax.broadcasted_iota(jnp.int32, (ROWS, ROWS), 0) == lax.broadcasted_iota(
        jnp.int32, (ROWS, ROWS), 1
    )
    for s in range(subs):
        for h in range(high):
            line = spread_ref[s : s + 1, h * ROWS : (h + 1) * ROWS]
            column = jnp.sum(jnp.where(eye, jnp.broadcast_to(line, (ROWS, ROWS)), 0.0), 1, keepdims=True)
            spread = jnp.where(lane // lats == s * high + h, column, spread)

    for copy in row_copies:
        copy.wait_recv()
    total = jnp.zeros((1, LANES), jnp.float32)
    for slot in range(tiles):
        total = total + rows[slot, 0:1, :]
    weights = circulant_row(jnp.broadcast_to(total, (ROWS, LANES)), lons * tiles)

    for copy in cross_copies:
        copy.wait_recv()

    def spread_out(x):
        parts = [turned(x, q * span) for q in range(lons)]
        outs = []
        for i in range(lons):
            out = parts[(0 - i) % lons]
            for g in range(1, subs):
                out = jnp.where(group == g, parts[(g - i) % lons], out)
            outs.append(out)
        return outs

    def to_all(x, g):
        outs = jnp.where(group == g, x, 0.0)
        by = 1
        while by < subs:
            outs = outs + turned(outs, by * span)
            by *= 2
        return outs

    up = jnp.where(sub > 0, 1.0, 0.0)
    down = jnp.where(sub < 1, 1.0, 0.0)
    place = len(beside) * lons
    previous, following = [None] * place, [None] * place
    for d in sorted(beside, key=abs):
        slot = d % tiles
        if d:
            near_copies[near.index(tiles - slot)].wait_recv()
        vs = spread_out(data[slot, lons * ROWS : (lons + 1) * ROWS, :])
        mixes = spread_out(jnp.broadcast_to(rows[slot, 1:2, :], (ROWS, LANES)))
        beyond = other[d + reach]
        for i in range(lons):
            here = (d + reach) * lons + i
            at_rows = pl.ds(here * ROWS, ROWS)
            f = data[slot, i * ROWS : (i + 1) * ROWS, :]
            m, u, v = mixes[i], 0.5 * to_all(f, subs - 1), 0.5 * vs[i]
            coef[0, at_rows, :] = 1.0 - 4.0 * m
            coef[1, at_rows, :] = m - u
            coef[2, at_rows, :] = m + u
            coef[3, at_rows, :] = jnp.where(lat == lats - 1, 0.0, m - v)
            coef[4, at_rows, :] = jnp.where(lat == 0, 0.0, m + v)
            g = data[slot, (lons + 1 + i) * ROWS : (lons + 2 + i) * ROWS, :]
            previous[here] = jnp.where(
                group == 0, up * turned(beyond, -i * span), turned(f, span)
            )
            following[here] = jnp.where(
                group == subs - 1, down * turned(beyond, (subs - 1 - i) * span), turned(g, -span)
            )
    extra = reach * lons - STEPS
    extent = place - 2 * extra
    f = jnp.concatenate(previous[extra : place - extra], axis=0)
    g = jnp.concatenate(following[extra : place - extra], axis=0)
    for step in range(STEPS):
        first = extra + step
        count = extent - 2 * step
        inner = pl.ds((first + 1) * ROWS, (count - 2) * ROWS)
        lower = pl.ds(first * ROWS, (count - 2) * ROWS)
        upper = pl.ds((first + 2) * ROWS, (count - 2) * ROWS)
        mid = f[ROWS:-ROWS]
        f = (
            coef[0, inner, :] * mid
            + coef[1, inner, :] * f[2 * ROWS :]
            + coef[2, inner, :] * f[: -2 * ROWS]
            + coef[3, inner, :] * turned(mid, -1)
            + coef[4, inner, :] * turned(mid, 1)
        )
        mid = g[ROWS:-ROWS]
        g = (
            coef[0, inner, :] * mid
            + coef[1, lower, :] * g[: -2 * ROWS]
            + coef[2, upper, :] * g[2 * ROWS :]
            + turned(coef[3, inner, :] * mid, 1)
            + turned(coef[4, inner, :] * mid, -1)
        )

    smooth = [jnp.zeros((ROWS, LANES), jnp.float32) for _ in range(lons)]
    ring = lons * tiles
    for slot in [0] + near + far:
        if slot in far:
            far_copies[far.index(tiles - slot)].wait_recv()
        for n in range(lons):
            x = data[slot, (lons + 1 + n) * ROWS : (lons + 2 + n) * ROWS, :]
            for i in range(lons):
                distance = (slot * lons + n - i) % ring
                smooth[i] = smooth[i] + weights[min(distance, ring - distance)] * x

    square = spread * spread
    for i in range(lons):
        here = slice(i * ROWS, (i + 1) * ROWS)
        packed_out[0, here, :] = square * smooth[i] + inc[i] - f[here]
        rest = data[0, (lons + 1 + i) * ROWS : (lons + 2 + i) * ROWS, :]
        packed_out[1, here, :] = rest - g[here]

    for copy in row_copies + near_copies + cross_copies + far_copies:
        copy.wait_send()


def unpack(packed_ref, model_out, dual_out):
    lons, subs, levs, lats = model_out.shape
    high = levs // ROWS
    for i in range(lons):
        for n, out in enumerate((model_out, dual_out)):
            tile = packed_ref[n, i * ROWS : (i + 1) * ROWS, :]
            for s in range(subs):
                for h in range(high):
                    by = (s * high + h) * lats
                    moved = pltpu.roll(tile, LANES - by, 1) if by else tile
                    out[i, s, h * ROWS : (h + 1) * ROWS, :] = moved[:, :lats]


def fills_tiles(tiles, subwins, increment):
    lons, subs, levs, lats = increment.shape
    reach = -(-STEPS // lons)
    return (
        subwins == 2
        and levs % ROWS == 0
        and subs == lons
        and subs * (levs // ROWS) * lats == LANES
        and 2 * reach < tiles <= 2 * ROWS
        and lons * tiles % 4 == 0
        and subs & (subs - 1) == 0
    )


def direct_body(increment, dual_vector, wind_u, wind_v, land_sea, length_sq, spread):
    tiles = lax.axis_size("tiles")
    lons = increment.shape[0]
    reach = -(-STEPS // lons)
    around = 2 * reach + 1
    vmem = pl.BlockSpec(memory_space=pltpu.VMEM)
    hbm = pl.BlockSpec(memory_space=pltpu.HBM)
    args = (increment, dual_vector, wind_u, wind_v, land_sea, length_sq.T, spread)
    result = jax.ShapeDtypeStruct(increment.shape, jnp.float32)
    packed = pl.pallas_call(
        functools.partial(kernel, tiles, reach),
        out_shape=pltpu.VMEM((2, lons * ROWS, LANES), jnp.float32),
        in_specs=[hbm] * len(args),
        out_specs=vmem,
        scratch_shapes=[pltpu.VMEM(x.shape, x.dtype) for x in args]
        + [
            pltpu.VMEM((tiles, (2 * lons + 1) * ROWS, LANES), jnp.float32),
            pltpu.VMEM((tiles, 2, LANES), jnp.float32),
            pltpu.VMEM((ROWS, LANES), jnp.float32),
            pltpu.VMEM((around, ROWS, LANES), jnp.float32),
            pltpu.VMEM((5, around * lons * ROWS, LANES), jnp.float32),
            pltpu.SemaphoreType.DMA((tiles,)),
            pltpu.SemaphoreType.DMA((tiles,)),
            pltpu.SemaphoreType.DMA((tiles,)),
            pltpu.SemaphoreType.DMA((tiles,)),
            pltpu.SemaphoreType.DMA((around,)),
            pltpu.SemaphoreType.DMA((around,)),
            pltpu.SemaphoreType.DMA((len(args),)),
        ],
        compiler_params=pltpu.CompilerParams(collective_id=0, has_side_effects=True),
    )(*args)
    return pl.pallas_call(
        unpack,
        out_shape=(result, result),
        in_specs=[vmem],
        out_specs=(vmem, vmem),
        compiler_params=pltpu.CompilerParams(vmem_limit_bytes=2 * 2**20),
    )(packed)


def body(*args):
    fits = fills_tiles(lax.axis_size("tiles"), lax.axis_size("subwin"), args[0])
    return direct_body(*args) if fits else stepwise_body(*args)


def solution(mesh):
    placed = (
        P(("groups", "tiles"), "subwin", None, None),
        P(("groups", "tiles"), "subwin", None, None),
        P("tiles", None, None),
        P("tiles", None, None),
        P("tiles", None),
        P("subwin", "tiles"),
        P("subwin", None),
    )
    return jax.shard_map(
        body,
        mesh=mesh,
        in_specs=placed,
        out_specs=(
            P(("groups", "tiles"), "subwin", None, None),
            P(("groups", "tiles"), "subwin", None, None),
        ),
        check_vma=False,
    )
```

```python
import functools
import math

import jax
import jax.numpy as jnp
from jax import lax
from jax.experimental import pallas as pl
from jax.experimental.pallas import tpu as pltpu
from jax.sharding import PartitionSpec as P

STEPS = 8
SWEEPS = 4
LON_DEV = 4


def extended(x, sides, width):
    for axis, dim in sides:
        devices, length = (lax.axis_size(axis), x.shape[dim])
        up = [(i, (i + 1) % devices) for i in range(devices)]
        down = [(j, i) for i, j in up]
        last = lax.slice_in_dim(x, length - width, length, axis=dim)
        leading = lax.slice_in_dim(x, 0, width, axis=dim)
        before = lax.ppermute(last, axis, up)
        after = lax.ppermute(leading, axis, down)
        x = jnp.concatenate([before, x, after], axis=dim)
    return x


def passed_along(x, axis, by):
    devices = lax.axis_size(axis)
    pairs = [(i, i + by) for i in range(devices) if 0 <= i + by < devices]
    return lax.ppermute(x, axis, pairs)


def from_north(values):
    return jnp.concatenate([values[..., 1:], jnp.zeros_like(values[..., :1])], axis=-1)


def from_south(values):
    return jnp.concatenate([jnp.zeros_like(values[..., :1]), values[..., :-1]], axis=-1)


def coefficients(wind_u, wind_v, mixing):
    return (
        1.0 - 4.0 * mixing,
        mixing - 0.5 * wind_u,
        mixing + 0.5 * wind_u,
        mixing - 0.5 * wind_v,
        mixing + 0.5 * wind_v,
    )


def tangent_step(fields, coeffs, offset):
    extent = fields.shape[0]
    centre, eastward, westward, northward, southward = [
        coeff[offset + 1 : offset + extent - 1][:, None] for coeff in coeffs
    ]
    middle = fields[1:-1]
    return (
        centre * middle
        + eastward * fields[2:]
        + westward * fields[:-2]
        + northward * from_north(middle)
        + southward * from_south(middle)
    )


def adjoint_step(fields, coeffs, offset):
    extent = fields.shape[0]
    centre = coeffs[0][offset + 1 : offset + extent - 1][:, None]
    northward = coeffs[3][offset + 1 : offset + extent - 1][:, None]
    southward = coeffs[4][offset + 1 : offset + extent - 1][:, None]
    eastward = coeffs[1][offset : offset + extent][:, None]
    westward = coeffs[2][offset : offset + extent][:, None]
    middle = fields[1:-1]
    return (
        centre * middle
        + (eastward * fields)[:-2]
        + (westward * fields)[2:]
        + from_south(northward * middle)
        + from_north(southward * middle)
    )


def run_tangent(fields, coeffs, margin):
    for repeat in range(STEPS // margin):
        grown = extended(fields, (("tiles", 0),), margin)
        for inner_step in range(margin):
            offset = (coeffs[0].shape[0] - grown.shape[0]) // 2
            grown = tangent_step(grown, coeffs, offset)
        fields = grown
    return fields


def run_adjoint(fields, coeffs, margin):
    for repeat in range(STEPS // margin):
        grown = extended(fields, (("tiles", 0),), margin)
        for inner_step in range(margin):
            offset = (coeffs[0].shape[0] - grown.shape[0]) // 2
            grown = adjoint_step(grown, coeffs, offset)
        fields = grown
    return fields


def square_tables(extent):
    index = jnp.arange(extent, dtype=jnp.int32)
    phases = index[:, None] * index[None, :] % extent
    angles = phases.astype(jnp.float32) * (2.0 * math.pi / extent)
    return (jnp.cos(angles), jnp.sin(angles))


def contract(form, first, second):
    return jnp.einsum(form, first, second, precision=lax.Precision.HIGHEST)


def smooth_bands(bands, length_sq):
    count = bands.shape[0]
    inner = LON_DEV
    outer = count // inner
    columns = bands.reshape(outer, inner, -1)
    cos_outer, sin_outer = square_tables(outer)
    cos_inner, sin_inner = square_tables(inner)
    outer_index = jnp.arange(outer, dtype=jnp.int32)
    inner_index = jnp.arange(inner, dtype=jnp.int32)
    twist = (outer_index[:, None] * inner_index[None, :] % count).astype(jnp.float32) * (
        2.0 * math.pi / count
    )
    twist_cos = jnp.cos(twist)[:, :, None]
    twist_sin = jnp.sin(twist)[:, :, None]
    first_real = contract("ab,bqc->aqc", cos_outer, columns)
    first_imag = -contract("ab,bqc->aqc", sin_outer, columns)
    turned_real = first_real * twist_cos + first_imag * twist_sin
    turned_imag = first_imag * twist_cos - first_real * twist_sin
    modes_real = contract("aqc,kq->akc", turned_real, cos_inner) + contract(
        "aqc,kq->akc", turned_imag, sin_inner
    )
    modes_imag = contract("aqc,kq->akc", turned_imag, cos_inner) - contract(
        "aqc,kq->akc", turned_real, sin_inner
    )
    wave = (outer_index[:, None] + outer * inner_index[None, :]).astype(jnp.float32)
    basic = 1.0 - jnp.cos(wave * (2.0 * math.pi / count))
    damping = (1.0 + 2.0 * length_sq[None, None, :, None, :] * basic[:, :, None, None, None]) ** (
        -SWEEPS
    )
    damping = jnp.broadcast_to(damping, (outer, inner) + bands.shape[1:]).reshape(outer, inner, -1)
    modes_real = modes_real * damping
    modes_imag = modes_imag * damping
    back_real = contract("akc,kq->aqc", modes_real, cos_inner) - contract(
        "akc,kq->aqc", modes_imag, sin_inner
    )
    back_imag = contract("akc,kq->aqc", modes_imag, cos_inner) + contract(
        "akc,kq->aqc", modes_real, sin_inner
    )
    final_real = back_real * twist_cos - back_imag * twist_sin
    final_imag = back_imag * twist_cos + back_real * twist_sin
    smoothed = contract("ab,bqc->aqc", cos_outer, final_real) - contract(
        "ab,bqc->aqc", sin_outer, final_imag
    )
    return (smoothed / count).reshape(bands.shape)


def stepwise_body(increment, dual_vector, wind_u, wind_v, land_sea, length_sq, spread):
    margin = 4
    mixing = 0.15 + 0.09 * land_sea.astype(jnp.float32)
    grown_u, grown_v, grown_mix = (
        extended(wind_u, (("tiles", 0),), margin),
        extended(wind_v, (("tiles", 0),), margin),
        extended(mixing, (("tiles", 0),), margin),
    )
    coeffs = coefficients(grown_u, grown_v, grown_mix[:, None, :])
    carried = passed_along(increment[:, -1:], "subwin", 1)
    previous = jnp.concatenate([carried, increment[:, :-1]], axis=1)
    later = passed_along(dual_vector[:, :1], "subwin", -1)
    following = jnp.concatenate([dual_vector[:, 1:], later], axis=1)
    weighted = dual_vector * spread[None, :, :, None]
    bands = lax.all_to_all(weighted, "tiles", split_axis=3, concat_axis=0, tiled=True)
    smoothed = smooth_bands(bands, length_sq)
    forward = run_tangent(previous, coeffs, margin)
    backward = run_adjoint(following, coeffs, margin)
    returned = lax.all_to_all(smoothed, "tiles", split_axis=0, concat_axis=3, tiled=True)
    covar = returned * spread[None, :, :, None]
    return (covar + increment - forward, dual_vector - backward)


ROWS = 8
LANES = 128
MESH = pl.DeviceIdType.MESH


def circulant_row(lengths, count):
    half = count // 2
    damped = []
    for wave in range(half + 1):
        basic = 1.0 - math.cos(2.0 * math.pi * wave / count)
        base = 1.0 + (2.0 * basic) * lengths
        power = base
        for _ in range(SWEEPS - 1):
            power = power * base
        weight = (1.0 if wave in (0, half) else 2.0) / count
        damped.append(weight / power)
    row = [None] * (half + 1)
    for distance in range(half // 2 + 1):
        sums = [jnp.zeros_like(lengths), jnp.zeros_like(lengths)]
        for wave in range(half + 1):
            factor = math.cos(2.0 * math.pi * (wave * distance % count) / count)
            sums[wave % 2] = sums[wave % 2] + factor * damped[wave]
        row[distance] = sums[0] + sums[1]
        row[half - distance] = sums[0] - sums[1]
    return row


def kernel(
    tiles,
    reach,
    *refs,
):
    count = 7
    held, packed_out = refs[:count], refs[count]
    here_refs = refs[count + 1 : 2 * count + 1]
    inc_ref, dual_ref, u_ref, v_ref, land_ref, length_ref, spread_ref = here_refs
    (
    data,
    rows,
    cross,
    other,
    coef,
    send_sem,
    recv_sem,
    row_send,
    row_recv,
    cross_send,
    cross_recv,
    load_sem,
    ) = refs[2 * count + 1 :]
    loads = [
        pltpu.make_async_copy(held[n], here_refs[n], load_sem.at[n]) for n in range(count)
    ]
    for load in loads:
        load.start()
    lons, subs, levs, lats = inc_ref.shape
    high = levs // ROWS
    span = high * lats
    bands = length_ref.shape[0]
    me = lax.axis_index("tiles")
    sub = lax.axis_index("subwin")
    near = [d for d in range(1, reach + 1)] + [tiles - d for d in range(1, reach + 1)]
    far = [d for d in range(1, tiles) if d not in near]
    beside = list(range(-reach, reach + 1))

    def at(distance):
        return lax.rem(me + (distance + tiles), tiles)

    barrier = pltpu.get_barrier_semaphore()
    for d in near + far:
        pl.semaphore_signal(barrier, inc=1, device_id={"tiles": at(d)}, device_id_type=MESH)
    for d in beside:
        pl.semaphore_signal(
            barrier, inc=1, device_id={"tiles": at(d), "subwin": 1 - sub}, device_id_type=MESH
        )

    lane = lax.broadcasted_iota(jnp.int32, (ROWS, LANES), 1)
    group = lane // span
    lat = lane % lats

    def joined(pieces):
        return jnp.concatenate(pieces, axis=1)

    def turned(x, by):
        by = by % LANES
        return x if by == 0 else pltpu.roll(x, by, 1)

    for load in loads:
        load.wait()
    dual = [
        joined([dual_ref[i, s, h * ROWS : (h + 1) * ROWS, :] for s in range(subs) for h in range(high)])
        for i in range(lons)
    ]
    wind_v = joined([v_ref[i, h * ROWS : (h + 1) * ROWS, :] for i in range(lons) for h in range(high)])
    mixing = 0.15 + 0.09 * land_ref[...].astype(jnp.float32)
    mixing = joined([mixing[i : i + 1] for i in range(lons) for h in range(high)])
    lengths = jnp.zeros((ROWS, LANES), jnp.float32)
    for s in range(subs):
        for b in range(bands):
            here = jnp.logical_and(group == s, lat == me * bands + b)
            lengths = jnp.where(here, length_ref[b : b + 1, s : s + 1], lengths)
    rows[0, 0:1, :] = lengths[:1]
    rows[0, 1:2, :] = mixing
    last_inc = joined(
        [inc_ref[i, subs - 1, h * ROWS : (h + 1) * ROWS, :] for i in range(lons) for h in range(high)]
    )
    first_dual = joined(
        [dual_ref[i, 0, h * ROWS : (h + 1) * ROWS, :] for i in range(lons) for h in range(high)]
    )
    inc_u = [
        joined(
            [inc_ref[i, s, h * ROWS : (h + 1) * ROWS, :] for s in range(subs - 1) for h in range(high)]
            + [u_ref[i, h * ROWS : (h + 1) * ROWS, :] for h in range(high)]
        )
        for i in range(lons)
    ]
    own = inc_u + [wind_v] + dual
    for n, tile in enumerate(own):
        data[0, n * ROWS : (n + 1) * ROWS, :] = tile
    cross[...] = jnp.where(sub == 0, last_inc, first_dual)

    pl.semaphore_wait(barrier, len(near) + len(far) + len(beside))

    far_from = (lons + 1) * ROWS
    far_copies, cross_copies, row_copies = [], [], []
    for d in near + far:
        copy = pltpu.make_async_remote_copy(
            src_ref=rows.at[0],
            dst_ref=rows.at[tiles - d],
            send_sem=row_send.at[d],
            recv_sem=row_recv.at[tiles - d],
            device_id={"tiles": at(d)},
            device_id_type=MESH,
        )
        copy.start()
        row_copies.append(copy)
    for d in beside:
        copy = pltpu.make_async_remote_copy(
            src_ref=cross,
            dst_ref=other.at[reach - d],
            send_sem=cross_send.at[reach + d],
            recv_sem=cross_recv.at[reach - d],
            device_id={"tiles": at(d), "subwin": 1 - sub},
            device_id_type=MESH,
        )
        copy.start()
        cross_copies.append(copy)
    outward = jnp.where(2 * me < tiles, -1, 1)

    def near_copy(d):
        slot = lax.rem(tiles - d, tiles)
        return pltpu.make_async_remote_copy(
            src_ref=data.at[0],
            dst_ref=data.at[slot],
            send_sem=send_sem.at[lax.rem(d + tiles, tiles)],
            recv_sem=recv_sem.at[slot],
            device_id={"tiles": at(d)},
            device_id_type=MESH,
        )

    for side in (outward, -outward):
        for d in range(reach, 0, -1):
            near_copy(side * d).start()
    near_copies = [near_copy(d) for d in near]
    inc = [
        joined([inc_ref[i, s, h * ROWS : (h + 1) * ROWS, :] for s in range(subs) for h in range(high)])
        for i in range(lons)
    ]

    spread = jnp.zeros((ROWS, LANES), jnp.float32)
    eye = lax.broadcasted_iota(jnp.int32, (ROWS, ROWS), 0) == lax.broadcasted_iota(
        jnp.int32, (ROWS, ROWS), 1
    )
    for s in range(subs):
        for h in range(high):
            line = spread_ref[s : s + 1, h * ROWS : (h + 1) * ROWS]
            column = jnp.sum(jnp.where(eye, jnp.broadcast_to(line, (ROWS, ROWS)), 0.0), 1, keepdims=True)
            spread = jnp.where(lane // lats == s * high + h, column, spread)

    for copy in row_copies:
        copy.wait_recv()
    total = jnp.zeros((1, LANES), jnp.float32)
    for slot in range(tiles):
        total = total + rows[slot, 0:1, :]
    weights = circulant_row(jnp.broadcast_to(total, (ROWS, LANES)), lons * tiles)

    for d in far:
        copy = pltpu.make_async_remote_copy(
            src_ref=data.at[0, pl.ds(far_from, lons * ROWS)],
            dst_ref=data.at[tiles - d, pl.ds(far_from, lons * ROWS)],
            send_sem=send_sem.at[d],
            recv_sem=recv_sem.at[tiles - d],
            device_id={"tiles": at(d)},
            device_id_type=MESH,
        )
        copy.start()
        far_copies.append(copy)

    for copy in cross_copies:
        copy.wait_recv()

    def spread_out(x):
        parts = [turned(x, q * span) for q in range(lons)]
        outs = []
        for i in range(lons):
            out = parts[(0 - i) % lons]
            for g in range(1, subs):
                out = jnp.where(group == g, parts[(g - i) % lons], out)
            outs.append(out)
        return outs

    def to_all(x, g):
        outs = jnp.where(group == g, x, 0.0)
        by = 1
        while by < subs:
            outs = outs + turned(outs, by * span)
            by *= 2
        return outs

    up = jnp.where(sub > 0, 1.0, 0.0)
    down = jnp.where(sub < 1, 1.0, 0.0)
    place = len(beside) * lons
    previous, following = [None] * place, [None] * place
    for d in sorted(beside, key=abs):
        slot = d % tiles
        if d:
            near_copies[near.index(tiles - slot)].wait_recv()
        vs = spread_out(data[slot, lons * ROWS : (lons + 1) * ROWS, :])
        mixes = spread_out(jnp.broadcast_to(rows[slot, 1:2, :], (ROWS, LANES)))
        beyond = other[d + reach]
        for i in range(lons):
            here = (d + reach) * lons + i
            at_rows = pl.ds(here * ROWS, ROWS)
            f = data[slot, i * ROWS : (i + 1) * ROWS, :]
            m, u, v = mixes[i], 0.5 * to_all(f, subs - 1), 0.5 * vs[i]
            coef[0, at_rows, :] = 1.0 - 4.0 * m
            coef[1, at_rows, :] = m - u
            coef[2, at_rows, :] = m + u
            coef[3, at_rows, :] = jnp.where(lat == lats - 1, 0.0, m - v)
            coef[4, at_rows, :] = jnp.where(lat == 0, 0.0, m + v)
            g = data[slot, (lons + 1 + i) * ROWS : (lons + 2 + i) * ROWS, :]
            previous[here] = jnp.where(
                group == 0, up * turned(beyond, -i * span), turned(f, span)
            )
            following[here] = jnp.where(
                group == subs - 1, down * turned(beyond, (subs - 1 - i) * span), turned(g, -span)
            )
    extra = reach * lons - STEPS
    extent = place - 2 * extra
    f = jnp.concatenate(previous[extra : place - extra], axis=0)
    g = jnp.concatenate(following[extra : place - extra], axis=0)
    for step in range(STEPS):
        first = extra + step
        count = extent - 2 * step
        inner = pl.ds((first + 1) * ROWS, (count - 2) * ROWS)
        lower = pl.ds(first * ROWS, (count - 2) * ROWS)
        upper = pl.ds((first + 2) * ROWS, (count - 2) * ROWS)
        mid = f[ROWS:-ROWS]
        f = (
            coef[0, inner, :] * mid
            + coef[1, inner, :] * f[2 * ROWS :]
            + coef[2, inner, :] * f[: -2 * ROWS]
            + coef[3, inner, :] * turned(mid, -1)
            + coef[4, inner, :] * turned(mid, 1)
        )
        mid = g[ROWS:-ROWS]
        g = (
            coef[0, inner, :] * mid
            + coef[1, lower, :] * g[: -2 * ROWS]
            + coef[2, upper, :] * g[2 * ROWS :]
            + turned(coef[3, inner, :] * mid, 1)
            + turned(coef[4, inner, :] * mid, -1)
        )

    smooth = [jnp.zeros((ROWS, LANES), jnp.float32) for _ in range(lons)]
    ring = lons * tiles
    for slot in [0] + near + far:
        if slot in far:
            far_copies[far.index(tiles - slot)].wait_recv()
        for n in range(lons):
            x = data[slot, (lons + 1 + n) * ROWS : (lons + 2 + n) * ROWS, :]
            for i in range(lons):
                distance = (slot * lons + n - i) % ring
                smooth[i] = smooth[i] + weights[min(distance, ring - distance)] * x

    square = spread * spread
    for i in range(lons):
        here = slice(i * ROWS, (i + 1) * ROWS)
        packed_out[0, here, :] = square * smooth[i] + inc[i] - f[here]
        rest = data[0, (lons + 1 + i) * ROWS : (lons + 2 + i) * ROWS, :]
        packed_out[1, here, :] = rest - g[here]

    for copy in row_copies + near_copies + cross_copies + far_copies:
        copy.wait_send()


def unpack(packed_ref, model_out, dual_out):
    lons, subs, levs, lats = model_out.shape
    high = levs // ROWS
    for i in range(lons):
        for n, out in enumerate((model_out, dual_out)):
            tile = packed_ref[n, i * ROWS : (i + 1) * ROWS, :]
            for s in range(subs):
                for h in range(high):
                    by = (s * high + h) * lats
                    moved = pltpu.roll(tile, LANES - by, 1) if by else tile
                    out[i, s, h * ROWS : (h + 1) * ROWS, :] = moved[:, :lats]


def fills_tiles(tiles, subwins, increment):
    lons, subs, levs, lats = increment.shape
    reach = -(-STEPS // lons)
    return (
        subwins == 2
        and levs % ROWS == 0
        and subs == lons
        and subs * (levs // ROWS) * lats == LANES
        and 2 * reach < tiles <= 2 * ROWS
        and lons * tiles % 4 == 0
        and subs & (subs - 1) == 0
    )


def direct_body(increment, dual_vector, wind_u, wind_v, land_sea, length_sq, spread):
    tiles = lax.axis_size("tiles")
    lons = increment.shape[0]
    reach = -(-STEPS // lons)
    around = 2 * reach + 1
    vmem = pl.BlockSpec(memory_space=pltpu.VMEM)
    hbm = pl.BlockSpec(memory_space=pltpu.HBM)
    args = (increment, dual_vector, wind_u, wind_v, land_sea, length_sq.T, spread)
    result = jax.ShapeDtypeStruct(increment.shape, jnp.float32)
    packed = pl.pallas_call(
        functools.partial(kernel, tiles, reach),
        out_shape=pltpu.VMEM((2, lons * ROWS, LANES), jnp.float32),
        in_specs=[hbm] * len(args),
        out_specs=vmem,
        scratch_shapes=[pltpu.VMEM(x.shape, x.dtype) for x in args]
        + [
            pltpu.VMEM((tiles, (2 * lons + 1) * ROWS, LANES), jnp.float32),
            pltpu.VMEM((tiles, 2, LANES), jnp.float32),
            pltpu.VMEM((ROWS, LANES), jnp.float32),
            pltpu.VMEM((around, ROWS, LANES), jnp.float32),
            pltpu.VMEM((5, around * lons * ROWS, LANES), jnp.float32),
            pltpu.SemaphoreType.DMA((tiles,)),
            pltpu.SemaphoreType.DMA((tiles,)),
            pltpu.SemaphoreType.DMA((tiles,)),
            pltpu.SemaphoreType.DMA((tiles,)),
            pltpu.SemaphoreType.DMA((around,)),
            pltpu.SemaphoreType.DMA((around,)),
            pltpu.SemaphoreType.DMA((len(args),)),
        ],
        compiler_params=pltpu.CompilerParams(collective_id=0, has_side_effects=True),
    )(*args)
    return pl.pallas_call(
        unpack,
        out_shape=(result, result),
        in_specs=[vmem],
        out_specs=(vmem, vmem),
        compiler_params=pltpu.CompilerParams(vmem_limit_bytes=2 * 2**20),
    )(packed)


def body(*args):
    fits = fills_tiles(lax.axis_size("tiles"), lax.axis_size("subwin"), args[0])
    return direct_body(*args) if fits else stepwise_body(*args)


def solution(mesh):
    placed = (
        P(("groups", "tiles"), "subwin", None, None),
        P(("groups", "tiles"), "subwin", None, None),
        P("tiles", None, None),
        P("tiles", None, None),
        P("tiles", None),
        P("subwin", "tiles"),
        P("subwin", None),
    )
    return jax.shard_map(
        body,
        mesh=mesh,
        in_specs=placed,
        out_specs=(
            P(("groups", "tiles"), "subwin", None, None),
            P(("groups", "tiles"), "subwin", None, None),
        ),
        check_vma=False,
    )
```

```python
import functools
import math

import jax
import jax.numpy as jnp
from jax import lax
from jax.experimental import pallas as pl
from jax.experimental.pallas import tpu as pltpu
from jax.sharding import PartitionSpec as P

STEPS = 8
SWEEPS = 4
LON_DEV = 4


def extended(x, sides, width):
    for axis, dim in sides:
        devices, length = (lax.axis_size(axis), x.shape[dim])
        up = [(i, (i + 1) % devices) for i in range(devices)]
        down = [(j, i) for i, j in up]
        last = lax.slice_in_dim(x, length - width, length, axis=dim)
        leading = lax.slice_in_dim(x, 0, width, axis=dim)
        before = lax.ppermute(last, axis, up)
        after = lax.ppermute(leading, axis, down)
        x = jnp.concatenate([before, x, after], axis=dim)
    return x


def passed_along(x, axis, by):
    devices = lax.axis_size(axis)
    pairs = [(i, i + by) for i in range(devices) if 0 <= i + by < devices]
    return lax.ppermute(x, axis, pairs)


def from_north(values):
    return jnp.concatenate([values[..., 1:], jnp.zeros_like(values[..., :1])], axis=-1)


def from_south(values):
    return jnp.concatenate([jnp.zeros_like(values[..., :1]), values[..., :-1]], axis=-1)


def coefficients(wind_u, wind_v, mixing):
    return (
        1.0 - 4.0 * mixing,
        mixing - 0.5 * wind_u,
        mixing + 0.5 * wind_u,
        mixing - 0.5 * wind_v,
        mixing + 0.5 * wind_v,
    )


def tangent_step(fields, coeffs, offset):
    extent = fields.shape[0]
    centre, eastward, westward, northward, southward = [
        coeff[offset + 1 : offset + extent - 1][:, None] for coeff in coeffs
    ]
    middle = fields[1:-1]
    return (
        centre * middle
        + eastward * fields[2:]
        + westward * fields[:-2]
        + northward * from_north(middle)
        + southward * from_south(middle)
    )


def adjoint_step(fields, coeffs, offset):
    extent = fields.shape[0]
    centre = coeffs[0][offset + 1 : offset + extent - 1][:, None]
    northward = coeffs[3][offset + 1 : offset + extent - 1][:, None]
    southward = coeffs[4][offset + 1 : offset + extent - 1][:, None]
    eastward = coeffs[1][offset : offset + extent][:, None]
    westward = coeffs[2][offset : offset + extent][:, None]
    middle = fields[1:-1]
    return (
        centre * middle
        + (eastward * fields)[:-2]
        + (westward * fields)[2:]
        + from_south(northward * middle)
        + from_north(southward * middle)
    )


def run_tangent(fields, coeffs, margin):
    for repeat in range(STEPS // margin):
        grown = extended(fields, (("tiles", 0),), margin)
        for inner_step in range(margin):
            offset = (coeffs[0].shape[0] - grown.shape[0]) // 2
            grown = tangent_step(grown, coeffs, offset)
        fields = grown
    return fields


def run_adjoint(fields, coeffs, margin):
    for repeat in range(STEPS // margin):
        grown = extended(fields, (("tiles", 0),), margin)
        for inner_step in range(margin):
            offset = (coeffs[0].shape[0] - grown.shape[0]) // 2
            grown = adjoint_step(grown, coeffs, offset)
        fields = grown
    return fields


def square_tables(extent):
    index = jnp.arange(extent, dtype=jnp.int32)
    phases = index[:, None] * index[None, :] % extent
    angles = phases.astype(jnp.float32) * (2.0 * math.pi / extent)
    return (jnp.cos(angles), jnp.sin(angles))


def contract(form, first, second):
    return jnp.einsum(form, first, second, precision=lax.Precision.HIGHEST)


def smooth_bands(bands, length_sq):
    count = bands.shape[0]
    inner = LON_DEV
    outer = count // inner
    columns = bands.reshape(outer, inner, -1)
    cos_outer, sin_outer = square_tables(outer)
    cos_inner, sin_inner = square_tables(inner)
    outer_index = jnp.arange(outer, dtype=jnp.int32)
    inner_index = jnp.arange(inner, dtype=jnp.int32)
    twist = (outer_index[:, None] * inner_index[None, :] % count).astype(jnp.float32) * (
        2.0 * math.pi / count
    )
    twist_cos = jnp.cos(twist)[:, :, None]
    twist_sin = jnp.sin(twist)[:, :, None]
    first_real = contract("ab,bqc->aqc", cos_outer, columns)
    first_imag = -contract("ab,bqc->aqc", sin_outer, columns)
    turned_real = first_real * twist_cos + first_imag * twist_sin
    turned_imag = first_imag * twist_cos - first_real * twist_sin
    modes_real = contract("aqc,kq->akc", turned_real, cos_inner) + contract(
        "aqc,kq->akc", turned_imag, sin_inner
    )
    modes_imag = contract("aqc,kq->akc", turned_imag, cos_inner) - contract(
        "aqc,kq->akc", turned_real, sin_inner
    )
    wave = (outer_index[:, None] + outer * inner_index[None, :]).astype(jnp.float32)
    basic = 1.0 - jnp.cos(wave * (2.0 * math.pi / count))
    damping = (1.0 + 2.0 * length_sq[None, None, :, None, :] * basic[:, :, None, None, None]) ** (
        -SWEEPS
    )
    damping = jnp.broadcast_to(damping, (outer, inner) + bands.shape[1:]).reshape(outer, inner, -1)
    modes_real = modes_real * damping
    modes_imag = modes_imag * damping
    back_real = contract("akc,kq->aqc", modes_real, cos_inner) - contract(
        "akc,kq->aqc", modes_imag, sin_inner
    )
    back_imag = contract("akc,kq->aqc", modes_imag, cos_inner) + contract(
        "akc,kq->aqc", modes_real, sin_inner
    )
    final_real = back_real * twist_cos - back_imag * twist_sin
    final_imag = back_imag * twist_cos + back_real * twist_sin
    smoothed = contract("ab,bqc->aqc", cos_outer, final_real) - contract(
        "ab,bqc->aqc", sin_outer, final_imag
    )
    return (smoothed / count).reshape(bands.shape)


def stepwise_body(increment, dual_vector, wind_u, wind_v, land_sea, length_sq, spread):
    margin = 4
    mixing = 0.15 + 0.09 * land_sea.astype(jnp.float32)
    grown_u, grown_v, grown_mix = (
        extended(wind_u, (("tiles", 0),), margin),
        extended(wind_v, (("tiles", 0),), margin),
        extended(mixing, (("tiles", 0),), margin),
    )
    coeffs = coefficients(grown_u, grown_v, grown_mix[:, None, :])
    carried = passed_along(increment[:, -1:], "subwin", 1)
    previous = jnp.concatenate([carried, increment[:, :-1]], axis=1)
    later = passed_along(dual_vector[:, :1], "subwin", -1)
    following = jnp.concatenate([dual_vector[:, 1:], later], axis=1)
    weighted = dual_vector * spread[None, :, :, None]
    bands = lax.all_to_all(weighted, "tiles", split_axis=3, concat_axis=0, tiled=True)
    smoothed = smooth_bands(bands, length_sq)
    forward = run_tangent(previous, coeffs, margin)
    backward = run_adjoint(following, coeffs, margin)
    returned = lax.all_to_all(smoothed, "tiles", split_axis=0, concat_axis=3, tiled=True)
    covar = returned * spread[None, :, :, None]
    return (covar + increment - forward, dual_vector - backward)


ROWS = 8
LANES = 128
MESH = pl.DeviceIdType.MESH


def circulant_row(lengths, count):
    half = count // 2
    damped = []
    for wave in range(half + 1):
        basic = 1.0 - math.cos(2.0 * math.pi * wave / count)
        base = 1.0 + (2.0 * basic) * lengths
        power = base
        for _ in range(SWEEPS - 1):
            power = power * base
        weight = (1.0 if wave in (0, half) else 2.0) / count
        damped.append(weight / power)
    row = [None] * (half + 1)
    for distance in range(half // 2 + 1):
        sums = [jnp.zeros_like(lengths), jnp.zeros_like(lengths)]
        for wave in range(half + 1):
            factor = math.cos(2.0 * math.pi * (wave * distance % count) / count)
            sums[wave % 2] = sums[wave % 2] + factor * damped[wave]
        row[distance] = sums[0] + sums[1]
        row[half - distance] = sums[0] - sums[1]
    return row


def kernel(
    tiles,
    reach,
    *refs,
):
    count = 7
    held, packed_out = refs[:count], refs[count]
    here_refs = refs[count + 1 : 2 * count + 1]
    inc_ref, dual_ref, u_ref, v_ref, land_ref, length_ref, spread_ref = here_refs
    (
    data,
    rows,
    cross,
    other,
    coef,
    send_sem,
    recv_sem,
    row_send,
    row_recv,
    cross_send,
    cross_recv,
    load_sem,
    ) = refs[2 * count + 1 :]
    loads = [
        pltpu.make_async_copy(held[n], here_refs[n], load_sem.at[n]) for n in range(count)
    ]
    for load in loads:
        load.start()
    lons, subs, levs, lats = inc_ref.shape
    high = levs // ROWS
    span = high * lats
    bands = length_ref.shape[0]
    me = lax.axis_index("tiles")
    sub = lax.axis_index("subwin")
    near = [d for d in range(1, reach + 1)] + [tiles - d for d in range(1, reach + 1)]
    far = [d for d in range(1, tiles) if d not in near]
    beside = list(range(-reach, reach + 1))

    def at(distance):
        return lax.rem(me + (distance + tiles), tiles)

    barrier = pltpu.get_barrier_semaphore()
    for d in near + far:
        pl.semaphore_signal(barrier, inc=1, device_id={"tiles": at(d)}, device_id_type=MESH)
    for d in beside:
        pl.semaphore_signal(
            barrier, inc=1, device_id={"tiles": at(d), "subwin": 1 - sub}, device_id_type=MESH
        )

    lane = lax.broadcasted_iota(jnp.int32, (ROWS, LANES), 1)
    group = lane // span
    lat = lane % lats

    def joined(pieces):
        return jnp.concatenate(pieces, axis=1)

    def turned(x, by):
        by = by % LANES
        return x if by == 0 else pltpu.roll(x, by, 1)

    for load in loads:
        load.wait()
    dual = [
        joined([dual_ref[i, s, h * ROWS : (h + 1) * ROWS, :] for s in range(subs) for h in range(high)])
        for i in range(lons)
    ]
    wind_v = joined([v_ref[i, h * ROWS : (h + 1) * ROWS, :] for i in range(lons) for h in range(high)])
    mixing = 0.15 + 0.09 * land_ref[...].astype(jnp.float32)
    mixing = joined([mixing[i : i + 1] for i in range(lons) for h in range(high)])
    lengths = jnp.zeros((ROWS, LANES), jnp.float32)
    for s in range(subs):
        for b in range(bands):
            here = jnp.logical_and(group == s, lat == me * bands + b)
            lengths = jnp.where(here, length_ref[b : b + 1, s : s + 1], lengths)
    rows[0, 0:1, :] = lengths[:1]
    rows[0, 1:2, :] = mixing
    last_inc = joined(
        [inc_ref[i, subs - 1, h * ROWS : (h + 1) * ROWS, :] for i in range(lons) for h in range(high)]
    )
    first_dual = joined(
        [dual_ref[i, 0, h * ROWS : (h + 1) * ROWS, :] for i in range(lons) for h in range(high)]
    )
    inc_u = [
        joined(
            [inc_ref[i, s, h * ROWS : (h + 1) * ROWS, :] for s in range(subs - 1) for h in range(high)]
            + [u_ref[i, h * ROWS : (h + 1) * ROWS, :] for h in range(high)]
        )
        for i in range(lons)
    ]
    own = inc_u + [wind_v] + dual
    for n, tile in enumerate(own):
        data[0, n * ROWS : (n + 1) * ROWS, :] = tile
    cross[...] = jnp.where(sub == 0, last_inc, first_dual)

    pl.semaphore_wait(barrier, len(near) + len(far) + len(beside))

    far_from = (lons + 1) * ROWS
    far_copies, cross_copies, row_copies = [], [], []
    for d in near + far:
        copy = pltpu.make_async_remote_copy(
            src_ref=rows.at[0],
            dst_ref=rows.at[tiles - d],
            send_sem=row_send.at[d],
            recv_sem=row_recv.at[tiles - d],
            device_id={"tiles": at(d)},
            device_id_type=MESH,
        )
        copy.start()
        row_copies.append(copy)
    for d in beside:
        copy = pltpu.make_async_remote_copy(
            src_ref=cross,
            dst_ref=other.at[reach - d],
            send_sem=cross_send.at[reach + d],
            recv_sem=cross_recv.at[reach - d],
            device_id={"tiles": at(d), "subwin": 1 - sub},
            device_id_type=MESH,
        )
        copy.start()
        cross_copies.append(copy)
    for d in far:
        copy = pltpu.make_async_remote_copy(
            src_ref=data.at[0, pl.ds(far_from, lons * ROWS)],
            dst_ref=data.at[tiles - d, pl.ds(far_from, lons * ROWS)],
            send_sem=send_sem.at[d],
            recv_sem=recv_sem.at[tiles - d],
            device_id={"tiles": at(d)},
            device_id_type=MESH,
        )
        copy.start()
        far_copies.append(copy)

    outward = jnp.where(2 * me < tiles, -1, 1)

    def near_copy(d):
        slot = lax.rem(tiles - d, tiles)
        return pltpu.make_async_remote_copy(
            src_ref=data.at[0],
            dst_ref=data.at[slot],
            send_sem=send_sem.at[lax.rem(d + tiles, tiles)],
            recv_sem=recv_sem.at[slot],
            device_id={"tiles": at(d)},
            device_id_type=MESH,
        )

    for side in (outward, -outward):
        for d in range(reach, 0, -1):
            near_copy(side * d).start()
    near_copies = [near_copy(d) for d in near]
    inc = [
        joined([inc_ref[i, s, h * ROWS : (h + 1) * ROWS, :] for s in range(subs) for h in range(high)])
        for i in range(lons)
    ]

    spread = jnp.zeros((ROWS, LANES), jnp.float32)
    eye = lax.broadcasted_iota(jnp.int32, (ROWS, ROWS), 0) == lax.broadcasted_iota(
        jnp.int32, (ROWS, ROWS), 1
    )
    for s in range(subs):
        for h in range(high):
            line = spread_ref[s : s + 1, h * ROWS : (h + 1) * ROWS]
            column = jnp.sum(jnp.where(eye, jnp.broadcast_to(line, (ROWS, ROWS)), 0.0), 1, keepdims=True)
            spread = jnp.where(lane // lats == s * high + h, column, spread)

    for copy in row_copies:
        copy.wait_recv()
    total = jnp.zeros((1, LANES), jnp.float32)
    for slot in range(tiles):
        total = total + rows[slot, 0:1, :]
    weights = circulant_row(jnp.broadcast_to(total, (ROWS, LANES)), lons * tiles)

    for copy in cross_copies:
        copy.wait_recv()

    def spread_out(x):
        parts = [turned(x, q * span) for q in range(lons)]
        outs = []
        for i in range(lons):
            out = parts[(0 - i) % lons]
            for g in range(1, subs):
                out = jnp.where(group == g, parts[(g - i) % lons], out)
            outs.append(out)
        return outs

    def to_all(x, g):
        outs = jnp.where(group == g, x, 0.0)
        by = 1
        while by < subs:
            outs = outs + turned(outs, by * span)
            by *= 2
        return outs

    up = jnp.where(sub > 0, 1.0, 0.0)
    down = jnp.where(sub < 1, 1.0, 0.0)
    place = len(beside) * lons
    previous, following = [None] * place, [None] * place
    for d in sorted(beside, key=abs):
        slot = d % tiles
        if d:
            near_copies[near.index(tiles - slot)].wait_recv()
        vs = spread_out(data[slot, lons * ROWS : (lons + 1) * ROWS, :])
        mixes = spread_out(jnp.broadcast_to(rows[slot, 1:2, :], (ROWS, LANES)))
        beyond = other[d + reach]
        for i in range(lons):
            here = (d + reach) * lons + i
            at_rows = pl.ds(here * ROWS, ROWS)
            f = data[slot, i * ROWS : (i + 1) * ROWS, :]
            m, u, v = mixes[i], 0.5 * to_all(f, subs - 1), 0.5 * vs[i]
            coef[0, at_rows, :] = 1.0 - 4.0 * m
            coef[1, at_rows, :] = m - u
            coef[2, at_rows, :] = m + u
            coef[3, at_rows, :] = jnp.where(lat == lats - 1, 0.0, m - v)
            coef[4, at_rows, :] = jnp.where(lat == 0, 0.0, m + v)
            g = data[slot, (lons + 1 + i) * ROWS : (lons + 2 + i) * ROWS, :]
            previous[here] = jnp.where(
                group == 0, up * turned(beyond, -i * span), turned(f, span)
            )
            following[here] = jnp.where(
                group == subs - 1, down * turned(beyond, (subs - 1 - i) * span), turned(g, -span)
            )
    extra = reach * lons - STEPS
    extent = place - 2 * extra
    f = jnp.concatenate(previous[extra : place - extra], axis=0)
    g = jnp.concatenate(following[extra : place - extra], axis=0)
    for step in range(STEPS):
        first = extra + step
        count = extent - 2 * step
        inner = pl.ds((first + 1) * ROWS, (count - 2) * ROWS)
        lower = pl.ds(first * ROWS, (count - 2) * ROWS)
        upper = pl.ds((first + 2) * ROWS, (count - 2) * ROWS)
        mid = f[ROWS:-ROWS]
        f = (
            coef[0, inner, :] * mid
            + coef[1, inner, :] * f[2 * ROWS :]
            + coef[2, inner, :] * f[: -2 * ROWS]
            + coef[3, inner, :] * turned(mid, -1)
            + coef[4, inner, :] * turned(mid, 1)
        )
        mid = g[ROWS:-ROWS]
        g = (
            coef[0, inner, :] * mid
            + coef[1, lower, :] * g[: -2 * ROWS]
            + coef[2, upper, :] * g[2 * ROWS :]
            + turned(coef[3, inner, :] * mid, 1)
            + turned(coef[4, inner, :] * mid, -1)
        )

    smooth = [jnp.zeros((ROWS, LANES), jnp.float32) for _ in range(lons)]
    ring = lons * tiles
    for slot in [0] + near + far:
        if slot in far:
            far_copies[far.index(tiles - slot)].wait_recv()
        for n in range(lons):
            x = data[slot, (lons + 1 + n) * ROWS : (lons + 2 + n) * ROWS, :]
            for i in range(lons):
                distance = (slot * lons + n - i) % ring
                smooth[i] = smooth[i] + weights[min(distance, ring - distance)] * x

    square = spread * spread
    for i in range(lons):
        here = slice(i * ROWS, (i + 1) * ROWS)
        packed_out[0, here, :] = square * smooth[i] + inc[i] - f[here]
        rest = data[0, (lons + 1 + i) * ROWS : (lons + 2 + i) * ROWS, :]
        packed_out[1, here, :] = rest - g[here]

    for copy in row_copies + near_copies + cross_copies + far_copies:
        copy.wait_send()


def unpack(packed_ref, model_out, dual_out):
    lons, subs, levs, lats = model_out.shape
    high = levs // ROWS
    for i in range(lons):
        for n, out in enumerate((model_out, dual_out)):
            tile = packed_ref[n, i * ROWS : (i + 1) * ROWS, :]
            for s in range(subs):
                for h in range(high):
                    by = (s * high + h) * lats
                    moved = pltpu.roll(tile, LANES - by, 1) if by else tile
                    out[i, s, h * ROWS : (h + 1) * ROWS, :] = moved[:, :lats]


def fills_tiles(tiles, subwins, increment):
    lons, subs, levs, lats = increment.shape
    reach = -(-STEPS // lons)
    return (
        subwins == 2
        and levs % ROWS == 0
        and subs == lons
        and subs * (levs // ROWS) * lats == LANES
        and 2 * reach < tiles <= 2 * ROWS
        and lons * tiles % 4 == 0
        and subs & (subs - 1) == 0
    )


def direct_body(increment, dual_vector, wind_u, wind_v, land_sea, length_sq, spread):
    tiles = lax.axis_size("tiles")
    lons = increment.shape[0]
    reach = -(-STEPS // lons)
    around = 2 * reach + 1
    vmem = pl.BlockSpec(memory_space=pltpu.VMEM)
    hbm = pl.BlockSpec(memory_space=pltpu.HBM)
    args = (increment, dual_vector, wind_u, wind_v, land_sea, length_sq.T, spread)
    result = jax.ShapeDtypeStruct(increment.shape, jnp.float32)
    packed = pl.pallas_call(
        functools.partial(kernel, tiles, reach),
        out_shape=pltpu.VMEM((2, lons * ROWS, LANES), jnp.float32),
        in_specs=[hbm] * len(args),
        out_specs=vmem,
        scratch_shapes=[pltpu.VMEM(x.shape, x.dtype) for x in args]
        + [
            pltpu.VMEM((tiles, (2 * lons + 1) * ROWS, LANES), jnp.float32),
            pltpu.VMEM((tiles, 2, LANES), jnp.float32),
            pltpu.VMEM((ROWS, LANES), jnp.float32),
            pltpu.VMEM((around, ROWS, LANES), jnp.float32),
            pltpu.VMEM((5, around * lons * ROWS, LANES), jnp.float32),
            pltpu.SemaphoreType.DMA((tiles,)),
            pltpu.SemaphoreType.DMA((tiles,)),
            pltpu.SemaphoreType.DMA((tiles,)),
            pltpu.SemaphoreType.DMA((tiles,)),
            pltpu.SemaphoreType.DMA((around,)),
            pltpu.SemaphoreType.DMA((around,)),
            pltpu.SemaphoreType.DMA((len(args),)),
        ],
        compiler_params=pltpu.CompilerParams(collective_id=0, has_side_effects=True),
    )(*args)
    return pl.pallas_call(
        unpack,
        out_shape=(result, result),
        in_specs=[vmem],
        out_specs=(vmem, vmem),
        compiler_params=pltpu.CompilerParams(vmem_limit_bytes=2 * 2**20),
    )(packed)


def body(*args):
    fits = fills_tiles(lax.axis_size("tiles"), lax.axis_size("subwin"), args[0])
    return direct_body(*args) if fits else stepwise_body(*args)


def solution(mesh):
    placed = (
        P(("groups", "tiles"), "subwin", None, None),
        P(("groups", "tiles"), "subwin", None, None),
        P("tiles", None, None),
        P("tiles", None, None),
        P("tiles", None),
        P("subwin", "tiles"),
        P("subwin", None),
    )
    return jax.shard_map(
        body,
        mesh=mesh,
        in_specs=placed,
        out_specs=(
            P(("groups", "tiles"), "subwin", None, None),
            P(("groups", "tiles"), "subwin", None, None),
        ),
        check_vma=False,
    )
```
